32 devices in a mesh: seq: 16 (over z, x, core), mlp: 2 (over y).
Axes of the slice: x: 2, y: 2, z: 4, core: 2. Of those that a mesh axis runs over, the one named last changes fastest.
Arguments:
- tokens: bfloat16 [32768, 768], P(('seq', 'mlp')), may hold values from -6 to 6
- time_table: float32 [1000, 128], replicated, may hold values from -6 to 6
- timesteps: int32 [32], P(('seq', 'mlp')), may hold values from 0 to 999
- lengths: int32 [256], P(('seq', 'mlp')), may hold values from 8 to 128
- ln1_gain: float32 [768], replicated, may hold values from 0.5 to 1.5
- ln2_gain: float32 [768], replicated, may hold values from 0.5 to 1.5
- w_qkv: bfloat16 [768, 2304], replicated, may hold values from -0.21875 to 0.21875
- w_out: bfloat16 [768, 768], replicated, may hold values from -1.75 to 1.75
- w_up: bfloat16 [768, 3072], P(None, 'mlp'), may hold values from -0.21875 to 0.21875
- b_up: bfloat16 [3072], P('mlp'), may hold values from -3 to 3
- w_down: bfloat16 [3072, 768], P('mlp'), may hold values from -0.109375 to 0.109375
- b_down: bfloat16 [768], replicated, may hold values from -3 to 3
- ada_w: float32 [128, 4608], replicated, may hold values from -0.5 to 0.5
- ada_b: float32 [4608], replicated, may hold values from -3 to 3
- out_grad: bfloat16 [32768, 768], P(('seq', 'mlp')), may hold values from -6 to 6
Outputs:
- output: bfloat16 [32768, 768], P(('seq', 'mlp'))
- d_tokens: bfloat16 [32768, 768], P(('seq', 'mlp'))
- d_time_table: float32 [1000, 128], replicated
- d_ln1_gain: float32 [768], replicated
- d_ln2_gain: float32 [768], replicated
- d_w_qkv: float32 [768, 2304], replicated
- d_w_out: float32 [768, 768], replicated
- d_w_up: float32 [768, 3072], P(None, 'mlp')
- d_b_up: float32 [3072], P('mlp')
- d_w_down: float32 [3072, 768], P('mlp')
- d_b_down: float32 [768], replicated
- d_ada_w: float32 [128, 4608], replicated
- d_ada_b: float32 [4608], replicated
The draws below stay inside these ranges and needn't reach their ends.
All inputs are finite; a program needn't handle non-finite values.
Results may differ from the reference program's by a relative error of at most 0.012.
The reference program's roundings to bfloat16 on the way count: a program that leaves them out, or rounds other values in their place, can miss the bound.
Values may be sent and summed in bfloat16 or wider, within the bound.
No kernel may reach another device: no remote copies, remote signals or barrier semaphores. Data moves between devices by JAX's collectives and lax.ppermute only.
A program may use at most 256 MiB of HBM per device.

```python
import jax
import jax.numpy as jnp
from jax import lax

D = 768
H = 12
FF = 3072
COND = 128
HD = 64
NT = 1000
SLOT = 128
SLOTS_ROW = 8
ROWS = 32
TOKENS = 32768
SLOTS = 256


def with_ends(array, own_key, least, high):
    dims = array.shape
    index_at = [jax.random.randint(jax.random.fold_in(own_key, axis), (), 0, dims[axis]) for axis in range(len(dims))]
    array = array.at[tuple(index_at)].set(least)
    longest = dims.index(max(dims))
    index_at[longest] = (index_at[longest] + 1) % dims[longest]
    return array.at[tuple(index_at)].set(high)


def level_of(rng, shape, cuts, least, high):
    level = 1.0
    for axis_at, blocks in cuts:
        heights = jax.random.uniform(jax.random.fold_in(jax.random.fold_in(rng, 6), axis_at), (blocks,), jnp.float32, least / len(cuts), high / len(cuts))
        level = level * jnp.repeat(jnp.exp(heights), shape[axis_at] // blocks).reshape((-1,) + (1,) * (len(shape) - 1 - axis_at))
    return level


def centred(stream_key, dims, scale, reach, cuts=(), held_as=jnp.bfloat16):
    entries = jax.random.normal(stream_key, dims, jnp.float32) * scale
    if len(cuts) > 0:
        entries = level_of(stream_key, dims, cuts, -0.22, 0.18) * entries
    return jnp.clip(entries, min=-reach, max=reach).astype(held_as)


def setup_inputs(seed: int = 0) -> dict:
    arg_keys = jax.random.split(jax.random.key(seed), 16)
    return {
        "tokens": centred(arg_keys[0], (TOKENS, D), 1.0, 6.0, ((0, 32),)),
        "time_table": centred(arg_keys[1], (NT, COND), 1.0, 6.0, (), jnp.float32),
        "timesteps": with_ends(jax.random.randint(arg_keys[2], (ROWS,), 0, NT), jax.random.fold_in(arg_keys[2], 1), 0, NT - 1).astype(jnp.int32),
        "lengths": with_ends(jax.random.randint(arg_keys[3], (SLOTS,), SLOT // 16, SLOT + 1), jax.random.fold_in(arg_keys[3], 1), SLOT // 16, SLOT).astype(jnp.int32),
        "ln1_gain": jnp.clip(1.0 + 0.1 * jax.random.normal(arg_keys[4], (D,), jnp.float32), 0.5, 1.5),
        "ln2_gain": jnp.clip(1.0 + 0.1 * jax.random.normal(arg_keys[5], (D,), jnp.float32), 0.5, 1.5),
        "w_qkv": centred(arg_keys[6], (D, 3 * D), D ** -0.5, 0.21875),
        "w_out": centred(arg_keys[7], (D, D), (max(1, D // 64)) ** -0.5, 1.75),
        "w_up": centred(arg_keys[8], (D, FF), D ** -0.5, 0.21875, ((1, 2),)),
        "b_up": centred(arg_keys[9], (FF,), 0.5, 3.0, ((0, 2),)),
        "w_down": centred(arg_keys[10], (FF, D), FF ** -0.5, 0.109375, ((0, 2),)),
        "b_down": centred(arg_keys[11], (D,), 0.5, 3.0),
        "ada_w": centred(arg_keys[12], (COND, 6 * D), COND ** -0.5, 0.5, (), jnp.float32),
        "ada_b": centred(arg_keys[13], (6 * D,), 0.5, 3.0, (), jnp.float32),
        "out_grad": centred(arg_keys[14], (TOKENS, D), 1.0, 6.0, ((0, 32),)),
    }


HIGH = lax.Precision.HIGHEST

@jax.custom_vjp
def low(v):
    return lax.optimization_barrier(v.astype(jnp.bfloat16)).astype(jnp.float32)

@jax.custom_vjp
def low_back(v):
    return v

def low_keep(v):
    return (low(v), None)

def low_pass(kept, grad):
    return (grad,)

def back_keep(v):
    return (v, None)

def back_low(kept, grad):
    return (low(grad),)
low.defvjp(low_keep, low_pass)
low_back.defvjp(back_keep, back_low)

def modulate(values, gain, shift, scale):
    center = values - lax.optimization_barrier(jnp.mean(values, axis=-1, keepdims=True))
    spread = lax.optimization_barrier(jnp.mean(center * center, axis=-1, keepdims=True))
    return center * lax.rsqrt(spread + 1e-06) * gain * (1.0 + scale) + shift

def rotary(values, positions):
    half = values.shape[-1] // 2
    freq = 10000.0 ** (-jnp.arange(half, dtype=jnp.float32) / half)
    angle = positions.astype(jnp.float32)[:, None] * freq[None, :]
    cosine = jnp.cos(angle)[:, None, :]
    sine = jnp.sin(angle)[:, None, :]
    first = values[..., :half]
    second = values[..., half:]
    return jnp.concatenate([first * cosine - second * sine, second * cosine + first * sine], axis=-1)

def attention(qkv, lens):
    slots = qkv.shape[0] // SLOT
    parts = qkv.reshape(slots, SLOT, 3, H, HD)
    positions = jnp.arange(SLOT, dtype=jnp.int32)
    query = low(rotary(parts[:, :, 0], positions))
    key = low(rotary(parts[:, :, 1], positions))
    value = low(parts[:, :, 2])
    scores = low_back(jnp.einsum('sqhd,skhd->shqk', query, key, precision=HIGH) * HD ** (-0.5))
    valid = (positions[None, :] < lens[:, None])[:, None, None, :]
    scores = jnp.where(valid, scores, -1e+30)
    top = lax.optimization_barrier(jnp.max(scores, axis=-1, keepdims=True))
    expo = jnp.exp(scores - top)
    probs = low(expo / lax.optimization_barrier(jnp.sum(expo, axis=-1, keepdims=True)))
    attended = low_back(low(jnp.einsum('shqk,skhd->sqhd', probs, value, precision=HIGH)))
    return attended.reshape(-1, D)

def block_forward(tok, params, onehot, lens):
    time_table, ln1_gain, ln2_gain, w_qkv, w_out, w_up, b_up, w_down, b_down, ada_w, ada_b = params
    cond = jnp.dot(onehot, time_table, precision=HIGH)
    mod = jnp.dot(cond, ada_w, precision=HIGH) + ada_b
    shift1, scale1, gate1, shift2, scale2, gate2 = jnp.split(mod, 6, axis=-1)
    h1 = low(modulate(tok, ln1_gain, shift1, scale1))
    qkv = low_back(jnp.dot(h1, w_qkv, precision=HIGH))
    attended = attention(qkv, lens)
    attn = low_back(jnp.dot(attended, w_out, precision=HIGH))
    mid = tok + gate1 * attn
    h2 = low(modulate(mid, ln2_gain, shift2, scale2))
    pre = low_back(jnp.dot(h2, w_up, precision=HIGH) + b_up)
    act = low(jax.nn.gelu(pre, approximate=True))
    branch = low_back(jnp.dot(act, w_down, precision=HIGH) + b_down)
    return mid + gate2 * branch

def reference(tokens, time_table, timesteps, lengths, ln1_gain, ln2_gain, w_qkv, w_out, w_up, b_up, w_down, b_down, ada_w, ada_b, out_grad):
    params = (time_table, ln1_gain, ln2_gain, w_qkv.astype(jnp.float32), w_out.astype(jnp.float32), w_up.astype(jnp.float32), b_up.astype(jnp.float32), w_down.astype(jnp.float32), b_down.astype(jnp.float32), ada_w, ada_b)
    row_len = SLOTS_ROW * SLOT
    rows = tokens.shape[0] // row_len
    tok_rows = tokens.astype(jnp.float32).reshape(rows, row_len, D)
    grad_rows = out_grad.astype(jnp.float32).reshape(rows, row_len, D)
    len_rows = lengths.reshape(rows, SLOTS_ROW)
    onehots = (timesteps[:, None] == jnp.arange(NT, dtype=jnp.int32)[None, :]).astype(jnp.float32)[:, None, :]

    def step(total, item):
        tok, grad, lens, onehot = item

        def forward(tok_in, params_in):
            return block_forward(tok_in, params_in, onehot, lens)
        result, back = jax.vjp(forward, tok, params)
        tok_grad, param_grads = back(grad)
        total = jax.tree.map(lambda left, right: left + right, total, param_grads)
        return (total, (result.astype(jnp.bfloat16), tok_grad.astype(jnp.bfloat16)))
    zeros = jax.tree.map(jnp.zeros_like, params)
    totals, (results, tok_grads) = lax.scan(step, zeros, (tok_rows, grad_rows, len_rows, onehots))
    return (results.reshape(-1, D), tok_grads.reshape(-1, D), totals[0], totals[1], totals[2], totals[3], totals[4], totals[5], totals[6], totals[7], totals[8], totals[9], totals[10])
```

```python
import functools

import jax
import jax.numpy as jnp
import numpy as np
from jax import lax
from jax.experimental import pallas as pl
from jax.experimental.pallas import tpu as pltpu
from jax.sharding import PartitionSpec as P

H = 12
SLOT = 128
HIGH = lax.Precision.HIGHEST
f32 = jnp.float32
bf16 = jnp.bfloat16
Y, CORE, X, Z0, Z1 = 1, 2, 4, 8, 16
LIMIT = 12 * 1024 * 1024
CHUNK = 256


def nn(a, b):
    return jnp.dot(a, b, preferred_element_type=f32)


def nt(a, b):
    return lax.dot_general(a, b, (((1,), (1,)), ((), ())), preferred_element_type=f32)


def tn(a, b):
    return lax.dot_general(a, b, (((0,), (0,)), ((), ())), preferred_element_type=f32)


def whiten(x):
    center = x - jnp.mean(x, axis=-1, keepdims=True)
    spread = jnp.mean(center * center, axis=-1, keepdims=True)
    rs = lax.rsqrt(spread + 1e-06)
    return center * rs, rs


def whiten_back(grad, unit, rs):
    return rs * (
        grad
        - jnp.mean(grad, axis=-1, keepdims=True)
        - unit * jnp.mean(grad * unit, axis=-1, keepdims=True)
    )


def half_turn(u, first):
    return jnp.where(first, pltpu.roll(u, 96, 1), pltpu.roll(u, 32, 1))


def split_heads(u, low):
    zero = jnp.zeros_like(u)
    return jnp.concatenate([jnp.where(low, u, zero), jnp.where(low, zero, u)], axis=0)


def lane_masks(shape):
    lane = lax.broadcasted_iota(jnp.int32, shape, 1)
    return lane < 64, lax.rem(lane, 64) < 32


def call(body, outs, args, scalars=1, scratch=(), limit=LIMIT, name=None, us=1):
    specs = [pl.BlockSpec(memory_space=pltpu.SMEM)] * scalars
    specs += [pl.BlockSpec(memory_space=pltpu.VMEM)] * (len(args) - scalars)
    return pl.pallas_call(
        body,
        in_specs=specs,
        out_specs=[pl.BlockSpec(memory_space=pltpu.VMEM)] * len(outs),
        out_shape=[jax.ShapeDtypeStruct(*o) for o in outs],
        scratch_shapes=list(scratch),
        compiler_params=pltpu.CompilerParams(vmem_limit_bytes=limit),
        cost_estimate=pl.CostEstimate(flops=int(us * 1.15e9), bytes_accessed=0, transcendentals=0),
        name=name,
    )(*args)


def chunk(i, size=CHUNK):
    return pl.ds(pl.multiple_of(i * size, size), size)


def add_row(ref, at, value):
    ref[at : at + 1, :] = ref[at : at + 1, :] + jnp.sum(value, axis=0, keepdims=True)


def mod_kernel(ts, tab, ada_w, vec, mod_o):
    width = mod_o.shape[1]
    cols = width // 128
    row = tab[pl.ds(ts[0], 1), :]
    col = jnp.broadcast_to(row, (128, 128)).T
    for j in range(6 * cols):
        sl = slice(128 * j, 128 * j + 128)
        out = jnp.sum(ada_w[:, sl] * col, axis=0, keepdims=True)
        to = slice(128 * (j % cols), 128 * (j % cols) + 128)
        mod_o[j // cols : j // cols + 1, to] = out + vec[j // cols : j // cols + 1, to]
    mod_o[6:8, :] = jnp.zeros((2, width), f32)


def forward_kernel(lens, mod, vec, tok, dy, wqkv, wout, cos, sin, h1_o, q_o, k_o, v_o, p_o, att_o, attn_o, h2_o, dbl_o, bd_o):
    width = tok.shape[1]
    cols = width // 128
    low, first = lane_masks((SLOT, 128))
    key_at = lax.broadcasted_iota(jnp.int32, (SLOT, SLOT), 1)
    slots = CHUNK // SLOT
    bd_o[...] = jnp.zeros_like(bd_o)

    def one(i, _):
        cr = chunk(i)
        x = tok[cr, :].astype(f32)
        unit, _ = whiten(x)
        h1 = (unit * (vec[6:7, :] * (1.0 + mod[1:2, :])) + mod[0:1, :]).astype(bf16)
        h1_o[cr, :] = h1
        qkv = nn(h1, wqkv[...])
        cosv = cos[...]
        sinv = sin[...]
        for s in range(slots):
            rows = slice(s * SLOT, s * SLOT + SLOT)
            out = pl.ds(pl.multiple_of(i * CHUNK + s * SLOT, SLOT), SLOT)
            valid = key_at < lens[i * slots + s]
            for j in range(cols):
                sl = slice(128 * j, 128 * j + 128)
                q = qkv[rows, 128 * j : 128 * j + 128]
                k = qkv[rows, width + 128 * j : width + 128 * j + 128]
                v = qkv[rows, 2 * width + 128 * j : 2 * width + 128 * j + 128].astype(bf16)
                q = (q * cosv + half_turn(q, first) * sinv).astype(bf16)
                k = (k * cosv + half_turn(k, first) * sinv).astype(bf16)
                q_o[out, sl] = q
                k_o[out, sl] = k
                v_o[out, sl] = v
                sc = nt(q, split_heads(k, low)) * 0.125
                probs = []
                for e in range(2):
                    part = jnp.where(valid, sc[:, SLOT * e : SLOT * e + SLOT], -1e30)
                    ex = jnp.exp(part - jnp.max(part, axis=-1, keepdims=True))
                    probs.append((ex * (1.0 / jnp.sum(ex, axis=-1, keepdims=True))).astype(bf16))
                pr = jnp.concatenate(probs, axis=1)
                p_o[out, 256 * j : 256 * j + 256] = pr
                att_o[out, sl] = nn(pr, split_heads(v, low)).astype(bf16)
        attn = nn(att_o[cr, :], wout[...])
        attn_o[cr, :] = attn
        unit2, _ = whiten(x + mod[2:3, :] * attn)
        h2_o[cr, :] = (unit2 * (vec[7:8, :] * (1.0 + mod[4:5, :])) + mod[3:4, :]).astype(bf16)
        dbl = (dy[cr, :].astype(f32) * mod[5:6, :]).astype(bf16)
        dbl_o[cr, :] = dbl
        add_row(bd_o, 0, dbl.astype(f32))
        return 0

    lax.fori_loop(0, tok.shape[0] // CHUNK, one, 0)


def call_forward(lens, mod, vec, tok, dy, wqkv, wout, cos, sin):
    tokens, width = tok.shape
    low = ((tokens, width), bf16)
    return call(
        forward_kernel,
        [low, low, low, low, ((tokens, H * SLOT), bf16), low, ((tokens, width), f32), low, low, ((8, width), f32)],
        [lens, mod, vec, tok, dy, wqkv, wout, cos, sin],
        name="attention_forward", us=18,
    )


def gelu_parts(v):
    c = 0.7978845608028654
    v2 = v * v
    t = jnp.tanh(v * (c + c * 0.044715 * v2))
    h = 0.5 + 0.5 * t
    act = v * h
    slope = h + act * (1.0 - h) * (2.0 * c + 6.0 * c * 0.044715 * v2)
    return act, slope


def put_rows(out, scratch, me, blocks, place):
    size = scratch.shape[0] // blocks
    for r in range(blocks):
        src = pl.multiple_of(lax.bitwise_xor(r, me) * size, size) if blocks > 1 else 0
        out[place(r) * size : place(r) * size + size, :] = scratch[pl.ds(src, size), :].astype(bf16)


def same(r):
    return r


def turned(r):
    return ((r & 3) << 1) | (r >> 2)


def ffn_kernel(blocks, half, far, first, bias_row, me, h2, dbl, wup, wdn, bup, *refs):
    dh_in = None if first else refs[0]
    act_o, dh_o, db_o, out0, out1, dpre_s, gup, gdn = refs if first else refs[1:]
    tokens = h2.shape[0]
    hb = act_o.shape[1]
    hid = half ^ me[0] if blocks > 1 else 0
    cols = pl.ds(pl.multiple_of(hid * hb, 128), hb)
    bias = bup[pl.ds(bias_row + hid, 1), :hb].astype(f32)
    if far:
        up = wup[...]
        dn = wdn[...]
    else:
        up = wup[:, cols]
        dn = wdn[cols, :]
    total = jnp.zeros((1, hb), f32)
    for m in range(tokens // CHUNK):
        rows = slice(m * CHUNK, m * CHUNK + CHUNK)
        pre = nt(h2[rows, :], up) if far else nn(h2[rows, :], up)
        act, slope = gelu_parts(pre + bias)
        act_o[rows, :] = act.astype(bf16)
        dpre = (nt(dbl[rows, :], dn) * slope).astype(bf16)
        dpre_s[rows, :] = dpre
        total = total + jnp.sum(dpre.astype(f32), axis=0, keepdims=True)
        back = nn(dpre, up) if far else nt(dpre, up)
        dh_o[rows, :] = back if first else dh_in[rows, :] + back
    db_o[...] = jnp.broadcast_to(total, db_o.shape)
    gup[...] = tn(h2[...], dpre_s[...])
    gdn[...] = tn(act_o[...], dbl[...])
    if blocks == 1:
        out0[...] = gup[...].astype(bf16)
        out1[...] = gdn[...].astype(bf16)
        return

    ours, theirs = (same, turned) if half == 0 else (turned, same)

    @pl.when(me[0] == 0)
    def _():
        put_rows(out0, gup, me[1], blocks, ours)
        put_rows(out1, gdn, me[1], blocks, theirs)

    @pl.when(me[0] != 0)
    def _():
        put_rows(out0, gdn, me[1], blocks, ours)
        put_rows(out1, gup, me[1], blocks, theirs)


def call_ffn(me, blocks, half, far, h2, dbl, wup, wdn, bup, dh, hb, bias_row):
    tokens, width = h2.shape
    first = dh is None
    return call(
        functools.partial(ffn_kernel, blocks, half, far, first, bias_row),
        [((tokens, hb), bf16), ((tokens, width), f32), ((8, hb), f32)]
        + ([((width, hb), bf16)] * 2 if hb == width else [((width, hb), bf16), ((hb, width), bf16)]),
        [me, h2, dbl, wup, wdn, bup] + ([] if first else [dh]),
        scratch=[pltpu.VMEM((tokens, hb), bf16), pltpu.VMEM((width, hb), f32), pltpu.VMEM((hb, width), f32)],
        name="feed_forward", us=8,
    )


def send_kernel(me, vec, wup, wdn, own, diag, cols, sem):
    size = own.shape[0]
    pairs = [(own, me[3]), (diag, me[3] ^ 3)]

    @pl.when(me[0] == 0)
    def _():
        copies = [
            pltpu.make_async_copy(wup.at[:, pl.ds(pl.multiple_of(quarter * size, 128), size)], cols.at[i], sem.at[i])
            for i, (out, quarter) in enumerate(pairs)
        ]
        for copy in copies:
            copy.start()
        for i, (out, quarter) in enumerate(pairs):
            copies[i].wait()
            out[:size, :] = cols[i].T

    @pl.when(me[0] != 0)
    def _():
        copies = [
            pltpu.make_async_copy(
                wdn.at[pl.ds(pl.multiple_of(quarter * size, 128), size), :], out.at[pl.ds(0, size), :], sem.at[i]
            )
            for i, (out, quarter) in enumerate(pairs)
        ]
        for copy in copies:
            copy.start()
        for copy in copies:
            copy.wait()

    diag[size : size + 16, :] = vec[...].astype(bf16)


def call_send(me, vec, wup, wdn):
    width = wup.shape[0]
    size = wup.shape[1] // 4
    return pl.pallas_call(
        send_kernel,
        in_specs=[
            pl.BlockSpec(memory_space=pltpu.SMEM), pl.BlockSpec(memory_space=pltpu.VMEM),
            pl.BlockSpec(memory_space=pl.ANY), pl.BlockSpec(memory_space=pl.ANY),
        ],
        out_specs=[pl.BlockSpec(memory_space=pltpu.VMEM)] * 2,
        out_shape=[jax.ShapeDtypeStruct((size, width), bf16), jax.ShapeDtypeStruct((size + 16, width), bf16)],
        scratch_shapes=[pltpu.VMEM((2, width, size), bf16), pltpu.SemaphoreType.DMA((2,))],
        compiler_params=pltpu.CompilerParams(vmem_limit_bytes=LIMIT),
        cost_estimate=pl.CostEstimate(flops=int(1.15e9), bytes_accessed=0, transcendentals=0),
        name="weight_parts",
    )(me, vec, wup, wdn)


def far_kernel(me, *refs):
    size = refs[0].shape[0]
    ups = refs[8:10]
    downs = refs[10:12]
    for r in range(4):
        quarter = me[3] ^ r
        half = (quarter >> 1) ^ me[0]
        at = pl.ds(pl.multiple_of((quarter & 1) * size, 16), size)
        mine = refs[r]
        other = refs[4 + r]
        for h in range(2):
            @pl.when(jnp.logical_and(half == h, me[0] == 0))
            def _():
                ups[h][at, :] = mine[:size, :]
                downs[h][at, :] = other[:size, :]

            @pl.when(jnp.logical_and(half == h, me[0] != 0))
            def _():
                ups[h][at, :] = other[:size, :]
                downs[h][at, :] = mine[:size, :]


def call_far(me, pieces):
    size, width = pieces[0].shape
    return call(far_kernel, [((2 * size, width), bf16)] * 4, [me] + pieces, name="far_weights", us=2)


def backward_kernel(mod, vec, tok, dy, attn, dh, q_i, k_i, v_i, p_i, wout, cos, sin, dmid_o, dqkv_o, dattn_o, sums):
    width = tok.shape[1]
    cols = width // 128
    low, first = lane_masks((SLOT, 128))
    sums[...] = jnp.zeros_like(sums)

    def one(i, _):
        cr = chunk(i)
        attnv = attn[cr, :]
        gate1 = mod[2:3, :]
        unit, rs = whiten(tok[cr, :].astype(f32) + gate1 * attnv)
        dh2 = dh[cr, :]
        dmid = dy[cr, :].astype(f32) + whiten_back(dh2 * (vec[7:8, :] * (1.0 + mod[4:5, :])), unit, rs)
        dmid_o[cr, :] = dmid
        add_row(sums, 0, dh2)
        add_row(sums, 1, dh2 * unit)
        add_row(sums, 2, dmid * attnv)
        dattn = (dmid * gate1).astype(bf16)
        dattn_o[cr, :] = dattn
        datt = nt(dattn, wout[...]).astype(bf16)
        cosv = cos[...]
        sinv = sin[...]
        for s in range(CHUNK // SLOT):
            rows = pl.ds(pl.multiple_of(i * CHUNK + s * SLOT, SLOT), SLOT)
            for j in range(cols):
                sl = slice(128 * j, 128 * j + 128)
                do = datt[s * SLOT : s * SLOT + SLOT, sl]
                dp = nt(do, split_heads(v_i[rows, sl], low))
                pl_low = p_i[rows, 256 * j : 256 * j + 256]
                pr = pl_low.astype(f32)
                ds = []
                for e in range(2):
                    ee = slice(SLOT * e, SLOT * e + SLOT)
                    d = jnp.sum(pr[:, ee] * dp[:, ee], axis=-1, keepdims=True)
                    ds.append((pr[:, ee] * (dp[:, ee] - d)).astype(bf16))
                ds = jnp.concatenate(ds, axis=1)
                dq = nn(ds, split_heads(k_i[rows, sl], low)) * 0.125
                dk = tn(ds, q_i[rows, sl])
                dk = jnp.where(low, dk[:SLOT], dk[SLOT:]) * 0.125
                dv = tn(pl_low, do)
                dv = jnp.where(low, dv[:SLOT], dv[SLOT:])
                dq = dq * cosv - half_turn(dq, first) * sinv
                dk = dk * cosv - half_turn(dk, first) * sinv
                dqkv_o[rows, sl] = dq.astype(bf16)
                dqkv_o[rows, width + 128 * j : width + 128 * j + 128] = dk.astype(bf16)
                dqkv_o[rows, 2 * width + 128 * j : 2 * width + 128 * j + 128] = dv.astype(bf16)
        return 0

    lax.fori_loop(0, tok.shape[0] // CHUNK, one, 0)


def call_backward(mod, vec, tok, dy, attn, dh, q, k, v, p, wout, cos, sin):
    tokens, width = tok.shape
    return call(
        backward_kernel,
        [((tokens, width), f32), ((tokens, 3 * width), bf16), ((tokens, width), bf16), ((8, width), f32)],
        [mod, vec, tok, dy, attn, dh, q, k, v, p, wout, cos, sin],
        scalars=0,
        name="attention_backward", us=24,
    )


def pair_kernel(blocks, c0, c1, me, a0, b0, a1, b1, out0, out1, acc0, acc1):
    width = out0.shape[1]
    acc0[...] = tn(a0[...], b0[:, c0 * width : c0 * width + width])
    acc1[...] = tn(a1[...], b1[:, c1 * width : c1 * width + width])

    @pl.when(me[0] == 0)
    def _():
        put_rows(out0, acc0, me[2], blocks, same)
        put_rows(out1, acc1, me[2], blocks, same)

    @pl.when(me[0] != 0)
    def _():
        put_rows(out0, acc1, me[2], blocks, same)
        put_rows(out1, acc0, me[2], blocks, same)


def call_pair(me, blocks, first, second):
    a0, b0, c0 = first
    a1, b1, c1 = second
    width = a0.shape[1]
    return call(
        functools.partial(pair_kernel, blocks, c0, c1),
        [((width, width), bf16)] * 2,
        [me, a0, b0, a1, b1],
        scratch=[pltpu.VMEM((width, width), f32)] * 2,
        name="weight_grads", us=4,
    )


def tokens_kernel(mod, vec, tok, dmid, dqkv, wqkv, dtok_o, sums):
    sums[...] = jnp.zeros_like(sums)
    for m in range(tok.shape[0] // CHUNK):
        cr = slice(m * CHUNK, m * CHUNK + CHUNK)
        dh1 = nt(dqkv[cr, :], wqkv[...])
        unit, rs = whiten(tok[cr, :].astype(f32))
        add_row(sums, 0, dh1)
        add_row(sums, 1, dh1 * unit)
        dtok_o[cr, :] = (dmid[cr, :] + whiten_back(dh1 * (vec[6:7, :] * (1.0 + mod[1:2, :])), unit, rs)).astype(bf16)


def call_tokens(mod, vec, tok, dmid, dqkv, wqkv):
    tokens, width = tok.shape
    return call(
        tokens_kernel, [((tokens, width), bf16), ((8, width), f32)], [mod, vec, tok, dmid, dqkv, wqkv],
        scalars=0, name="token_grads", us=6, limit=18 * 1024 * 1024,
    )


def result_kernel(parts, far, me, mod, vec, tok, dy, attn, *refs):
    acts = refs[:parts]
    downs = refs[parts:-2]
    out_o, sums = refs[-2:]
    hb = acts[0].shape[1]
    sums[...] = jnp.zeros_like(sums)

    for m in range(tok.shape[0] // CHUNK):
        cr = slice(m * CHUNK, m * CHUNK + CHUNK)
        branch = vec[8:9, :] + jnp.zeros((CHUNK, tok.shape[1]), f32)
        for n in range(parts):
            if far:
                dn = downs[0][chunk(n ^ me[0], hb), :] if n < 2 else downs[n - 1][...]
            else:
                dn = downs[n][...]
            branch = branch + nn(acts[n][cr, :], dn)
        out_o[cr, :] = (
            tok[cr, :].astype(f32) + mod[2:3, :] * attn[cr, :] + mod[5:6, :] * branch
        ).astype(bf16)
        add_row(sums, 0, dy[cr, :].astype(f32) * branch)


def call_result(me, far, mod, vec, tok, dy, attn, acts, downs):
    tokens, width = tok.shape
    return call(
        functools.partial(result_kernel, len(acts), far),
        [((tokens, width), bf16), ((8, width), f32)],
        [me, mod, vec, tok, dy, attn] + acts + downs,
        name="output_rows", us=7, limit=18 * 1024 * 1024,
    )


def ffn_out_kernel(me, *refs):
    up_o, down_o = refs[4:]
    width = refs[0].shape[1]
    size = width // 8
    for a in range(2):
        for z in range(4):
            at = pl.multiple_of(lax.bitwise_xor(a * 4 + z, me[1]) * size, size)
            for t in range(2):
                src = slice((2 * z + t) * size, (2 * z + t) * size + size)

                @pl.when(me[0] == 0)
                def _():
                    up_o[pl.ds(at, size), t * width : t * width + width] = refs[a][src, :].astype(f32)
                    down_o[pl.ds((1 - t) * width + at, size), :] = refs[2 + a][src, :].astype(f32)

                @pl.when(me[0] != 0)
                def _():
                    up_o[pl.ds(at, size), t * width : t * width + width] = refs[2 + a][src, :].astype(f32)
                    down_o[pl.ds((1 - t) * width + at, size), :] = refs[a][src, :].astype(f32)


def call_ffn_out(me, pieces):
    width = pieces[0].shape[1]
    return call(
        ffn_out_kernel, [((width, 2 * width), f32), ((2 * width, width), f32)], [me] + pieces,
        name="feed_forward_grads", us=5, limit=24 * 1024 * 1024,
    )


def attn_out_kernel(me, *refs):
    qkv_o, out_o = refs[16:]
    width = out_o.shape[1]
    size = width // 16
    for pair in range(2):
        every = refs[8 * pair].shape[0] // 4
        for n, xy in enumerate((0, 8, 4, 12)):
            for z in range(4):
                at = pl.ds(pl.multiple_of(lax.bitwise_xor(xy + z, me[2]) * size, size), size)
                src = slice(z * every, z * every + size)

                for core in range(2):
                    @pl.when(me[0] == core)
                    def _():
                        first = refs[8 * pair + 4 * core + n][src, :].astype(f32)
                        second = refs[8 * pair + 4 * (1 - core) + n][src, :].astype(f32)
                        if pair == 1:
                            qkv_o[at, :width] = first
                            qkv_o[at, width : 2 * width] = second
                        else:
                            qkv_o[at, 2 * width :] = first
                            out_o[at, :] = second


def call_attn_out(me, pieces):
    width = pieces[0].shape[1]
    return call(
        attn_out_kernel, [((width, 3 * width), f32), ((width, width), f32)], [me] + pieces,
        name="attention_grads", us=6, limit=24 * 1024 * 1024,
    )


def split2(a):
    high = a.astype(bf16)
    return high, (a - high.astype(f32)).astype(bf16)


def pack_kernel(ts, tab, mod, vec, bd, sums1, sums2, sums3, d0, d1, d2, d3, out):
    rows = [
        sums1[0:1, :], sums1[1:2, :] * vec[6:7, :], sums2[2:3, :], sums2[0:1, :], sums2[1:2, :] * vec[7:8, :],
        sums3[0:1, :], sums1[1:2, :] * (1.0 + mod[1:2, :]), sums2[1:2, :] * (1.0 + mod[4:5, :]), bd[0:1, :],
        jnp.zeros_like(bd[0:1, :]), d0[0:1, :], d1[0:1, :], d2[0:1, :], d3[0:1, :], bd[0:1, :], bd[0:1, :],
    ]
    out[...] = jnp.concatenate(rows, axis=0).astype(bf16)
    cond = tab[pl.ds(ts[0], 1), :]
    high, low = split2(cond)
    lane = lax.broadcasted_iota(jnp.int32, (1, 128), 1)
    step = jnp.where(lane == 0, ts[0] // 128, jnp.where(lane == 1, lax.rem(ts[0], 128), 0)).astype(f32)
    out[9:10, :128] = high
    out[9:10, 128:256] = low
    out[9:10, 256:384] = step.astype(bf16)


def call_pack(ts, tab, mod, vec, bd, sums1, sums2, sums3, db):
    width = mod.shape[1]
    return call(
        pack_kernel, [((16, width), bf16)], [ts, tab, mod, vec, bd, sums1, sums2, sums3] + db, name="small_rows"
    )[0]


def small_kernel(me, ada_w, *refs):
    table_o, gains_o, bias_o, ada_w_o, ada_b_o, rows_s = refs[8:]
    width = gains_o.shape[1]
    every = refs[0].shape[0] // 4
    bias = [jnp.zeros((1, width), f32), jnp.zeros((1, width), f32)]
    for n in range(8):
        for z in range(4):
            at = 4 * n + z
            pack = refs[n][z * every + every - 16 : z * every + every, :].astype(f32)
            for kind in range(10):
                rows_s[kind, at : at + 1, :] = pack[kind : kind + 1, :]
            base = 10 if (n & 2) == 0 else 12
            for h in range(2):
                to = h if n < 4 else 1 - h
                bias[to] = bias[to] + pack[base + h : base + h + 1, :]
    for h in range(2):
        bias_o[h : h + 1, :] = jnp.where(me[0] == 0, bias[h], bias[1 - h])
    for kind in range(3):
        gains_o[kind : kind + 1, :] = jnp.sum(rows_s[6 + kind], axis=0, keepdims=True)
    extra = rows_s[9]
    high = extra[:, :128].astype(bf16)
    low = extra[:, 128:256].astype(bf16)
    step = extra[:, 256:257] * 128.0 + extra[:, 257:258]
    total = jnp.zeros((32, 128), f32)
    for kind in range(6):
        grad = rows_s[kind].astype(bf16)
        cols = slice(kind * width, kind * width + width)
        ada_b_o[kind : kind + 1, :] = jnp.sum(rows_s[kind], axis=0, keepdims=True)
        ada_w_o[:, cols] = tn(high, grad) + tn(low, grad)
        whigh, wlow = split2(ada_w[:, cols])
        total = total + nt(grad, whigh) + nt(grad, wlow)
    lane = lax.broadcasted_iota(jnp.int32, (32, 1024), 1)
    hot = jnp.where(lane.astype(f32) == step, 1.0, 0.0).astype(bf16)
    thigh, tlow = split2(total)
    table_o[...] = (tn(hot, thigh) + tn(hot, tlow))[: table_o.shape[0], :]


def call_small(me, ada_w, pieces, entries):
    width = pieces[0].shape[1]
    return call(
        small_kernel,
        [
            ((entries, 128), f32), ((8, width), f32), ((2, width), f32), ((128, 6 * width), f32), ((6, width), f32),
        ],
        [me, ada_w] + pieces, scratch=[pltpu.VMEM((10, 32, width), f32)], name="small_grads", us=4,
        limit=16 * 1024 * 1024,
    )


def swap(array, mask):
    return lax.ppermute(array, ("seq", "mlp"), [(i, i ^ mask) for i in range(32)])


def combine_kernel(sizes, *refs):
    outs = refs[sum(sizes):]
    rows = outs[0].shape[0]
    at = 0
    base = 0
    for n in sizes:
        group = refs[at : at + n]
        at += n
        size = group[0].shape[0]
        step = min(size, rows)
        for r in range(0, size, step):
            part = slice(r, r + step)
            if n == 1:
                value = group[0][part, :]
            else:
                value = group[0][part, :].astype(f32)
                for other in group[1:]:
                    value = value + other[part, :].astype(f32)
                value = value.astype(outs[0].dtype)
            out = (base + r) // rows
            to = base + r - out * rows
            outs[out][to : to + step, :] = value
        base += size


def combine(groups, pieces=1):
    arrays = [a for group in groups for a in group]
    rows = sum(group[0].shape[0] for group in groups)
    shape = (rows // pieces, arrays[0].shape[1])
    out = call(
        functools.partial(combine_kernel, [len(group) for group in groups]),
        [(shape, arrays[0].dtype)] * pieces, arrays, scalars=0, name="sums",
    )
    return out if pieces > 1 else out[0]


class Order:
    def __init__(self):
        self.last = None

    def run(self, function, *args, **kwargs):
        leaves, tree = jax.tree.flatten(list(args))
        if self.last is not None:
            at = [i for i, a in enumerate(leaves) if isinstance(a, jax.Array)][0]
            leaves[at] = tie(leaves[at], self.last)
        args = jax.tree.unflatten(tree, leaves)
        out = function(*args, **kwargs)
        self.last = min(out, key=lambda a: a.size) if isinstance(out, (list, tuple)) else out
        return out

    def swap(self, array, *masks):
        if self.last is not None:
            array = tie(array, self.last)
        out = [swap(array, mask) for mask in masks]
        return out if len(out) > 1 else out[0]


def tie(array, *after):
    return lax.optimization_barrier((array,) + after)[0]


def rope_tables(width):
    half = 32
    freq = np.float32(10000.0) ** (-np.arange(half, dtype=np.float32) / np.float32(half))
    angle = np.arange(SLOT, dtype=np.float32)[:, None] * freq[None, :]
    cos = np.cos(angle).astype(np.float32)
    sin = np.sin(angle).astype(np.float32)
    return (
        jnp.asarray(np.concatenate([cos, cos, cos, cos], axis=1)),
        jnp.asarray(np.concatenate([-sin, sin, -sin, sin], axis=1)),
    )


def shards(
    tuned, tokens, time_table, timesteps, lengths, ln1_gain, ln2_gain, w_qkv, w_out, w_up, b_up, w_down, b_down,
    ada_w, ada_b, out_grad,
):
    width = tokens.shape[1]
    local = w_up.shape[1]
    cos, sin = rope_tables(width)
    ups = local // min(local, width)
    vec = jnp.concatenate([
        ada_b.reshape(6, width), ln1_gain[None], ln2_gain[None], b_down[None].astype(f32),
        jnp.pad(b_up.reshape(ups, -1).astype(f32), ((0, 7 - ups), (0, width - local // ups))),
    ])
    seq = lax.axis_index("seq")
    mlp = lax.axis_index("mlp")
    cond = lax.dynamic_slice_in_dim(time_table, timesteps[0], 1, 0)
    if tuned:
        core = seq & 1
        x = (seq >> 1) & 1
        z = seq >> 2
        me = jnp.stack([core, x * 4 + z, x * 8 + mlp * 4 + z, x * 2 + (z & 1)]).astype(jnp.int32)
        order = Order()
        run = order.run
        send = order.swap
        own, diag = run(call_send, me, vec, w_up, w_down)
        own = send(own, Y)
        diag = send(diag, Y)
        (mod,) = run(
            lambda *a: call(mod_kernel, [((8, width), f32)], list(a), name="modulation"),
            timesteps, time_table, ada_w, vec,
        )
        h1, q, k, v, p, att, attn, h2, dbl, bd = run(
            call_forward, lengths, mod, vec, tokens, out_grad, w_qkv, w_out, cos, sin
        )
        own_x = send(own, X)
        own_z = send(own, Z0)
        own_c = send(own, CORE)
        hb = local // 2
        zs = (Z0, Z1, Z0 | Z1)
        xys = (Y, X, X | Y)
        act0, dh, db0, na0, na1 = run(call_ffn, me, 8, 0, False, h2, dbl, w_up, w_down, vec, None, hb, 9)
        na1 = send(na1, CORE)
        diag_c = send(diag, CORE)
        act1, dh, db1, nb0, nb1 = run(call_ffn, me, 8, 1, False, h2, dbl, w_up, w_down, vec, dh, hb, 9)
        nb1 = send(nb1, CORE)
        x_c = send(own_x, CORE)
        z_c = send(own_z, CORE)
        n1 = run(combine, [[nb0, na1]], 4)
        n1 = [n1[0]] + [send(a, m) for a, m in zip(n1[1:], zs)]
        up_a, up_b, down_a, down_b = run(
            call_far, me, [own, own_z, own_x, diag, own_c, z_c, x_c, diag_c]
        )
        far_vec = diag[diag.shape[0] - 16 :][9:].astype(f32)
        n0a, n0b = run(combine, [[na0, nb1]], 2)
        n0b = send(n0b, X)
        act2, dh, db2, fa0, fa1 = run(call_ffn, me, 8, 0, True, h2, dbl, up_a, down_a, far_vec, dh, hb, 0)
        fa1 = send(fa1, CORE)
        act3, dh, db3, fb0, fb1 = run(call_ffn, me, 8, 1, True, h2, dbl, up_b, down_b, far_vec, dh, hb, 0)
        fb1 = send(fb1, CORE)
        f1 = run(combine, [[fb0, fa1]], 4)
        f1 = [f1[0]] + [send(a, m) for a, m in zip(f1[1:], zs)]
        f0a, f0b = run(combine, [[fa0, fb1]], 2)
        f0b = send(f0b, X)
        dmid, dqkv, dattn, sums2 = run(
            call_backward, mod, vec, tokens, out_grad, attn, dh, q, k, v, p, w_out, cos, sin
        )
        f0 = run(combine, [[f0a, f0b]])
        f0 = send(f0, Y)
        f1 = run(combine, [f1])
        f1 = send(f1, Y)
        g0, g1 = run(call_pair, me, 16, (h1, dqkv, 2), (att, dattn, 0))
        g1 = send(g1, CORE)
        e0, e1 = run(call_pair, me, 16, (h1, dqkv, 0), (h1, dqkv, 1))
        e1 = send(e1, CORE)
        g = run(combine, [[g0, g1]], 4)
        g = [g[0]] + [send(a, m) for a, m in zip(g[1:], xys)]
        e = run(combine, [[e0, e1]], 4)
        e = [e[0]] + [send(a, m) for a, m in zip(e[1:], xys)]
        p0 = run(combine, [[n0a, n0b, f0]], 4)
        p0 = [p0[0]] + [send(a, m) for a, m in zip(p0[1:], zs)]
        p1a, p1b = run(combine, [n1 + [f1]], 2)
        p1b = send(p1b, X)
        tok_grad, sums1 = run(call_tokens, mod, vec, tokens, dmid, dqkv, w_qkv)
        g = run(combine, [g], 4)
        g = [g[0]] + [send(a, m) for a, m in zip(g[1:], zs)]
        result, sums3 = run(
            call_result, me, True, mod, vec, tokens, out_grad, attn, [act0, act1, act2, act3],
            [w_down, down_a, down_b],
        )
        e = run(combine, [e], 4)
        e = [e[0]] + [send(a, m) for a, m in zip(e[1:], zs)]
        pack = run(call_pack, timesteps, time_table, mod, vec, bd, sums1, sums2, sums3, [db0, db1, db2, db3])
        g = run(combine, [g, [pack]])
        g = [g] + send(g, *zs)
        ffn = run(combine, [p0, [p1a, p1b]])
        ffn = [ffn] + send(ffn, *zs)
        e = run(combine, [e])
        e = [e] + send(e, *zs)
        g = run(combine, [[a] for a in g])
        g = [g] + send(g, X, Y, X | Y)
        e = run(combine, [[a] for a in e])
        e = [e] + send(e, X, Y, X | Y)
        ffn = run(combine, [[a] for a in ffn])
        ffn = [ffn, send(ffn, X)]
        g += [send(a, CORE) for a in g]
        table_grad, gains, bias_grad, ada_w_grad, ada_b_grad = run(call_small, me, ada_w, g, time_table.shape[0])
        e += [send(a, CORE) for a in e]
        qkv_wgrad, out_wgrad = run(call_attn_out, me, g + e)
        ffn += [send(a, CORE) for a in ffn]
        up_grad, down_grad = run(call_ffn_out, me, ffn)
        return (
            result, tok_grad, table_grad, gains[0], gains[1], qkv_wgrad, out_wgrad, up_grad, bias_grad.reshape(-1),
            down_grad, gains[2], ada_w_grad, ada_b_grad.reshape(-1),
        )

    me = jnp.zeros((4,), jnp.int32)
    (mod,) = call(
        mod_kernel, [((8, width), f32)], [timesteps, time_table, ada_w, vec], name="modulation"
    )
    h1, q, k, v, p, att, attn, h2, dbl, bd = call_forward(
        lengths, mod, vec, tokens, out_grad, w_qkv, w_out, cos, sin
    )
    n = lax.axis_size("mlp")
    dh, acts, downs, up_sum, down_sum, bup_sum = None, [], [], 0.0, 0.0, 0.0
    for r in range(n):
        there = [(i, (i + r) % n) for i in range(n)]
        back = [((i + r) % n, i) for i in range(n)]
        move = lambda a: lax.ppermute(a, "mlp", there) if r else a
        home = lambda a: lax.ppermute(a, "mlp", back) if r else a
        downs.append(move(w_down))
        act, dh, db, g_up, g_down = call_ffn(
            me, 1, 0, True, h2, dbl, move(w_up).T, downs[-1], move(vec), dh, local, 9
        )
        acts.append(act)
        up_sum = up_sum + home(g_up).astype(f32)
        down_sum = down_sum + home(g_down).astype(f32)
        bup_sum = bup_sum + home(db[0])
    dmid, dqkv, dattn, sums2 = call_backward(mod, vec, tokens, out_grad, attn, dh, q, k, v, p, w_out, cos, sin)
    w0, w1 = call_pair(me, 1, (h1, dqkv, 0), (h1, dqkv, 1))
    w2, w3 = call_pair(me, 1, (h1, dqkv, 2), (att, dattn, 0))
    tok_grad, sums1 = call_tokens(mod, vec, tokens, dmid, dqkv, w_qkv)
    result, sums3 = call_result(me, False, mod, vec, tokens, out_grad, attn, acts, downs)
    up_grad, down_grad, bias_grad = lax.psum((up_sum, down_sum, bup_sum), "seq")
    mod_grad = jnp.concatenate([
        sums1[0], sums1[1] * ln1_gain, sums2[2], sums2[0], sums2[1] * ln2_gain, sums3[0],
    ])[None]
    gains = jnp.stack([sums1[1] * (1.0 + mod[1]), sums2[1] * (1.0 + mod[4]), bd[0]])
    hot = (timesteps[:, None] == jnp.arange(time_table.shape[0], dtype=jnp.int32)[None, :]).astype(f32)
    qkv_wgrad = jnp.concatenate([w0, w1, w2], axis=1).astype(f32)
    qkv_wgrad, out_wgrad, ada_w_grad, ada_b_grad, table_grad, gains = lax.psum(
        (
            qkv_wgrad, w3.astype(f32), jnp.dot(cond.T, mod_grad, precision=HIGH), mod_grad[0],
            jnp.dot(hot.T, jnp.dot(mod_grad, ada_w.T, precision=HIGH), precision=HIGH), gains,
        ),
        ("seq", "mlp"),
    )
    return (
        result, tok_grad, table_grad, gains[0], gains[1], qkv_wgrad, out_wgrad, up_grad, bias_grad, down_grad,
        gains[2], ada_w_grad, ada_b_grad,
    )


def solution(mesh):
    tuned = mesh.shape["seq"] == 16 and mesh.shape["mlp"] == 2
    rows = P(("seq", "mlp"), None)
    flat = P(("seq", "mlp"))

    def whole(
        tokens, time_table, timesteps, lengths, ln1_gain, ln2_gain, w_qkv, w_out, w_up, b_up, w_down, b_down,
        ada_w, ada_b, out_grad,
    ):
        return shards(
            tuned, tokens, time_table, timesteps, lengths, ln1_gain, ln2_gain, w_qkv, w_out, w_up, b_up, w_down,
            b_down, ada_w, ada_b, out_grad,
        )

    return jax.shard_map(
        whole,
        mesh=mesh,
        in_specs=(
            rows, P(), flat, flat, P(), P(), P(), P(), P(None, "mlp"), P("mlp"), P("mlp", None), P(), P(), P(), rows,
        ),
        out_specs=(
            rows, rows, P(), P(), P(), P(), P(), P(None, "mlp"), P("mlp"), P("mlp", None), P(), P(), P(),
        ),
        check_vma=False,
    )
```

```python
import functools

import jax
import jax.numpy as jnp
import numpy as np
from jax import lax
from jax.experimental import pallas as pl
from jax.experimental.pallas import tpu as pltpu
from jax.sharding import PartitionSpec as P

H = 12
SLOT = 128
HIGH = lax.Precision.HIGHEST
f32 = jnp.float32
bf16 = jnp.bfloat16
Y, CORE, X, Z0, Z1 = 1, 2, 4, 8, 16
LIMIT = 12 * 1024 * 1024
CHUNK = 256
SCALE = 0.01
FORWARD = 33 * 1024 * 1024
GROUP = 6


def nn(a, b):
    return jnp.dot(a, b, preferred_element_type=f32)


def nt(a, b):
    return lax.dot_general(a, b, (((1,), (1,)), ((), ())), preferred_element_type=f32)


def tn(a, b):
    return lax.dot_general(a, b, (((0,), (0,)), ((), ())), preferred_element_type=f32)


def whiten(x):
    center = x - jnp.mean(x, axis=-1, keepdims=True)
    spread = jnp.mean(center * center, axis=-1, keepdims=True)
    rs = lax.rsqrt(spread + 1e-06)
    return center * rs, rs


def whiten_back(grad, unit, rs):
    return rs * (
        grad
        - jnp.mean(grad, axis=-1, keepdims=True)
        - unit * jnp.mean(grad * unit, axis=-1, keepdims=True)
    )


def half_turn(u, first):
    return jnp.where(first, pltpu.roll(u, 96, 1), pltpu.roll(u, 32, 1))


def split_heads(u, low):
    zero = jnp.zeros_like(u)
    return jnp.concatenate([jnp.where(low, u, zero), jnp.where(low, zero, u)], axis=0)


def lane_masks(shape):
    lane = lax.broadcasted_iota(jnp.int32, shape, 1)
    return lane < 64, lax.rem(lane, 64) < 32


def call(body, outs, args, scalars=1, scratch=(), limit=LIMIT, name=None, us=1):
    specs = [pl.BlockSpec(memory_space=pltpu.SMEM)] * scalars
    specs += [pl.BlockSpec(memory_space=pltpu.VMEM)] * (len(args) - scalars)
    return pl.pallas_call(
        body,
        in_specs=specs,
        out_specs=[pl.BlockSpec(memory_space=pltpu.VMEM)] * len(outs),
        out_shape=[jax.ShapeDtypeStruct(*o) for o in outs],
        scratch_shapes=list(scratch),
        compiler_params=pltpu.CompilerParams(vmem_limit_bytes=limit),
        cost_estimate=pl.CostEstimate(flops=int(us * SCALE * 1.15e9), bytes_accessed=0, transcendentals=0),
        name=name,
    )(*args)


def chunk(i, size=CHUNK):
    return pl.ds(pl.multiple_of(i * size, size), size)


def add_row(ref, at, value):
    ref[at : at + 1, :] = ref[at : at + 1, :] + jnp.sum(value, axis=0, keepdims=True)


def mod_rows(row, ada_w, vec, mod_o):
    width = mod_o.shape[1]
    cols = width // 128
    col = jnp.broadcast_to(row, (128, 128)).T
    for j in range(6 * cols):
        sl = slice(128 * j, 128 * j + 128)
        out = jnp.sum(ada_w[:, sl] * col, axis=0, keepdims=True)
        to = slice(128 * (j % cols), 128 * (j % cols) + 128)
        mod_o[j // cols : j // cols + 1, to] = out + vec[j // cols : j // cols + 1, to]
    mod_o[6:8, :] = jnp.zeros((2, width), f32)


def forward_kernel(
    lens, ts, me, ada_b, gain1, gain2, bdown, bup, cos, sin, tab_h, ada_h, tok_h, dy_h, wqkv_h, wout_h, wup_h, wdn_h,
    h1_o, q_o, k_o, v_o, p_o, att_o, attn_o, h2_o, dbl_o, bd_o, mod, vec, ups, downs,
    tab, ada_w, tok, dy, wqkv, wout, sem,
):
    loads = [
        pltpu.make_async_copy(tab_h.at[pl.ds(pl.multiple_of(ts[0] // 8 * 8, 8), 8), :], tab, sem.at[0]),
        pltpu.make_async_copy(ada_h, ada_w, sem.at[1]),
        pltpu.make_async_copy(tok_h, tok, sem.at[2]),
        pltpu.make_async_copy(wqkv_h, wqkv, sem.at[3]),
        pltpu.make_async_copy(dy_h, dy, sem.at[4]),
        pltpu.make_async_copy(wout_h, wout, sem.at[5]),
    ]
    size = ups.shape[2]
    for h in range(ups.shape[0]):
        at = pl.ds(pl.multiple_of((h ^ me[0]) * size, 128), size)
        loads.append(pltpu.make_async_copy(wup_h.at[:, at], ups.at[h], sem.at[6 + 2 * h]))
        loads.append(pltpu.make_async_copy(wdn_h.at[at, :], downs.at[h], sem.at[7 + 2 * h]))
    for load in loads[:2]:
        load.start()
    vec_rows(ada_b, gain1, gain2, bdown, bup, vec)
    loads[0].wait()
    loads[1].wait()
    for load in loads[2:4]:
        load.start()
    mod_rows(tab[pl.ds(lax.rem(ts[0], 8), 1), :], ada_w, vec, mod)
    for load in loads[4:]:
        load.start()
    loads[2].wait()
    loads[3].wait()
    width = tok.shape[1]
    cols = width // 128
    low, first = lane_masks((SLOT, 128))
    key_at = lax.broadcasted_iota(jnp.int32, (SLOT, SLOT), 0)
    slots = CHUNK // SLOT
    bd_o[...] = jnp.zeros_like(bd_o)

    def one(i, _):
        cr = chunk(i)
        x = tok[cr, :].astype(f32)
        unit, _ = whiten(x)
        h1 = (unit * (vec[6:7, :] * (1.0 + mod[1:2, :])) + mod[0:1, :]).astype(bf16)
        h1_o[cr, :] = h1
        qkv = nn(h1, wqkv[...])
        cosv = cos[...]
        sinv = sin[...]
        units = [(s, j) for s in range(slots) for j in range(cols)]
        for g0 in range(0, len(units), GROUP):
            part = units[g0 : g0 + GROUP]
            kept = []
            for s, j in part:
                rows = slice(s * SLOT, s * SLOT + SLOT)
                out = pl.ds(pl.multiple_of(i * CHUNK + s * SLOT, SLOT), SLOT)
                sl = slice(128 * j, 128 * j + 128)
                q = qkv[rows, 128 * j : 128 * j + 128]
                k = qkv[rows, width + 128 * j : width + 128 * j + 128]
                v = qkv[rows, 2 * width + 128 * j : 2 * width + 128 * j + 128].astype(bf16)
                q = (q * cosv + half_turn(q, first) * sinv).astype(bf16)
                k = (k * cosv + half_turn(k, first) * sinv).astype(bf16)
                q_o[out, sl] = q
                k_o[out, sl] = k
                v_o[out, sl] = v
                kept.append((nt(split_heads(k, low), q), v))
            probs = []
            for (s, j), (sc, v) in zip(part, kept):
                valid = key_at < lens[i * slots + s]
                two = []
                for e in range(2):
                    x2 = jnp.where(valid, sc[SLOT * e : SLOT * e + SLOT, :], -1e30)
                    ex = jnp.exp((x2 - jnp.max(x2, axis=0, keepdims=True)) * 0.125)
                    two.append((ex * (1.0 / jnp.sum(ex, axis=0, keepdims=True))).astype(bf16))
                pr = jnp.concatenate(two, axis=0)
                at = ((i * slots + s) * cols + j) * 256
                p_o[pl.ds(pl.multiple_of(at, 256), 256), :] = pr
                probs.append(pr)
            for (s, j), (sc, v), pr in zip(part, kept, probs):
                out = pl.ds(pl.multiple_of(i * CHUNK + s * SLOT, SLOT), SLOT)
                att_o[out, 128 * j : 128 * j + 128] = tn(pr, split_heads(v, low)).astype(bf16)
        if i == 0:
            loads[5].wait()
            loads[4].wait()
        attn = nn(att_o[cr, :], wout[...])
        attn_o[cr, :] = attn
        unit2, _ = whiten(x + mod[2:3, :] * attn)
        h2_o[cr, :] = (unit2 * (vec[7:8, :] * (1.0 + mod[4:5, :])) + mod[3:4, :]).astype(bf16)
        dbl = (dy[cr, :].astype(f32) * mod[5:6, :]).astype(bf16)
        dbl_o[cr, :] = dbl
        add_row(bd_o, 0, dbl.astype(f32))
        return 0

    for i in range(tok.shape[0] // CHUNK):
        one(i, 0)
    for load in loads[6:]:
        load.wait()


def call_forward(lens, ts, me, small, cos, sin, tab, ada_w, tok, dy, wqkv, wout, wup, wdn, halves):
    tokens, width = tok.shape
    hb = wup.shape[1] // halves
    s = jax.ShapeDtypeStruct
    low = s((tokens, width), bf16)
    args = [lens, ts, me, *small, cos, sin, tab, ada_w, tok, dy, wqkv, wout, wup, wdn]
    return pl.pallas_call(
        forward_kernel,
        in_specs=[pl.BlockSpec(memory_space=pltpu.SMEM)] * 3
        + [pl.BlockSpec(memory_space=pltpu.VMEM)] * 7
        + [pl.BlockSpec(memory_space=pltpu.HBM)] * 8,
        out_specs=[pl.BlockSpec(memory_space=pltpu.VMEM)] * 14,
        out_shape=[
            low, low, low, low, s((tokens * H, SLOT), bf16), low, s((tokens, width), f32), low, low,
            s((8, width), f32), s((8, width), f32), s((16, width), f32), s((halves, width, hb), bf16), s((halves, hb, width), bf16),
        ],
        scratch_shapes=[
            pltpu.VMEM((8, 128), f32), pltpu.VMEM(ada_w.shape, f32), pltpu.VMEM(tok.shape, bf16),
            pltpu.VMEM(dy.shape, bf16), pltpu.VMEM(wqkv.shape, bf16), pltpu.VMEM(wout.shape, bf16),
            pltpu.SemaphoreType.DMA((6 + 2 * halves,)),
        ],
        compiler_params=pltpu.CompilerParams(vmem_limit_bytes=FORWARD),
        cost_estimate=pl.CostEstimate(flops=int(12 * SCALE * 1.15e9), bytes_accessed=0, transcendentals=0),
        name="attention_forward",
    )(*args)


def gelu_parts(v):
    c = 0.7978845608028654
    v2 = v * v
    t = jnp.tanh(v * (c + c * 0.044715 * v2))
    h = 0.5 + 0.5 * t
    act = v * h
    slope = h + act * (1.0 - h) * (2.0 * c + 6.0 * c * 0.044715 * v2)
    return act, slope


def put_rows(outs, scratch, me, blocks, place):
    size = scratch.shape[0] // blocks
    for r in range(blocks):
        src = pl.multiple_of(lax.bitwise_xor(r, me) * size, size)
        half, at = divmod(place(r), blocks // 2)
        outs[half][at * size : at * size + size, :] = scratch[pl.ds(src, size), :].astype(bf16)


def same(r):
    return r


def ffn_first(r):
    return (r & 4) | ((r & 1) << 1) | ((r & 2) >> 1)


def ffn_second(r):
    return ((r & 1) << 2) | (r & 2) | (r >> 2)


def xy_first(r):
    return (r & 12) | ((r & 1) << 1) | ((r & 2) >> 1)


def yx_first(r):
    return ((r & 4) << 1) | ((r & 8) >> 1) | ((r & 1) << 1) | ((r & 2) >> 1)


def ffn_kernel(blocks, half, far, first, bias_row, me, h2, dbl, wup, wdn, bup, *refs):
    dh_in = None if first else refs[0]
    act_o, dh_o, db_o, *outs, dpre_s, gup, gdn = refs if first else refs[1:]
    tokens = h2.shape[0]
    hb = act_o.shape[1]
    hid = half ^ me[0] if blocks > 1 else 0
    bias = bup[pl.ds(bias_row + hid, 1), :hb].astype(f32)
    up = wup[...] if far else wup[half]
    dn = wdn[...] if far else wdn[half]
    total = jnp.zeros((1, hb), f32)
    for m in range(tokens // CHUNK):
        rows = slice(m * CHUNK, m * CHUNK + CHUNK)
        pre = nt(h2[rows, :], up) if far else nn(h2[rows, :], up)
        act, slope = gelu_parts(pre + bias)
        act_o[rows, :] = act.astype(bf16)
        dpre = (nt(dbl[rows, :], dn) * slope).astype(bf16)
        dpre_s[rows, :] = dpre
        total = total + jnp.sum(dpre.astype(f32), axis=0, keepdims=True)
        back = nn(dpre, up) if far else nt(dpre, up)
        dh_o[rows, :] = back if first else dh_in[rows, :] + back
    db_o[...] = jnp.broadcast_to(total, db_o.shape)
    gup[...] = tn(h2[...], dpre_s[...])
    gdn[...] = tn(act_o[...], dbl[...])
    if blocks == 1:
        outs[0][...] = gup[...].astype(bf16)
        outs[1][...] = gdn[...].astype(bf16)
        return

    ours, theirs = (ffn_first, ffn_second) if half == 0 else (ffn_second, ffn_first)

    @pl.when(me[0] == 0)
    def _():
        put_rows(outs[:2], gup, me[1], blocks, ours)
        put_rows(outs[2:], gdn, me[1], blocks, theirs)

    @pl.when(me[0] != 0)
    def _():
        put_rows(outs[:2], gdn, me[1], blocks, ours)
        put_rows(outs[2:], gup, me[1], blocks, theirs)


def call_ffn(me, blocks, half, far, h2, dbl, wup, wdn, bup, dh, hb, bias_row):
    tokens, width = h2.shape
    first = dh is None
    return call(
        functools.partial(ffn_kernel, blocks, half, far, first, bias_row),
        [((tokens, hb), bf16), ((tokens, width), f32), ((8, hb), f32)]
        + ([((width, hb), bf16), ((hb, width), bf16)] if blocks == 1 else [((width // 2, hb), bf16)] * 4),
        [me, h2, dbl, wup, wdn, bup] + ([] if first else [dh]),
        scratch=[pltpu.VMEM((tokens, hb), bf16), pltpu.VMEM((width, hb), f32), pltpu.VMEM((hb, width), f32)],
        name="feed_forward", us=8,
    )


def vec_rows(ada_b, gain1, gain2, bdown, bup, vec):
    width = vec.shape[1]
    vec[...] = jnp.zeros_like(vec)
    for j in range(6):
        vec[j : j + 1, :] = ada_b[j * width : j * width + width].reshape(1, width)
    vec[6:7, :] = gain1[...].reshape(1, width)
    vec[7:8, :] = gain2[...].reshape(1, width)
    vec[8:9, :] = bdown[...].astype(f32).reshape(1, width)
    size = min(width, bup.shape[0])
    for j in range(bup.shape[0] // size):
        vec[9 + j : 10 + j, :size] = bup[j * size : j * size + size].astype(f32).reshape(1, size)


def send_kernel(me, bup, wup, wdn, own, diag, rows, cols, sem):
    size = own.shape[0]
    pairs = [(own, me[3]), (diag, me[3] ^ 3)]
    @pl.when(me[0] == 0)
    def _():
        copies = [
            pltpu.make_async_copy(wup.at[:, pl.ds(pl.multiple_of(quarter * size, 128), size)], cols.at[i], sem.at[i])
            for i, (out, quarter) in enumerate(pairs)
        ]
        for copy in copies:
            copy.start()
        for i, (out, quarter) in enumerate(pairs):
            copies[i].wait()
            out[:size, :] = cols[i].T

    @pl.when(me[0] != 0)
    def _():
        copies = [
            pltpu.make_async_copy(wdn.at[pl.ds(pl.multiple_of(quarter * size, 128), size), :], rows.at[i], sem.at[i])
            for i, (out, quarter) in enumerate(pairs)
        ]
        for copy in copies:
            copy.start()
        for i, (out, quarter) in enumerate(pairs):
            copies[i].wait()
            out[:size, :] = rows[i]

    width = own.shape[1]
    diag[size : size + 16, :] = jnp.zeros((16, width), bf16)
    for j in range(bup.shape[0] // width):
        diag[size + j : size + j + 1, :] = bup[j * width : j * width + width].reshape(1, width)


def call_send(me, bup, wup, wdn):
    width = wup.shape[0]
    size = wup.shape[1] // 4
    return pl.pallas_call(
        send_kernel,
        in_specs=[pl.BlockSpec(memory_space=pltpu.SMEM), pl.BlockSpec(memory_space=pltpu.VMEM)]
        + [pl.BlockSpec(memory_space=pltpu.HBM)] * 2,
        out_specs=[pl.BlockSpec(memory_space=pltpu.VMEM)] * 2,
        out_shape=[
            jax.ShapeDtypeStruct((size, width), bf16), jax.ShapeDtypeStruct((size + 16, width), bf16),
        ],
        scratch_shapes=[
            pltpu.VMEM((2, size, width), bf16), pltpu.VMEM((2, width, size), bf16), pltpu.SemaphoreType.DMA((2,)),
        ],
        compiler_params=pltpu.CompilerParams(vmem_limit_bytes=60 * 1024 * 1024),
        cost_estimate=pl.CostEstimate(flops=int(SCALE * 1.15e9), bytes_accessed=0, transcendentals=0),
        name="weight_parts",
    )(me, bup, wup, wdn)


def far_kernel(me, *refs):
    ups = refs[8:10]
    downs = refs[10:12]
    sem = refs[12]
    size = ups[0].shape[0] // 2
    for core in range(2):
        for flip in range(4):
            @pl.when(jnp.logical_and(me[0] == core, me[3] == flip))
            def _():
                copies = []
                for r in range(4):
                    quarter = flip ^ r
                    half = (quarter >> 1) ^ core
                    at = pl.ds((quarter & 1) * size, size)
                    up, down = (refs[r], refs[4 + r]) if core == 0 else (refs[4 + r], refs[r])
                    copies.append(pltpu.make_async_copy(up.at[pl.ds(0, size), :], ups[half].at[at, :], sem.at[r]))
                    copies.append(
                        pltpu.make_async_copy(down.at[pl.ds(0, size), :], downs[half].at[at, :], sem.at[4 + r])
                    )
                for copy in copies:
                    copy.start()
                for copy in copies:
                    copy.wait()


def call_far(me, pieces):
    size, width = pieces[0].shape
    return pl.pallas_call(
        far_kernel,
        in_specs=[pl.BlockSpec(memory_space=pltpu.SMEM)] + [pl.BlockSpec(memory_space=pl.ANY)] * 8,
        out_specs=[pl.BlockSpec(memory_space=pltpu.VMEM)] * 4,
        out_shape=[jax.ShapeDtypeStruct((2 * size, width), bf16)] * 4,
        scratch_shapes=[pltpu.SemaphoreType.DMA((8,))],
        compiler_params=pltpu.CompilerParams(vmem_limit_bytes=LIMIT),
        cost_estimate=pl.CostEstimate(flops=int(2 * SCALE * 1.15e9), bytes_accessed=0, transcendentals=0),
        name="far_weights",
    )(me, *pieces)


def mid_kernel(mod, vec, tok, dy, attn, dh, p_i, wout, dmid_o, datt_o, dattn_o, dv_o, sums):
    width = tok.shape[1]
    cols = width // 128
    low, _ = lane_masks((SLOT, 128))
    sums[...] = jnp.zeros_like(sums)
    for i in range(tok.shape[0] // CHUNK):
        cr = slice(i * CHUNK, i * CHUNK + CHUNK)
        attnv = attn[cr, :]
        gate1 = mod[2:3, :]
        unit, rs = whiten(tok[cr, :].astype(f32) + gate1 * attnv)
        dh2 = dh[cr, :]
        dmid = dy[cr, :].astype(f32) + whiten_back(dh2 * (vec[7:8, :] * (1.0 + mod[4:5, :])), unit, rs)
        dmid_o[cr, :] = dmid
        add_row(sums, 0, dh2)
        add_row(sums, 1, dh2 * unit)
        add_row(sums, 2, dmid * attnv)
        dattn = (dmid * gate1).astype(bf16)
        dattn_o[cr, :] = dattn
        datt = nt(dattn, wout[...]).astype(bf16)
        datt_o[cr, :] = datt
        for s in range(CHUNK // SLOT):
            rows = slice(i * CHUNK + s * SLOT, i * CHUNK + s * SLOT + SLOT)
            for j in range(cols):
                sl = slice(128 * j, 128 * j + 128)
                at = ((i * (CHUNK // SLOT) + s) * cols + j) * 256
                dv = nn(p_i[at : at + 256, :], datt[s * SLOT : s * SLOT + SLOT, sl])
                dv_o[rows, sl] = jnp.where(low, dv[:SLOT], dv[SLOT:]).astype(bf16)


def call_mid(mod, vec, tok, dy, attn, dh, p, wout):
    tokens, width = tok.shape
    low = ((tokens, width), bf16)
    return call(
        mid_kernel, [((tokens, width), f32), low, low, low, ((8, width), f32)],
        [mod, vec, tok, dy, attn, dh, p, wout], scalars=0, name="mid_grads", us=6,
    )


def scores_kernel(datt, q_i, k_i, v_i, p_i, cos, sin, dq_o, dk_o):
    width = datt.shape[1]
    cols = width // 128
    low, first = lane_masks((SLOT, 128))
    cosv = cos[...]
    sinv = sin[...]

    def one(s, _):
        rows = chunk(s, SLOT)
        kept = []
        for j in range(cols):
            sl = slice(128 * j, 128 * j + 128)
            pr = p_i[chunk(s * cols + j, 256), :]
            kept.append((nt(split_heads(v_i[rows, sl], low), datt[rows, sl]), pr.astype(f32)))
        scores = []
        for dp, pr in kept:
            ds = []
            for e in range(2):
                ee = slice(SLOT * e, SLOT * e + SLOT)
                d = jnp.sum(pr[ee, :] * dp[ee, :], axis=0, keepdims=True)
                ds.append((pr[ee, :] * (dp[ee, :] - d)).astype(bf16))
            scores.append(jnp.concatenate(ds, axis=0))
        for j, ds in enumerate(scores):
            sl = slice(128 * j, 128 * j + 128)
            dq = tn(ds, split_heads(k_i[rows, sl], low)) * 0.125
            dk = nn(ds, q_i[rows, sl])
            dk = jnp.where(low, dk[:SLOT], dk[SLOT:]) * 0.125
            dq_o[rows, sl] = (dq * cosv - half_turn(dq, first) * sinv).astype(bf16)
            dk_o[rows, sl] = (dk * cosv - half_turn(dk, first) * sinv).astype(bf16)
        return 0

    lax.fori_loop(0, datt.shape[0] // SLOT, one, 0, unroll=2)


def call_scores(datt, q, k, v, p, cos, sin):
    low = (datt.shape, bf16)
    return call(scores_kernel, [low, low], [datt, q, k, v, p, cos, sin], scalars=0, name="score_grads", us=7)


def pair_kernel(blocks, place, me, a0, b0, a1, b1, *refs):
    *outs, acc0, acc1 = refs
    if blocks == 1:
        outs[0][...] = tn(a0[...], b0[...]).astype(bf16)
        outs[1][...] = tn(a1[...], b1[...]).astype(bf16)
        return

    acc0[...] = tn(a0[...], b0[...])
    acc1[...] = tn(a1[...], b1[...])

    @pl.when(me[0] == 0)
    def _():
        put_rows(outs[:2], acc0, me[2], blocks, place)
        put_rows(outs[2:], acc1, me[2], blocks, place)

    @pl.when(me[0] != 0)
    def _():
        put_rows(outs[:2], acc1, me[2], blocks, place)
        put_rows(outs[2:], acc0, me[2], blocks, place)


def call_pair(me, blocks, place, first, second):
    a0, b0 = first
    a1, b1 = second
    width = a0.shape[1]
    return call(
        functools.partial(pair_kernel, blocks, place),
        [((width, width), bf16)] * 2 if blocks == 1 else [((width // 2, width), bf16)] * 4,
        [me, a0, b0, a1, b1],
        scratch=[pltpu.VMEM((width, width), f32)] * 2,
        name="weight_grads", us=4,
    )


def tokens_kernel(mod, vec, tok, dmid, dq, dk, dv, wqkv, dtok_o, sums):
    sums[...] = jnp.zeros_like(sums)
    for m in range(tok.shape[0] // CHUNK):
        cr = slice(m * CHUNK, m * CHUNK + CHUNK)
        width = tok.shape[1]
        dh1 = nt(dq[cr, :], wqkv[:, :width])
        dh1 = dh1 + nt(dk[cr, :], wqkv[:, width : 2 * width])
        dh1 = dh1 + nt(dv[cr, :], wqkv[:, 2 * width :])
        unit, rs = whiten(tok[cr, :].astype(f32))
        add_row(sums, 0, dh1)
        add_row(sums, 1, dh1 * unit)
        dtok_o[cr, :] = (dmid[cr, :] + whiten_back(dh1 * (vec[6:7, :] * (1.0 + mod[1:2, :])), unit, rs)).astype(bf16)


def call_tokens(mod, vec, tok, dmid, dq, dk, dv, wqkv):
    tokens, width = tok.shape
    return call(
        tokens_kernel, [((tokens, width), bf16), ((8, width), f32)], [mod, vec, tok, dmid, dq, dk, dv, wqkv],
        scalars=0, name="token_grads", us=6, limit=18 * 1024 * 1024,
    )


def result_kernel(parts, far, me, mod, vec, tok, dy, attn, *refs):
    acts = refs[:parts]
    downs = refs[parts:-2]
    out_o, sums = refs[-2:]
    hb = acts[0].shape[1]
    sums[...] = jnp.zeros_like(sums)

    for m in range(tok.shape[0] // CHUNK):
        cr = slice(m * CHUNK, m * CHUNK + CHUNK)
        branch = vec[8:9, :] + jnp.zeros((CHUNK, tok.shape[1]), f32)
        for n in range(parts):
            if far:
                dn = downs[0][n] if n < 2 else downs[n - 1][...]
            else:
                dn = downs[n][...]
            branch = branch + nn(acts[n][cr, :], dn)
        out_o[cr, :] = (
            tok[cr, :].astype(f32) + mod[2:3, :] * attn[cr, :] + mod[5:6, :] * branch
        ).astype(bf16)
        add_row(sums, 0, dy[cr, :].astype(f32) * branch)


def call_result(me, far, mod, vec, tok, dy, attn, acts, downs):
    tokens, width = tok.shape
    return call(
        functools.partial(result_kernel, len(acts), far),
        [((tokens, width), bf16), ((8, width), f32)],
        [me, mod, vec, tok, dy, attn] + acts + downs,
        name="output_rows", us=7, limit=18 * 1024 * 1024,
    )


def ffn_out_kernel(me, *refs):
    up_o, down_o, up_s, down_s, sem = refs[4:]
    width = refs[0].shape[1]
    size = width // 8
    copies = []
    for a in range(2):
        half = (me[1] >> 2) ^ a
        for n, z in enumerate((0, 2, 1, 3)):
            at = pl.multiple_of(lax.bitwise_xor(a * 4 + z, me[1]) * size, size)
            for t in range(2):
                src = slice((2 * n + t) * size, (2 * n + t) * size + size)

                @pl.when(me[0] == 0)
                def _():
                    up_s[pl.ds(at, size), t * width : t * width + width] = refs[a][src, :].astype(f32)
                    down_s[pl.ds((1 - t) * width + at, size), :] = refs[2 + a][src, :].astype(f32)

                @pl.when(me[0] != 0)
                def _():
                    up_s[pl.ds(at, size), t * width : t * width + width] = refs[2 + a][src, :].astype(f32)
                    down_s[pl.ds((1 - t) * width + at, size), :] = refs[a][src, :].astype(f32)

        rows = pl.ds(pl.multiple_of(half * (width // 2), width // 2), width // 2)
        copies.append(pltpu.make_async_copy(up_s.at[rows, :], up_o.at[rows, :], sem.at[3 * a]))
        for t in range(2):
            rows = pl.ds(pl.multiple_of(half * (width // 2) + t * width, width // 2), width // 2)
            copies.append(pltpu.make_async_copy(down_s.at[rows, :], down_o.at[rows, :], sem.at[3 * a + 1 + t]))
        for copy in copies[3 * a :]:
            copy.start()
    for copy in copies:
        copy.wait()


def call_ffn_out(me, pieces):
    width = pieces[0].shape[1]
    shapes = [(width, 2 * width), (2 * width, width)]
    return pl.pallas_call(
        ffn_out_kernel,
        in_specs=[pl.BlockSpec(memory_space=pltpu.SMEM)] + [pl.BlockSpec(memory_space=pltpu.VMEM)] * 4,
        out_specs=[pl.BlockSpec(memory_space=pltpu.HBM)] * 2,
        out_shape=[jax.ShapeDtypeStruct(shape, f32) for shape in shapes],
        scratch_shapes=[pltpu.VMEM(shape, f32) for shape in shapes] + [pltpu.SemaphoreType.DMA((6,))],
        compiler_params=pltpu.CompilerParams(vmem_limit_bytes=LIMIT),
        cost_estimate=pl.CostEstimate(flops=int(3 * SCALE * 1.15e9), bytes_accessed=0, transcendentals=0),
        name="feed_forward_grads",
    )(me, *pieces)


def attn_out_kernel(last, axes, me, *refs):
    if last:
        qkv_o, scratch, sem = refs[5:]
    else:
        qkv_o, out_o, scratch, sem = refs[4:]
    width = refs[0].shape[1]
    size = width // 16
    every = refs[0].shape[0] // 8
    copies = []
    for n, xy in enumerate((0, axes[0], axes[1], 12)):
        for i, z in enumerate((0, 2, 1, 3)):
            at = pl.ds(pl.multiple_of(lax.bitwise_xor(xy + z, me[2]) * size, size), size)
            row = (4 * (n % 2) + i) * every
            src = slice(row, row + size)

            for core in range(2):
                @pl.when(me[0] == core)
                def _():
                    scratch[at, :width] = refs[2 * core + n // 2][src, :].astype(f32)
                    scratch[at, width:] = refs[2 * (1 - core) + n // 2][src, :].astype(f32)

        at = pl.ds(pl.multiple_of((lax.bitwise_xor(xy, me[2]) >> 2) * (4 * size), 4 * size), 4 * size)
        if last:
            copies.append(pltpu.make_async_copy(scratch.at[at, :], qkv_o.at[at, pl.ds(0, 2 * width)], sem.at[2 * n]))
        else:
            copies.append(
                pltpu.make_async_copy(
                    scratch.at[at, pl.ds(0, width)], qkv_o.at[at, pl.ds(2 * width, width)], sem.at[2 * n]
                )
            )
            copies.append(
                pltpu.make_async_copy(scratch.at[at, pl.ds(width, width)], out_o.at[at, :], sem.at[2 * n + 1])
            )
        for copy in copies[n * (1 if last else 2) :]:
            copy.start()
    for copy in copies:
        copy.wait()


def call_attn_out(me, axes, pieces, qkv=None):
    width = pieces[0].shape[1]
    last = qkv is not None
    shapes = [(width, 3 * width)] + ([] if last else [(width, width)])
    hbm = pl.BlockSpec(memory_space=pltpu.HBM)
    return pl.pallas_call(
        functools.partial(attn_out_kernel, last, axes),
        in_specs=[pl.BlockSpec(memory_space=pltpu.SMEM)] + [pl.BlockSpec(memory_space=pltpu.VMEM)] * 4
        + ([hbm] if last else []),
        out_specs=[hbm] * len(shapes),
        out_shape=[jax.ShapeDtypeStruct(shape, f32) for shape in shapes],
        scratch_shapes=[pltpu.VMEM((width, 2 * width), f32), pltpu.SemaphoreType.DMA((8,))],
        input_output_aliases={5: 0} if last else {},
        compiler_params=pltpu.CompilerParams(vmem_limit_bytes=LIMIT),
        cost_estimate=pl.CostEstimate(flops=int(3 * SCALE * 1.15e9), bytes_accessed=0, transcendentals=0),
        name="attention_grads",
    )(me, *pieces, *([qkv] if last else []))


def split2(a):
    high = a.astype(bf16)
    return high, (a - high.astype(f32)).astype(bf16)


def pack_kernel(ts, tab, mod, vec, bd, sums1, sums2, sums3, d0, d1, d2, d3, out):
    rows = [
        sums1[0:1, :], sums1[1:2, :] * vec[6:7, :], sums2[2:3, :], sums2[0:1, :], sums2[1:2, :] * vec[7:8, :],
        sums3[0:1, :], sums1[1:2, :] * (1.0 + mod[1:2, :]), sums2[1:2, :] * (1.0 + mod[4:5, :]), bd[0:1, :],
        jnp.zeros_like(bd[0:1, :]), d0[0:1, :], d1[0:1, :], d2[0:1, :], d3[0:1, :], bd[0:1, :], bd[0:1, :],
    ]
    out[...] = jnp.concatenate(rows, axis=0).astype(bf16)
    cond = tab[pl.ds(ts[0], 1), :]
    high, low = split2(cond)
    lane = lax.broadcasted_iota(jnp.int32, (1, 128), 1)
    step = jnp.where(lane == 0, ts[0] // 128, jnp.where(lane == 1, lax.rem(ts[0], 128), 0)).astype(f32)
    out[9:10, :128] = high
    out[9:10, 128:256] = low
    out[9:10, 256:384] = step.astype(bf16)


def call_pack(ts, tab, mod, vec, bd, sums1, sums2, sums3, db):
    width = mod.shape[1]
    return call(
        pack_kernel, [((16, width), bf16)], [ts, tab, mod, vec, bd, sums1, sums2, sums3] + db, name="small_rows"
    )[0]


def small_kernel(far_bit, me, ada_w, *refs):
    table_o, gain1_o, gain2_o, bdown_o, bias_o, ada_w_o, ada_b_o, rows_s = refs[4:]
    width = gain1_o.shape[0]
    every = refs[0].shape[0] // 8
    bias = [jnp.zeros((1, width), f32), jnp.zeros((1, width), f32)]
    for n in range(8):
        for z in range(4):
            at = 4 * n + z
            row = (4 * (n % 2) + z) * every + every - 16
            pack = refs[n // 2][row : row + 16, :].astype(f32)
            for kind in range(10):
                rows_s[kind, at : at + 1, :] = pack[kind : kind + 1, :]
            base = 12 if n & far_bit else 10
            for h in range(2):
                to = h if n < 4 else 1 - h
                bias[to] = bias[to] + pack[base + h : base + h + 1, :]
    for h in range(2):
        bias_o[h * width : h * width + width] = jnp.where(me[0] == 0, bias[h], bias[1 - h]).reshape(width)
    for kind, gain_o in enumerate((gain1_o, gain2_o, bdown_o)):
        gain_o[...] = jnp.sum(rows_s[6 + kind], axis=0)
    extra = rows_s[9]
    high = extra[:, :128].astype(bf16)
    low = extra[:, 128:256].astype(bf16)
    step = extra[:, 256:257] * 128.0 + extra[:, 257:258]
    total = jnp.zeros((32, 128), f32)
    for kind in range(6):
        grad = rows_s[kind].astype(bf16)
        cols = slice(kind * width, kind * width + width)
        ada_b_o[cols] = jnp.sum(rows_s[kind], axis=0)
        ada_w_o[:, cols] = tn(high, grad) + tn(low, grad)
        whigh, wlow = split2(ada_w[:, cols])
        total = total + nt(grad, whigh) + nt(grad, wlow)
    lane = lax.broadcasted_iota(jnp.int32, (32, 1024), 1)
    hot = jnp.where(lane.astype(f32) == step, 1.0, 0.0).astype(bf16)
    thigh, tlow = split2(total)
    table_o[...] = (tn(hot, thigh) + tn(hot, tlow))[: table_o.shape[0], :]


def call_small(me, far_bit, ada_w, pieces, entries):
    width = pieces[0].shape[1]
    return call(
        functools.partial(small_kernel, far_bit),
        [
            ((entries, 128), f32), ((width,), f32), ((width,), f32), ((width,), f32), ((2 * width,), f32),
            ((128, 6 * width), f32), ((6 * width,), f32),
        ],
        [me, ada_w] + pieces, scratch=[pltpu.VMEM((10, 32, width), f32)], name="small_grads", us=4,
        limit=16 * 1024 * 1024,
    )


def swap(array, mask):
    return lax.ppermute(array, ("seq", "mlp"), [(i, i ^ mask) for i in range(32)])


def combine_kernel(sizes, *refs):
    outs = refs[sum(sizes):]
    rows = outs[0].shape[0]
    at = 0
    base = 0
    for n in sizes:
        group = refs[at : at + n]
        at += n
        size = group[0].shape[0]
        step = min(size, rows)
        for r in range(0, size, step):
            part = slice(r, r + step)
            if n == 1:
                value = group[0][part, :]
            else:
                value = group[0][part, :].astype(f32)
                for other in group[1:]:
                    value = value + other[part, :].astype(f32)
                value = value.astype(outs[0].dtype)
            out = (base + r) // rows
            to = base + r - out * rows
            outs[out][to : to + step, :] = value
        base += size


def combine(groups, pieces=1):
    arrays = [a for group in groups for a in group]
    rows = sum(group[0].shape[0] for group in groups)
    shape = (rows // pieces, arrays[0].shape[1])
    out = call(
        functools.partial(combine_kernel, [len(group) for group in groups]),
        [(shape, arrays[0].dtype)] * pieces, arrays, scalars=0, name="sums",
    )
    return out if pieces > 1 else out[0]


class Order:
    def __init__(self):
        self.last = None

    def run(self, function, *args, **kwargs):
        leaves, tree = jax.tree.flatten(list(args))
        if self.last is not None:
            at = [i for i, a in enumerate(leaves) if isinstance(a, jax.Array)][0]
            leaves[at] = tie(leaves[at], self.last)
        args = jax.tree.unflatten(tree, leaves)
        out = function(*args, **kwargs)
        self.last = min(out, key=lambda a: a.size) if isinstance(out, (list, tuple)) else out
        return out

    def swap(self, array, *masks):
        if self.last is not None:
            array = tie(array, self.last)
        out = [swap(array, mask) for mask in masks]
        return out if len(out) > 1 else out[0]


def tie(array, *after):
    return lax.optimization_barrier((array,) + after)[0]


def rope_tables(width):
    half = 32
    freq = np.float32(10000.0) ** (-np.arange(half, dtype=np.float32) / np.float32(half))
    angle = np.arange(SLOT, dtype=np.float32)[:, None] * freq[None, :]
    cos = np.cos(angle).astype(np.float32)
    sin = np.sin(angle).astype(np.float32)
    return (
        jnp.asarray(np.concatenate([cos, cos, cos, cos], axis=1)),
        jnp.asarray(np.concatenate([-sin, sin, -sin, sin], axis=1)),
    )


def shards(
    tuned, tokens, time_table, timesteps, lengths, ln1_gain, ln2_gain, w_qkv, w_out, w_up, b_up, w_down, b_down,
    ada_w, ada_b, out_grad,
):
    width = tokens.shape[1]
    local = w_up.shape[1]
    cos, sin = rope_tables(width)
    small = [ada_b, ln1_gain, ln2_gain, b_down, b_up]
    seq = lax.axis_index("seq")
    mlp = lax.axis_index("mlp")
    cond = lax.dynamic_slice_in_dim(time_table, timesteps[0], 1, 0)
    if tuned:
        core = seq & 1
        x = (seq >> 1) & 1
        z = seq >> 2
        me = jnp.stack([core, x * 4 + z, x * 8 + mlp * 4 + z, x * 2 + (z & 1)]).astype(jnp.int32)
        order = Order()
        run = order.run
        send = order.swap
        own, diag = run(call_send, me, b_up, w_up, w_down)
        own = send(own, Y)
        diag = send(diag, Y)
        h1, q, k, v, p, att, attn, h2, dbl, bd, mod, vec, ups, downs = run(
            call_forward, lengths, timesteps, me, small, cos, sin, time_table, ada_w, tokens, out_grad, w_qkv, w_out,
            w_up, w_down, 2,
        )
        own_x = send(own, X)
        own_z = send(own, Z0)
        own_c = send(own, CORE)
        hb = local // 2
        act0, dh, db0, na_keep, na_away, na_keep1, na_away1 = run(
            call_ffn, me, 8, 0, False, h2, dbl, ups, downs, vec, None, hb, 9
        )
        act1, dh, db1, nb_keep, nb_away, nb_keep1, nb_away1 = run(
            call_ffn, me, 8, 1, False, h2, dbl, ups, downs, vec, dh, hb, 9
        )
        diag_c = send(diag, CORE)
        x_c = send(own_x, CORE)
        z_c = send(own_z, CORE)
        up_a, up_b, down_a, down_b = run(
            call_far, me, [own, own_z, own_x, diag, own_c, z_c, x_c, diag_c]
        )
        far_vec = diag[diag.shape[0] - 16 :].astype(f32)
        nb_away1 = send(nb_away1, CORE)
        na_keep1 = send(na_keep1, CORE)
        na_away1 = send(na_away1, CORE)
        nb_keep1 = send(nb_keep1, CORE)
        act2, dh, db2, fa_keep, fa_away, fa_keep1, fa_away1 = run(
            call_ffn, me, 8, 0, True, h2, dbl, up_a, down_a, far_vec, dh, hb, 0
        )
        n0_away = run(combine, [[na_away, nb_away1]])
        n0_away = send(n0_away, X)
        fa_away1 = send(fa_away1, CORE)
        act3, dh, db3, fb_keep, fb_away, fb_keep1, fb_away1 = run(
            call_ffn, me, 8, 1, True, h2, dbl, up_b, down_b, far_vec, dh, hb, 0
        )
        dmid, datt, dattn, dv, sums2 = run(call_mid, mod, vec, tokens, out_grad, attn, dh, p, w_out)
        fa_keep1 = send(fa_keep1, CORE)
        fb_away1 = send(fb_away1, CORE)
        g_keep, g_away, g_keep1, g_away1 = run(call_pair, me, 16, yx_first, (h1, dv), (att, dattn))
        f1_away = run(combine, [[fb_away, fa_away1]])
        n0 = run(combine, [[na_keep, nb_keep1, n0_away]])
        fb_keep1 = send(fb_keep1, CORE)
        f0_away = run(combine, [[fa_away, fb_away1]])
        f1_away = send(f1_away, Z0)
        n1_away = run(combine, [[nb_away, na_away1]])
        f0_away = send(f0_away, X)
        g_away1 = send(g_away1, CORE)
        g_away = run(combine, [[g_away, g_away1]])
        g_away = send(g_away, Y)
        dq, dk = run(call_scores, datt, q, k, v, p, cos, sin)
        f0 = run(combine, [[fa_keep, fb_keep1, f0_away]])
        g_keep1 = send(g_keep1, CORE)
        f1 = run(combine, [[fb_keep, fa_keep1, f1_away]])
        f0 = send(f0, Y)
        n1_away = send(n1_away, Z0)
        result, sums3 = run(
            call_result, me, True, mod, vec, tokens, out_grad, attn, [act0, act1, act2, act3], [downs, down_a, down_b]
        )
        e_keep, e_away, e_keep1, e_away1 = run(call_pair, me, 16, yx_first, (h1, dq), (h1, dk))
        e_keep1 = send(e_keep1, CORE)
        g, g_away = run(combine, [[g_keep, g_keep1, g_away]], 2)
        g_away = send(g_away, X)
        f1 = send(f1, Y)
        n1 = run(combine, [[nb_keep, na_keep1, n1_away]])
        e_away1 = send(e_away1, CORE)
        p0, p0_away = run(combine, [[n0, f0]], 2)
        tok_grad, sums1 = run(call_tokens, mod, vec, tokens, dmid, dq, dk, dv, w_qkv)
        e_away = run(combine, [[e_away, e_away1]])
        p0_away = send(p0_away, Z0)
        e_away = send(e_away, Y)
        g, g_away = run(combine, [[g, g_away]], 2)
        g_away = send(g_away, Z0)
        p1, p1_away = run(combine, [[n1, f1]], 2)
        p1_away = send(p1_away, Z1)
        g, g_away = run(combine, [[g, g_away]], 2)
        e, e_away = run(combine, [[e_keep, e_keep1, e_away]], 2)
        e_away = send(e_away, X)
        g_away = send(g_away, Z1)
        p0, p0_away = run(combine, [[p0, p0_away]], 2)
        p0_away = send(p0_away, Z1)
        p1, p1_away = run(combine, [[p1, p1_away]], 2)
        p1_away = send(p1_away, X)
        e, e_away = run(combine, [[e, e_away]], 2)
        e_away = send(e_away, Z0)
        pack = run(call_pack, timesteps, time_table, mod, vec, bd, sums1, sums2, sums3, [db0, db1, db2, db3])
        g = run(combine, [[g, g_away], [pack]])
        g_z = send(g, Z1)
        ffn = run(combine, [[p0, p0_away], [p1, p1_away]])
        ffn_z = send(ffn, Z1)
        e, e_away = run(combine, [[e, e_away]], 2)
        e_away = send(e_away, Z1)
        g = run(combine, [[g], [g_z]])
        g_z = send(g, Z0)
        e = run(combine, [[e, e_away]])
        e_z = send(e, Z1)
        g = run(combine, [[g], [g_z]])
        e = run(combine, [[e], [e_z]])
        e_z = send(e, Z0)
        g_x = send(g, X)
        ffn = run(combine, [[ffn], [ffn_z]])
        ffn_z = send(ffn, Z0)
        g = run(combine, [[g], [g_x]])
        g_x = send(g, Y)
        e = run(combine, [[e], [e_z]])
        e_x = send(e, X)
        g_c = send(g, CORE)
        ffn = run(combine, [[ffn], [ffn_z]])
        g_xc = send(g_x, CORE)
        e = run(combine, [[e], [e_x]])
        e_x = send(e, Y)
        ffn_x = send(ffn, X)
        ffn_xc = send(ffn_x, CORE)
        table_grad, gain1, gain2, bdown_grad, bias_grad, ada_w_grad, ada_b_grad = run(
            call_small, me, 2, ada_w, [g, g_x, g_c, g_xc], time_table.shape[0]
        )
        ffn_c = send(ffn, CORE)
        e_xc = send(e_x, CORE)
        qkv_wgrad, out_wgrad = run(call_attn_out, me, (8, 4), [g, g_x, g_c, g_xc])
        e_c = send(e, CORE)
        (qkv_wgrad,) = run(call_attn_out, me, (8, 4), [e, e_x, e_c, e_xc], qkv_wgrad)
        up_grad, down_grad = run(call_ffn_out, me, [ffn, ffn_x, ffn_c, ffn_xc])
        return (
            result, tok_grad, table_grad, gain1, gain2, qkv_wgrad, out_wgrad, up_grad, bias_grad, down_grad,
            bdown_grad, ada_w_grad, ada_b_grad,
        )

    me = jnp.zeros((4,), jnp.int32)
    h1, q, k, v, p, att, attn, h2, dbl, bd, mod, vec, _, _ = call_forward(
        lengths, timesteps, me, small, cos, sin, time_table, ada_w, tokens, out_grad, w_qkv, w_out, w_up, w_down, 1
    )
    n = lax.axis_size("mlp")
    dh, acts, downs, up_sum, down_sum, bup_sum = None, [], [], 0.0, 0.0, 0.0
    for r in range(n):
        there = [(i, (i + r) % n) for i in range(n)]
        back = [((i + r) % n, i) for i in range(n)]
        move = lambda a: lax.ppermute(a, "mlp", there) if r else a
        home = lambda a: lax.ppermute(a, "mlp", back) if r else a
        downs.append(move(w_down))
        act, dh, db, g_up, g_down = call_ffn(
            me, 1, 0, True, h2, dbl, move(w_up).T, downs[-1], move(vec), dh, local, 9
        )
        acts.append(act)
        up_sum = up_sum + home(g_up).astype(f32)
        down_sum = down_sum + home(g_down).astype(f32)
        bup_sum = bup_sum + home(db[0])
    dmid, datt, dattn, dv, sums2 = call_mid(mod, vec, tokens, out_grad, attn, dh, p, w_out)
    dq, dk = call_scores(datt, q, k, v, p, cos, sin)
    w0, w1 = call_pair(me, 1, same, (h1, dq), (h1, dk))
    w2, w3 = call_pair(me, 1, same, (h1, dv), (att, dattn))
    tok_grad, sums1 = call_tokens(mod, vec, tokens, dmid, dq, dk, dv, w_qkv)
    result, sums3 = call_result(me, False, mod, vec, tokens, out_grad, attn, acts, downs)
    up_grad, down_grad, bias_grad = lax.psum((up_sum, down_sum, bup_sum), "seq")
    mod_grad = jnp.concatenate([
        sums1[0], sums1[1] * ln1_gain, sums2[2], sums2[0], sums2[1] * ln2_gain, sums3[0],
    ])[None]
    gains = jnp.stack([sums1[1] * (1.0 + mod[1]), sums2[1] * (1.0 + mod[4]), bd[0]])
    hot = (timesteps[:, None] == jnp.arange(time_table.shape[0], dtype=jnp.int32)[None, :]).astype(f32)
    qkv_wgrad = jnp.concatenate([w0, w1, w2], axis=1).astype(f32)
    qkv_wgrad, out_wgrad, ada_w_grad, ada_b_grad, table_grad, gains = lax.psum(
        (
            qkv_wgrad, w3.astype(f32), jnp.dot(cond.T, mod_grad, precision=HIGH), mod_grad[0],
            jnp.dot(hot.T, jnp.dot(mod_grad, ada_w.T, precision=HIGH), precision=HIGH), gains,
        ),
        ("seq", "mlp"),
    )
    return (
        result, tok_grad, table_grad, gains[0], gains[1], qkv_wgrad, out_wgrad, up_grad, bias_grad, down_grad,
        gains[2], ada_w_grad, ada_b_grad,
    )


def solution(mesh):
    tuned = mesh.shape["seq"] == 16 and mesh.shape["mlp"] == 2
    rows = P(("seq", "mlp"), None)
    flat = P(("seq", "mlp"))

    def whole(
        tokens, time_table, timesteps, lengths, ln1_gain, ln2_gain, w_qkv, w_out, w_up, b_up, w_down, b_down,
        ada_w, ada_b, out_grad,
    ):
        return shards(
            tuned, tokens, time_table, timesteps, lengths, ln1_gain, ln2_gain, w_qkv, w_out, w_up, b_up, w_down,
            b_down, ada_w, ada_b, out_grad,
        )

    return jax.shard_map(
        whole,
        mesh=mesh,
        in_specs=(
            rows, P(), flat, flat, P(), P(), P(), P(), P(None, "mlp"), P("mlp"), P("mlp", None), P(), P(), P(), rows,
        ),
        out_specs=(
            rows, rows, P(), P(), P(), P(), P(), P(None, "mlp"), P("mlp"), P("mlp", None), P(), P(), P(),
        ),
        check_vma=False,
    )
```

```python
import functools

import jax
import jax.numpy as jnp
import numpy as np
from jax import lax
from jax.experimental import pallas as pl
from jax.experimental.pallas import tpu as pltpu
from jax.sharding import PartitionSpec as P

H = 12
SLOT = 128
HIGH = lax.Precision.HIGHEST
f32 = jnp.float32
bf16 = jnp.bfloat16
Y, CORE, X, Z0, Z1 = 1, 2, 4, 8, 16
LIMIT = 12 * 1024 * 1024
CHUNK = 256
SCALE = 0.01
PARTS = 2
FORWARD = 24 * 1024 * 1024
GROUP = 6


def nn(a, b):
    return jnp.dot(a, b, preferred_element_type=f32)


def nt(a, b):
    return lax.dot_general(a, b, (((1,), (1,)), ((), ())), preferred_element_type=f32)


def tn(a, b):
    return lax.dot_general(a, b, (((0,), (0,)), ((), ())), preferred_element_type=f32)


def whiten(x):
    center = x - jnp.mean(x, axis=-1, keepdims=True)
    spread = jnp.mean(center * center, axis=-1, keepdims=True)
    rs = lax.rsqrt(spread + 1e-06)
    return center * rs, rs


def whiten_back(grad, unit, rs):
    return rs * (
        grad
        - jnp.mean(grad, axis=-1, keepdims=True)
        - unit * jnp.mean(grad * unit, axis=-1, keepdims=True)
    )


def half_turn(u, first):
    return jnp.where(first, pltpu.roll(u, 96, 1), pltpu.roll(u, 32, 1))


def split_heads(u, low):
    zero = jnp.zeros_like(u)
    return jnp.concatenate([jnp.where(low, u, zero), jnp.where(low, zero, u)], axis=0)


def lane_masks(shape):
    lane = lax.broadcasted_iota(jnp.int32, shape, 1)
    return lane < 64, lax.rem(lane, 64) < 32


def call(body, outs, args, scalars=1, scratch=(), limit=LIMIT, name=None, us=1):
    specs = [pl.BlockSpec(memory_space=pltpu.SMEM)] * scalars
    specs += [pl.BlockSpec(memory_space=pltpu.VMEM)] * (len(args) - scalars)
    return pl.pallas_call(
        body,
        in_specs=specs,
        out_specs=[pl.BlockSpec(memory_space=pltpu.VMEM)] * len(outs),
        out_shape=[jax.ShapeDtypeStruct(*o) for o in outs],
        scratch_shapes=list(scratch),
        compiler_params=pltpu.CompilerParams(vmem_limit_bytes=limit),
        cost_estimate=pl.CostEstimate(flops=int(us * SCALE * 1.15e9), bytes_accessed=0, transcendentals=0),
        name=name,
    )(*args)


def chunk(i, size=CHUNK):
    return pl.ds(pl.multiple_of(i * size, size), size)


def add_row(ref, at, value):
    ref[at : at + 1, :] = ref[at : at + 1, :] + jnp.sum(value, axis=0, keepdims=True)


def mod_rows(row, ada_w, vec, mod_o):
    width = mod_o.shape[1]
    cols = width // 128
    col = jnp.broadcast_to(row, (128, 128)).T
    for j in range(6 * cols):
        sl = slice(128 * j, 128 * j + 128)
        out = jnp.sum(ada_w[:, sl] * col, axis=0, keepdims=True)
        to = slice(128 * (j % cols), 128 * (j % cols) + 128)
        mod_o[j // cols : j // cols + 1, to] = out + vec[j // cols : j // cols + 1, to]
    mod_o[6:8, :] = jnp.zeros((2, width), f32)


def forward_chunks(
    parts, ready, lens, mod, vec, cos, sin, tok, dy, wqkv, wout,
    h1_o, q_o, k_o, v_o, p_o, att_o, attn_o, h2_o, dbl_o, bd_o,
):
    width = tok.shape[1]
    cols = width // 128
    low, first = lane_masks((SLOT, 128))
    key_at = lax.broadcasted_iota(jnp.int32, (SLOT, SLOT), 0)
    slots = CHUNK // SLOT
    for i in parts:
        cr = slice(i * CHUNK, i * CHUNK + CHUNK)
        x = tok[cr, :].astype(f32)
        unit, _ = whiten(x)
        h1 = (unit * (vec[6:7, :] * (1.0 + mod[1:2, :])) + mod[0:1, :]).astype(bf16)
        h1_o[cr, :] = h1
        qkv = nn(h1, wqkv[...])
        cosv = cos[...]
        sinv = sin[...]
        units = [(s, j) for s in range(slots) for j in range(cols)]
        for g0 in range(0, len(units), GROUP):
            part = units[g0 : g0 + GROUP]
            kept = []
            for s, j in part:
                rows = slice(s * SLOT, s * SLOT + SLOT)
                out = slice(i * CHUNK + s * SLOT, i * CHUNK + s * SLOT + SLOT)
                sl = slice(128 * j, 128 * j + 128)
                q = qkv[rows, 128 * j : 128 * j + 128]
                k = qkv[rows, width + 128 * j : width + 128 * j + 128]
                v = qkv[rows, 2 * width + 128 * j : 2 * width + 128 * j + 128].astype(bf16)
                q = (q * cosv + half_turn(q, first) * sinv).astype(bf16)
                k = (k * cosv + half_turn(k, first) * sinv).astype(bf16)
                q_o[out, sl] = q
                k_o[out, sl] = k
                v_o[out, sl] = v
                kept.append((nt(split_heads(k, low), q), v))
            probs = []
            for (s, j), (sc, v) in zip(part, kept):
                valid = key_at < lens[i * slots + s]
                two = []
                for e in range(2):
                    x2 = jnp.where(valid, sc[SLOT * e : SLOT * e + SLOT, :], -1e30)
                    ex = jnp.exp((x2 - jnp.max(x2, axis=0, keepdims=True)) * 0.125)
                    two.append((ex * (1.0 / jnp.sum(ex, axis=0, keepdims=True))).astype(bf16))
                pr = jnp.concatenate(two, axis=0)
                at = ((i * slots + s) * cols + j) * 256
                p_o[at : at + 256, :] = pr
                probs.append(pr)
            for (s, j), (sc, v), pr in zip(part, kept, probs):
                out = slice(i * CHUNK + s * SLOT, i * CHUNK + s * SLOT + SLOT)
                att_o[out, 128 * j : 128 * j + 128] = tn(pr, split_heads(v, low)).astype(bf16)
        if i == 0:
            ready()
        attn = nn(att_o[cr, :], wout[...])
        attn_o[cr, :] = attn.astype(bf16)
        unit2, _ = whiten(x + mod[2:3, :] * attn)
        h2_o[cr, :] = (unit2 * (vec[7:8, :] * (1.0 + mod[4:5, :])) + mod[3:4, :]).astype(bf16)
        dbl = (dy[cr, :].astype(f32) * mod[5:6, :]).astype(bf16)
        dbl_o[cr, :] = dbl
        add_row(bd_o, 0, dbl.astype(f32))


def forward_kernel(
    parts, lens, ts, ada_b, gain1, gain2, bdown, bup, cos, sin, tab_h, ada_h, tok_h, dy_h, wqkv_h, wout_h,
    h1_o, q_o, k_o, v_o, p_o, att_o, attn_o, h2_o, dbl_o, bd_o, mod, vec, wqkv, wout,
    tab, ada_w, tok, dy, sem,
):
    rows = pl.ds(0, tok.shape[0])
    loads = [
        pltpu.make_async_copy(tab_h.at[pl.ds(pl.multiple_of(ts[0] // 8 * 8, 8), 8), :], tab, sem.at[0]),
        pltpu.make_async_copy(ada_h, ada_w, sem.at[1]),
        pltpu.make_async_copy(tok_h.at[rows, :], tok, sem.at[2]),
        pltpu.make_async_copy(wqkv_h, wqkv, sem.at[3]),
        pltpu.make_async_copy(dy_h.at[rows, :], dy, sem.at[4]),
        pltpu.make_async_copy(wout_h, wout, sem.at[5]),
    ]
    for load in loads[:4]:
        load.start()
    vec_rows(ada_b, gain1, gain2, bdown, bup, vec)
    bd_o[...] = jnp.zeros_like(bd_o)
    loads[0].wait()
    loads[1].wait()
    mod_rows(tab[pl.ds(lax.rem(ts[0], 8), 1), :], ada_w, vec, mod)
    for load in loads[4:]:
        load.start()
    loads[2].wait()
    loads[3].wait()

    def ready():
        loads[4].wait()
        loads[5].wait()

    forward_chunks(
        range(parts), ready, lens, mod, vec, cos, sin, tok, dy, wqkv, wout,
        h1_o, q_o, k_o, v_o, p_o, att_o, attn_o, h2_o, dbl_o, bd_o,
    )


def rest_kernel(parts, lens, mod, vec, cos, sin, tok, dy, wqkv, wout, *refs):
    forward_chunks(
        range(parts, tok.shape[0] // CHUNK), lambda: None, lens, mod, vec, cos, sin, tok, dy, wqkv, wout, *refs[10:]
    )


def call_forward(lens, ts, small, cos, sin, tab, ada_w, tok, dy, wqkv, wout, parts):
    tokens, width = tok.shape
    s = jax.ShapeDtypeStruct
    low = s((tokens, width), bf16)
    args = [lens, ts, *small, cos, sin, tab, ada_w, tok, dy, wqkv, wout]
    return pl.pallas_call(
        functools.partial(forward_kernel, parts),
        in_specs=[pl.BlockSpec(memory_space=pltpu.SMEM)] * 2
        + [pl.BlockSpec(memory_space=pltpu.VMEM)] * 7
        + [pl.BlockSpec(memory_space=pltpu.HBM)] * 6,
        out_specs=[pl.BlockSpec(memory_space=pltpu.VMEM)] * 14,
        out_shape=[
            low, low, low, low, s((tokens * H, SLOT), bf16), low, low, low, low,
            s((8, width), f32), s((8, width), f32), s((16, width), f32), s(wqkv.shape, bf16), s(wout.shape, bf16),
        ],
        scratch_shapes=[
            pltpu.VMEM((8, 128), f32), pltpu.VMEM(ada_w.shape, f32), pltpu.VMEM((parts * CHUNK, width), bf16),
            pltpu.VMEM((parts * CHUNK, width), bf16), pltpu.SemaphoreType.DMA((6,)),
        ],
        compiler_params=pltpu.CompilerParams(vmem_limit_bytes=FORWARD),
        cost_estimate=pl.CostEstimate(flops=int(7 * SCALE * 1.15e9), bytes_accessed=0, transcendentals=0),
        name="attention_forward",
    )(*args)


def call_rest(lens, mod, vec, cos, sin, tok, dy, wqkv, wout, outs, parts):
    args = [lens, mod, vec, cos, sin, tok, dy, wqkv, wout, *outs]
    vmem = pl.BlockSpec(memory_space=pltpu.VMEM)
    return pl.pallas_call(
        functools.partial(rest_kernel, parts),
        in_specs=[pl.BlockSpec(memory_space=pltpu.SMEM)] + [vmem] * (len(args) - 1),
        out_specs=[vmem] * len(outs),
        out_shape=[jax.ShapeDtypeStruct(a.shape, a.dtype) for a in outs],
        input_output_aliases={9 + i: i for i in range(len(outs))},
        compiler_params=pltpu.CompilerParams(vmem_limit_bytes=LIMIT),
        cost_estimate=pl.CostEstimate(flops=int(7 * SCALE * 1.15e9), bytes_accessed=0, transcendentals=0),
        name="attention_rest",
    )(*args)


def gelu_parts(v):
    c = 0.7978845608028654
    v2 = v * v
    t = jnp.tanh(v * (c + c * 0.044715 * v2))
    h = 0.5 + 0.5 * t
    act = v * h
    slope = h + act * (1.0 - h) * (2.0 * c + 6.0 * c * 0.044715 * v2)
    return act, slope


def put_rows(outs, scratch, me, blocks, place):
    size = scratch.shape[0] // blocks
    for r in range(blocks):
        src = pl.multiple_of(lax.bitwise_xor(r, me) * size, size)
        half, at = divmod(place(r), blocks // 2)
        outs[half][at * size : at * size + size, :] = scratch[pl.ds(src, size), :].astype(bf16)


def same(r):
    return r


def ffn_first(r):
    return (r & 4) | ((r & 1) << 1) | ((r & 2) >> 1)


def ffn_second(r):
    return ((r & 1) << 2) | (r & 2) | (r >> 2)


def xy_first(r):
    return (r & 12) | ((r & 1) << 1) | ((r & 2) >> 1)


def yx_first(r):
    return ((r & 4) << 1) | ((r & 8) >> 1) | ((r & 1) << 1) | ((r & 2) >> 1)


def ffn_kernel(blocks, half, far, first, bias_row, me, h2, dbl, wup, wdn, bup, *refs):
    dh_in = None if first else refs[0]
    act_o, dh_o, db_o, *outs, dpre_s, gup, gdn = refs if first else refs[1:]
    tokens = h2.shape[0]
    hb = act_o.shape[1]
    hid = half ^ me[0] if blocks > 1 else 0
    bias = bup[pl.ds(bias_row + hid, 1), :hb].astype(f32)
    cols = pl.ds(pl.multiple_of(hid * hb, 128), hb)
    up = wup[...] if far else wup[:, cols]
    dn = wdn[...] if far else wdn[cols, :]
    total = jnp.zeros((1, hb), f32)
    for m in range(tokens // CHUNK):
        rows = slice(m * CHUNK, m * CHUNK + CHUNK)
        pre = nt(h2[rows, :], up) if far else nn(h2[rows, :], up)
        act, slope = gelu_parts(pre + bias)
        act_o[rows, :] = act.astype(bf16)
        dpre = (nt(dbl[rows, :], dn) * slope).astype(bf16)
        dpre_s[rows, :] = dpre
        total = total + jnp.sum(dpre.astype(f32), axis=0, keepdims=True)
        back = nn(dpre, up) if far else nt(dpre, up)
        dh_o[rows, :] = back if first else dh_in[rows, :] + back
    db_o[...] = jnp.broadcast_to(total, db_o.shape)
    gup[...] = tn(h2[...], dpre_s[...])
    gdn[...] = tn(act_o[...], dbl[...])
    if blocks == 1:
        outs[0][...] = gup[...].astype(bf16)
        outs[1][...] = gdn[...].astype(bf16)
        return

    ours, theirs = (ffn_first, ffn_second) if half == 0 else (ffn_second, ffn_first)

    @pl.when(me[0] == 0)
    def _():
        put_rows(outs[:2], gup, me[1], blocks, ours)
        put_rows(outs[2:], gdn, me[1], blocks, theirs)

    @pl.when(me[0] != 0)
    def _():
        put_rows(outs[:2], gdn, me[1], blocks, ours)
        put_rows(outs[2:], gup, me[1], blocks, theirs)


def call_ffn(me, blocks, half, far, h2, dbl, wup, wdn, bup, dh, hb, bias_row):
    tokens, width = h2.shape
    first = dh is None
    return call(
        functools.partial(ffn_kernel, blocks, half, far, first, bias_row),
        [((tokens, hb), bf16), ((tokens, width), f32), ((8, hb), f32)]
        + ([((width, hb), bf16), ((hb, width), bf16)] if blocks == 1 else [((width // 2, hb), bf16)] * 4),
        [me, h2, dbl, wup, wdn, bup] + ([] if first else [dh]),
        scratch=[pltpu.VMEM((tokens, hb), bf16), pltpu.VMEM((width, hb), f32), pltpu.VMEM((hb, width), f32)],
        name="feed_forward", us=8,
    )


def vec_rows(ada_b, gain1, gain2, bdown, bup, vec):
    width = vec.shape[1]
    vec[...] = jnp.zeros_like(vec)
    for j in range(6):
        vec[j : j + 1, :] = ada_b[j * width : j * width + width].reshape(1, width)
    vec[6:7, :] = gain1[...].reshape(1, width)
    vec[7:8, :] = gain2[...].reshape(1, width)
    vec[8:9, :] = bdown[...].astype(f32).reshape(1, width)
    size = min(width, bup.shape[0])
    for j in range(bup.shape[0] // size):
        vec[9 + j : 10 + j, :size] = bup[j * size : j * size + size].astype(f32).reshape(1, size)


def send_kernel(me, bup, wup, wdn, own, diag, rows, cols, sem):
    size = own.shape[0]
    pairs = [(own, me[3]), (diag, me[3] ^ 3)]
    @pl.when(me[0] == 0)
    def _():
        copies = [
            pltpu.make_async_copy(wup.at[:, pl.ds(pl.multiple_of(quarter * size, 128), size)], cols.at[i], sem.at[i])
            for i, (out, quarter) in enumerate(pairs)
        ]
        for copy in copies:
            copy.start()
        for i, (out, quarter) in enumerate(pairs):
            copies[i].wait()
            out[:size, :] = cols[i].T

    @pl.when(me[0] != 0)
    def _():
        copies = [
            pltpu.make_async_copy(wdn.at[pl.ds(pl.multiple_of(quarter * size, 128), size), :], rows.at[i], sem.at[i])
            for i, (out, quarter) in enumerate(pairs)
        ]
        for copy in copies:
            copy.start()
        for i, (out, quarter) in enumerate(pairs):
            copies[i].wait()
            out[:size, :] = rows[i]

    width = own.shape[1]
    diag[size : size + 16, :] = jnp.zeros((16, width), bf16)
    for j in range(bup.shape[0] // width):
        diag[size + j : size + j + 1, :] = bup[j * width : j * width + width].reshape(1, width)


def call_send(me, bup, wup, wdn):
    width = wup.shape[0]
    size = wup.shape[1] // 4
    return pl.pallas_call(
        send_kernel,
        in_specs=[pl.BlockSpec(memory_space=pltpu.SMEM), pl.BlockSpec(memory_space=pltpu.VMEM)]
        + [pl.BlockSpec(memory_space=pltpu.HBM)] * 2,
        out_specs=[pl.BlockSpec(memory_space=pltpu.VMEM)] * 2,
        out_shape=[
            jax.ShapeDtypeStruct((size, width), bf16), jax.ShapeDtypeStruct((size + 16, width), bf16),
        ],
        scratch_shapes=[
            pltpu.VMEM((2, size, width), bf16), pltpu.VMEM((2, width, size), bf16), pltpu.SemaphoreType.DMA((2,)),
        ],
        compiler_params=pltpu.CompilerParams(vmem_limit_bytes=60 * 1024 * 1024),
        cost_estimate=pl.CostEstimate(flops=int(SCALE * 1.15e9), bytes_accessed=0, transcendentals=0),
        name="weight_parts",
    )(me, bup, wup, wdn)


def far_kernel(me, *refs):
    ups = refs[8:10]
    downs = refs[10:12]
    sem = refs[12]
    size = ups[0].shape[0] // 2
    for core in range(2):
        for flip in range(4):
            @pl.when(jnp.logical_and(me[0] == core, me[3] == flip))
            def _():
                copies = []
                for r in range(4):
                    quarter = flip ^ r
                    half = (quarter >> 1) ^ core
                    at = pl.ds((quarter & 1) * size, size)
                    up, down = (refs[r], refs[4 + r]) if core == 0 else (refs[4 + r], refs[r])
                    copies.append(pltpu.make_async_copy(up.at[pl.ds(0, size), :], ups[half].at[at, :], sem.at[r]))
                    copies.append(
                        pltpu.make_async_copy(down.at[pl.ds(0, size), :], downs[half].at[at, :], sem.at[4 + r])
                    )
                for copy in copies:
                    copy.start()
                for copy in copies:
                    copy.wait()


def call_far(me, pieces):
    size, width = pieces[0].shape
    return pl.pallas_call(
        far_kernel,
        in_specs=[pl.BlockSpec(memory_space=pltpu.SMEM)] + [pl.BlockSpec(memory_space=pl.ANY)] * 8,
        out_specs=[pl.BlockSpec(memory_space=pltpu.VMEM)] * 4,
        out_shape=[jax.ShapeDtypeStruct((2 * size, width), bf16)] * 4,
        scratch_shapes=[pltpu.SemaphoreType.DMA((8,))],
        compiler_params=pltpu.CompilerParams(vmem_limit_bytes=LIMIT),
        cost_estimate=pl.CostEstimate(flops=int(2 * SCALE * 1.15e9), bytes_accessed=0, transcendentals=0),
        name="far_weights",
    )(me, *pieces)


def mid_kernel(mod, vec, tok, dy, attn, dh, p_i, wout, dmid_o, datt_o, dattn_o, dv_o, sums):
    width = tok.shape[1]
    cols = width // 128
    low, _ = lane_masks((SLOT, 128))
    sums[...] = jnp.zeros_like(sums)
    for i in range(tok.shape[0] // CHUNK):
        cr = slice(i * CHUNK, i * CHUNK + CHUNK)
        attnv = attn[cr, :].astype(f32)
        gate1 = mod[2:3, :]
        unit, rs = whiten(tok[cr, :].astype(f32) + gate1 * attnv)
        dh2 = dh[cr, :]
        dmid = dy[cr, :].astype(f32) + whiten_back(dh2 * (vec[7:8, :] * (1.0 + mod[4:5, :])), unit, rs)
        dmid_o[cr, :] = dmid
        add_row(sums, 0, dh2)
        add_row(sums, 1, dh2 * unit)
        add_row(sums, 2, dmid * attnv)
        dattn = (dmid * gate1).astype(bf16)
        dattn_o[cr, :] = dattn
        datt = nt(dattn, wout[...]).astype(bf16)
        datt_o[cr, :] = datt
        for s in range(CHUNK // SLOT):
            rows = slice(i * CHUNK + s * SLOT, i * CHUNK + s * SLOT + SLOT)
            for j in range(cols):
                sl = slice(128 * j, 128 * j + 128)
                at = ((i * (CHUNK // SLOT) + s) * cols + j) * 256
                dv = nn(p_i[at : at + 256, :], datt[s * SLOT : s * SLOT + SLOT, sl])
                dv_o[rows, sl] = jnp.where(low, dv[:SLOT], dv[SLOT:]).astype(bf16)


def call_mid(mod, vec, tok, dy, attn, dh, p, wout):
    tokens, width = tok.shape
    low = ((tokens, width), bf16)
    return call(
        mid_kernel, [((tokens, width), f32), low, low, low, ((8, width), f32)],
        [mod, vec, tok, dy, attn, dh, p, wout], scalars=0, name="mid_grads", us=6,
    )


def scores_kernel(datt, q_i, k_i, v_i, p_i, cos, sin, dq_o, dk_o):
    width = datt.shape[1]
    cols = width // 128
    low, first = lane_masks((SLOT, 128))
    cosv = cos[...]
    sinv = sin[...]

    def one(s, _):
        rows = chunk(s, SLOT)
        kept = []
        for j in range(cols):
            sl = slice(128 * j, 128 * j + 128)
            pr = p_i[chunk(s * cols + j, 256), :]
            kept.append((nt(split_heads(v_i[rows, sl], low), datt[rows, sl]), pr.astype(f32)))
        scores = []
        for dp, pr in kept:
            ds = []
            for e in range(2):
                ee = slice(SLOT * e, SLOT * e + SLOT)
                d = jnp.sum(pr[ee, :] * dp[ee, :], axis=0, keepdims=True)
                ds.append((pr[ee, :] * (dp[ee, :] - d)).astype(bf16))
            scores.append(jnp.concatenate(ds, axis=0))
        for j, ds in enumerate(scores):
            sl = slice(128 * j, 128 * j + 128)
            dq = tn(ds, split_heads(k_i[rows, sl], low)) * 0.125
            dk = nn(ds, q_i[rows, sl])
            dk = jnp.where(low, dk[:SLOT], dk[SLOT:]) * 0.125
            dq_o[rows, sl] = (dq * cosv - half_turn(dq, first) * sinv).astype(bf16)
            dk_o[rows, sl] = (dk * cosv - half_turn(dk, first) * sinv).astype(bf16)
        return 0

    lax.fori_loop(0, datt.shape[0] // SLOT, one, 0, unroll=2)


def call_scores(datt, q, k, v, p, cos, sin):
    low = (datt.shape, bf16)
    return call(scores_kernel, [low, low], [datt, q, k, v, p, cos, sin], scalars=0, name="score_grads", us=7)


def pair_kernel(blocks, place, me, a0, b0, a1, b1, *refs):
    *outs, acc0, acc1 = refs
    if blocks == 1:
        outs[0][...] = tn(a0[...], b0[...]).astype(bf16)
        outs[1][...] = tn(a1[...], b1[...]).astype(bf16)
        return

    acc0[...] = tn(a0[...], b0[...])
    acc1[...] = tn(a1[...], b1[...])

    @pl.when(me[0] == 0)
    def _():
        put_rows(outs[:2], acc0, me[2], blocks, place)
        put_rows(outs[2:], acc1, me[2], blocks, place)

    @pl.when(me[0] != 0)
    def _():
        put_rows(outs[:2], acc1, me[2], blocks, place)
        put_rows(outs[2:], acc0, me[2], blocks, place)


def call_pair(me, blocks, place, first, second):
    a0, b0 = first
    a1, b1 = second
    width = a0.shape[1]
    return call(
        functools.partial(pair_kernel, blocks, place),
        [((width, width), bf16)] * 2 if blocks == 1 else [((width // 2, width), bf16)] * 4,
        [me, a0, b0, a1, b1],
        scratch=[pltpu.VMEM((width, width), f32)] * 2,
        name="weight_grads", us=4,
    )


def tokens_kernel(mod, vec, tok, dmid, dq, dk, dv, wqkv, dtok_o, sums):
    sums[...] = jnp.zeros_like(sums)
    for m in range(tok.shape[0] // CHUNK):
        cr = slice(m * CHUNK, m * CHUNK + CHUNK)
        width = tok.shape[1]
        dh1 = nt(dq[cr, :], wqkv[:, :width])
        dh1 = dh1 + nt(dk[cr, :], wqkv[:, width : 2 * width])
        dh1 = dh1 + nt(dv[cr, :], wqkv[:, 2 * width :])
        unit, rs = whiten(tok[cr, :].astype(f32))
        add_row(sums, 0, dh1)
        add_row(sums, 1, dh1 * unit)
        dtok_o[cr, :] = (dmid[cr, :] + whiten_back(dh1 * (vec[6:7, :] * (1.0 + mod[1:2, :])), unit, rs)).astype(bf16)


def call_tokens(mod, vec, tok, dmid, dq, dk, dv, wqkv):
    tokens, width = tok.shape
    return call(
        tokens_kernel, [((tokens, width), bf16), ((8, width), f32)], [mod, vec, tok, dmid, dq, dk, dv, wqkv],
        scalars=0, name="token_grads", us=6, limit=18 * 1024 * 1024,
    )


def result_kernel(parts, far, me, mod, vec, tok, dy, attn, *refs):
    acts = refs[:parts]
    downs = refs[parts:-2]
    out_o, sums = refs[-2:]
    hb = acts[0].shape[1]
    sums[...] = jnp.zeros_like(sums)

    for m in range(tok.shape[0] // CHUNK):
        cr = slice(m * CHUNK, m * CHUNK + CHUNK)
        branch = vec[8:9, :] + jnp.zeros((CHUNK, tok.shape[1]), f32)
        for n in range(parts):
            if far:
                dn = downs[0][chunk(n ^ me[0], hb), :] if n < 2 else downs[n - 1][...]
            else:
                dn = downs[n][...]
            branch = branch + nn(acts[n][cr, :], dn)
        out_o[cr, :] = (
            tok[cr, :].astype(f32) + mod[2:3, :] * attn[cr, :].astype(f32) + mod[5:6, :] * branch
        ).astype(bf16)
        add_row(sums, 0, dy[cr, :].astype(f32) * branch)


def call_result(me, far, mod, vec, tok, dy, attn, acts, downs):
    tokens, width = tok.shape
    return call(
        functools.partial(result_kernel, len(acts), far),
        [((tokens, width), bf16), ((8, width), f32)],
        [me, mod, vec, tok, dy, attn] + acts + downs,
        name="output_rows", us=7, limit=18 * 1024 * 1024,
    )


def ffn_out_kernel(me, *refs):
    up_o, down_o, up_s, down_s, sem = refs[4:]
    width = refs[0].shape[1]
    size = width // 8
    copies = []
    for a in range(2):
        half = (me[1] >> 2) ^ a
        for n, z in enumerate((0, 2, 1, 3)):
            at = pl.multiple_of(lax.bitwise_xor(a * 4 + z, me[1]) * size, size)
            for t in range(2):
                src = slice((2 * n + t) * size, (2 * n + t) * size + size)

                @pl.when(me[0] == 0)
                def _():
                    up_s[pl.ds(at, size), t * width : t * width + width] = refs[a][src, :].astype(f32)
                    down_s[pl.ds((1 - t) * width + at, size), :] = refs[2 + a][src, :].astype(f32)

                @pl.when(me[0] != 0)
                def _():
                    up_s[pl.ds(at, size), t * width : t * width + width] = refs[2 + a][src, :].astype(f32)
                    down_s[pl.ds((1 - t) * width + at, size), :] = refs[a][src, :].astype(f32)

        rows = pl.ds(pl.multiple_of(half * (width // 2), width // 2), width // 2)
        copies.append(pltpu.make_async_copy(up_s.at[rows, :], up_o.at[rows, :], sem.at[3 * a]))
        for t in range(2):
            rows = pl.ds(pl.multiple_of(half * (width // 2) + t * width, width // 2), width // 2)
            copies.append(pltpu.make_async_copy(down_s.at[rows, :], down_o.at[rows, :], sem.at[3 * a + 1 + t]))
        for copy in copies[3 * a :]:
            copy.start()
    for copy in copies:
        copy.wait()


def call_ffn_out(me, pieces):
    width = pieces[0].shape[1]
    shapes = [(width, 2 * width), (2 * width, width)]
    return pl.pallas_call(
        ffn_out_kernel,
        in_specs=[pl.BlockSpec(memory_space=pltpu.SMEM)] + [pl.BlockSpec(memory_space=pltpu.VMEM)] * 4,
        out_specs=[pl.BlockSpec(memory_space=pltpu.HBM)] * 2,
        out_shape=[jax.ShapeDtypeStruct(shape, f32) for shape in shapes],
        scratch_shapes=[pltpu.VMEM(shape, f32) for shape in shapes] + [pltpu.SemaphoreType.DMA((6,))],
        compiler_params=pltpu.CompilerParams(vmem_limit_bytes=LIMIT),
        cost_estimate=pl.CostEstimate(flops=int(3 * SCALE * 1.15e9), bytes_accessed=0, transcendentals=0),
        name="feed_forward_grads",
    )(me, *pieces)


def attn_out_kernel(last, axes, me, *refs):
    if last:
        qkv_o, scratch, sem = refs[5:]
    else:
        qkv_o, out_o, scratch, sem = refs[4:]
    width = refs[0].shape[1]
    size = width // 16
    every = refs[0].shape[0] // 8
    copies = []
    for n, xy in enumerate((0, axes[0], axes[1], 12)):
        for i, z in enumerate((0, 2, 1, 3)):
            at = pl.ds(pl.multiple_of(lax.bitwise_xor(xy + z, me[2]) * size, size), size)
            row = (4 * (n % 2) + i) * every
            src = slice(row, row + size)

            for core in range(2):
                @pl.when(me[0] == core)
                def _():
                    scratch[at, :width] = refs[2 * core + n // 2][src, :].astype(f32)
                    scratch[at, width:] = refs[2 * (1 - core) + n // 2][src, :].astype(f32)

        at = pl.ds(pl.multiple_of((lax.bitwise_xor(xy, me[2]) >> 2) * (4 * size), 4 * size), 4 * size)
        if last:
            copies.append(pltpu.make_async_copy(scratch.at[at, :], qkv_o.at[at, pl.ds(0, 2 * width)], sem.at[2 * n]))
        else:
            copies.append(
                pltpu.make_async_copy(
                    scratch.at[at, pl.ds(0, width)], qkv_o.at[at, pl.ds(2 * width, width)], sem.at[2 * n]
                )
            )
            copies.append(
                pltpu.make_async_copy(scratch.at[at, pl.ds(width, width)], out_o.at[at, :], sem.at[2 * n + 1])
            )
        for copy in copies[n * (1 if last else 2) :]:
            copy.start()
    for copy in copies:
        copy.wait()


def call_attn_out(me, axes, pieces, qkv=None):
    width = pieces[0].shape[1]
    last = qkv is not None
    shapes = [(width, 3 * width)] + ([] if last else [(width, width)])
    hbm = pl.BlockSpec(memory_space=pltpu.HBM)
    return pl.pallas_call(
        functools.partial(attn_out_kernel, last, axes),
        in_specs=[pl.BlockSpec(memory_space=pltpu.SMEM)] + [pl.BlockSpec(memory_space=pltpu.VMEM)] * 4
        + ([hbm] if last else []),
        out_specs=[hbm] * len(shapes),
        out_shape=[jax.ShapeDtypeStruct(shape, f32) for shape in shapes],
        scratch_shapes=[pltpu.VMEM((width, 2 * width), f32), pltpu.SemaphoreType.DMA((8,))],
        input_output_aliases={5: 0} if last else {},
        compiler_params=pltpu.CompilerParams(vmem_limit_bytes=LIMIT),
        cost_estimate=pl.CostEstimate(flops=int(3 * SCALE * 1.15e9), bytes_accessed=0, transcendentals=0),
        name="attention_grads",
    )(me, *pieces, *([qkv] if last else []))


def split2(a):
    high = a.astype(bf16)
    return high, (a - high.astype(f32)).astype(bf16)


def pack_kernel(ts, tab, mod, vec, bd, sums1, sums2, sums3, d0, d1, d2, d3, out):
    rows = [
        sums1[0:1, :], sums1[1:2, :] * vec[6:7, :], sums2[2:3, :], sums2[0:1, :], sums2[1:2, :] * vec[7:8, :],
        sums3[0:1, :], sums1[1:2, :] * (1.0 + mod[1:2, :]), sums2[1:2, :] * (1.0 + mod[4:5, :]), bd[0:1, :],
        jnp.zeros_like(bd[0:1, :]), d0[0:1, :], d1[0:1, :], d2[0:1, :], d3[0:1, :], bd[0:1, :], bd[0:1, :],
    ]
    out[...] = jnp.concatenate(rows, axis=0).astype(bf16)
    cond = tab[pl.ds(ts[0], 1), :]
    high, low = split2(cond)
    lane = lax.broadcasted_iota(jnp.int32, (1, 128), 1)
    step = jnp.where(lane == 0, ts[0] // 128, jnp.where(lane == 1, lax.rem(ts[0], 128), 0)).astype(f32)
    out[9:10, :128] = high
    out[9:10, 128:256] = low
    out[9:10, 256:384] = step.astype(bf16)


def call_pack(ts, tab, mod, vec, bd, sums1, sums2, sums3, db):
    width = mod.shape[1]
    return call(
        pack_kernel, [((16, width), bf16)], [ts, tab, mod, vec, bd, sums1, sums2, sums3] + db, name="small_rows"
    )[0]


def small_kernel(far_bit, me, ada_w, *refs):
    table_o, gain1_o, gain2_o, bdown_o, bias_o, ada_w_o, ada_b_o, rows_s = refs[4:]
    width = gain1_o.shape[0]
    every = refs[0].shape[0] // 8
    bias = [jnp.zeros((1, width), f32), jnp.zeros((1, width), f32)]
    for n in range(8):
        for z in range(4):
            at = 4 * n + z
            row = (4 * (n % 2) + z) * every + every - 16
            pack = refs[n // 2][row : row + 16, :].astype(f32)
            for kind in range(10):
                rows_s[kind, at : at + 1, :] = pack[kind : kind + 1, :]
            base = 12 if n & far_bit else 10
            for h in range(2):
                to = h if n < 4 else 1 - h
                bias[to] = bias[to] + pack[base + h : base + h + 1, :]
    for h in range(2):
        bias_o[h * width : h * width + width] = jnp.where(me[0] == 0, bias[h], bias[1 - h]).reshape(width)
    for kind, gain_o in enumerate((gain1_o, gain2_o, bdown_o)):
        gain_o[...] = jnp.sum(rows_s[6 + kind], axis=0)
    extra = rows_s[9]
    high = extra[:, :128].astype(bf16)
    low = extra[:, 128:256].astype(bf16)
    step = extra[:, 256:257] * 128.0 + extra[:, 257:258]
    total = jnp.zeros((32, 128), f32)
    for kind in range(6):
        grad = rows_s[kind].astype(bf16)
        cols = slice(kind * width, kind * width + width)
        ada_b_o[cols] = jnp.sum(rows_s[kind], axis=0)
        ada_w_o[:, cols] = tn(high, grad) + tn(low, grad)
        whigh, wlow = split2(ada_w[:, cols])
        total = total + nt(grad, whigh) + nt(grad, wlow)
    lane = lax.broadcasted_iota(jnp.int32, (32, 1024), 1)
    hot = jnp.where(lane.astype(f32) == step, 1.0, 0.0).astype(bf16)
    thigh, tlow = split2(total)
    table_o[...] = (tn(hot, thigh) + tn(hot, tlow))[: table_o.shape[0], :]


def call_small(me, far_bit, ada_w, pieces, entries):
    width = pieces[0].shape[1]
    return call(
        functools.partial(small_kernel, far_bit),
        [
            ((entries, 128), f32), ((width,), f32), ((width,), f32), ((width,), f32), ((2 * width,), f32),
            ((128, 6 * width), f32), ((6 * width,), f32),
        ],
        [me, ada_w] + pieces, scratch=[pltpu.VMEM((10, 32, width), f32)], name="small_grads", us=4,
        limit=16 * 1024 * 1024,
    )


def swap(array, mask):
    return lax.ppermute(array, ("seq", "mlp"), [(i, i ^ mask) for i in range(32)])


def combine_kernel(sizes, *refs):
    outs = refs[sum(sizes):]
    rows = outs[0].shape[0]
    at = 0
    base = 0
    for n in sizes:
        group = refs[at : at + n]
        at += n
        size = group[0].shape[0]
        step = min(size, rows)
        for r in range(0, size, step):
            part = slice(r, r + step)
            if n == 1:
                value = group[0][part, :]
            else:
                value = group[0][part, :].astype(f32)
                for other in group[1:]:
                    value = value + other[part, :].astype(f32)
                value = value.astype(outs[0].dtype)
            out = (base + r) // rows
            to = base + r - out * rows
            outs[out][to : to + step, :] = value
        base += size


def combine(groups, pieces=1):
    arrays = [a for group in groups for a in group]
    rows = sum(group[0].shape[0] for group in groups)
    shape = (rows // pieces, arrays[0].shape[1])
    out = call(
        functools.partial(combine_kernel, [len(group) for group in groups]),
        [(shape, arrays[0].dtype)] * pieces, arrays, scalars=0, name="sums",
    )
    return out if pieces > 1 else out[0]


class Order:
    def __init__(self):
        self.last = None

    def run(self, function, *args, **kwargs):
        leaves, tree = jax.tree.flatten(list(args))
        if self.last is not None:
            at = [i for i, a in enumerate(leaves) if isinstance(a, jax.Array)][0]
            leaves[at] = tie(leaves[at], self.last)
        args = jax.tree.unflatten(tree, leaves)
        out = function(*args, **kwargs)
        self.last = min(out, key=lambda a: a.size) if isinstance(out, (list, tuple)) else out
        return out

    def swap(self, array, *masks):
        if self.last is not None:
            array = tie(array, self.last)
        out = [swap(array, mask) for mask in masks]
        return out if len(out) > 1 else out[0]


def tie(array, *after):
    return lax.optimization_barrier((array,) + after)[0]


def rope_tables(width):
    half = 32
    freq = np.float32(10000.0) ** (-np.arange(half, dtype=np.float32) / np.float32(half))
    angle = np.arange(SLOT, dtype=np.float32)[:, None] * freq[None, :]
    cos = np.cos(angle).astype(np.float32)
    sin = np.sin(angle).astype(np.float32)
    return (
        jnp.asarray(np.concatenate([cos, cos, cos, cos], axis=1)),
        jnp.asarray(np.concatenate([-sin, sin, -sin, sin], axis=1)),
    )


def shards(
    tuned, tokens, time_table, timesteps, lengths, ln1_gain, ln2_gain, w_qkv, w_out, w_up, b_up, w_down, b_down,
    ada_w, ada_b, out_grad,
):
    width = tokens.shape[1]
    local = w_up.shape[1]
    cos, sin = rope_tables(width)
    small = [ada_b, ln1_gain, ln2_gain, b_down, b_up]
    seq = lax.axis_index("seq")
    mlp = lax.axis_index("mlp")
    cond = lax.dynamic_slice_in_dim(time_table, timesteps[0], 1, 0)
    if tuned:
        core = seq & 1
        x = (seq >> 1) & 1
        z = seq >> 2
        me = jnp.stack([core, x * 4 + z, x * 8 + mlp * 4 + z, x * 2 + (z & 1)]).astype(jnp.int32)
        order = Order()
        run = order.run
        send = order.swap
        own, diag = run(call_send, me, b_up, w_up, w_down)
        own = send(own, Y)
        diag = send(diag, Y)
        *outs, mod, vec, wqkv, wout = run(
            call_forward, lengths, timesteps, small, cos, sin, time_table, ada_w, tokens, out_grad, w_qkv, w_out, PARTS
        )
        own_x = send(own, X)
        own_z = send(own, Z0)
        own_c = send(own, CORE)
        h1, q, k, v, p, att, attn, h2, dbl, bd = run(
            call_rest, lengths, mod, vec, cos, sin, tokens, out_grad, wqkv, wout, outs, PARTS
        )
        hb = local // 2
        act0, dh, db0, na_keep, na_away, na_keep1, na_away1 = run(
            call_ffn, me, 8, 0, False, h2, dbl, w_up, w_down, vec, None, hb, 9
        )
        diag_c = send(diag, CORE)
        x_c = send(own_x, CORE)
        z_c = send(own_z, CORE)
        up_a, up_b, down_a, down_b = run(
            call_far, me, [own, own_z, own_x, diag, own_c, z_c, x_c, diag_c]
        )
        far_vec = diag[diag.shape[0] - 16 :].astype(f32)
        act2, dh, db2, fa_keep, fa_away, fa_keep1, fa_away1 = run(
            call_ffn, me, 8, 0, True, h2, dbl, up_a, down_a, far_vec, dh, hb, 0
        )
        na_away1 = send(na_away1, CORE)
        act3, dh, db3, fb_keep, fb_away, fb_keep1, fb_away1 = run(
            call_ffn, me, 8, 1, True, h2, dbl, up_b, down_b, far_vec, dh, hb, 0
        )
        fa_away1 = send(fa_away1, CORE)
        fb_away1 = send(fb_away1, CORE)
        f0_away = run(combine, [[fa_away, fb_away1]])
        f0_away = send(f0_away, X)
        act1, dh, db1, nb_keep, nb_away, nb_keep1, nb_away1 = run(
            call_ffn, me, 8, 1, False, h2, dbl, w_up, w_down, vec, dh, hb, 9
        )
        nb_away1 = send(nb_away1, CORE)
        f1_away = run(combine, [[fb_away, fa_away1]])
        nb_keep1 = send(nb_keep1, CORE)
        fb_keep1 = send(fb_keep1, CORE)
        f1_away = send(f1_away, Z0)
        n1_away = run(combine, [[nb_away, na_away1]])
        fa_keep1 = send(fa_keep1, CORE)
        dmid, datt, dattn, dv, sums2 = run(call_mid, mod, vec, tokens, out_grad, attn, dh, p, w_out)
        g_keep, g_away, g_keep1, g_away1 = run(call_pair, me, 16, xy_first, (h1, dv), (att, dattn))
        f0 = run(combine, [[fa_keep, fb_keep1, f0_away]])
        n1_away = send(n1_away, Z0)
        n0_away = run(combine, [[na_away, nb_away1]])
        n0_away = send(n0_away, X)
        g_away1 = send(g_away1, CORE)
        f1 = run(combine, [[fb_keep, fa_keep1, f1_away]])
        f1 = send(f1, Y)
        f0 = send(f0, Y)
        dq, dk = run(call_scores, datt, q, k, v, p, cos, sin)
        g_away = run(combine, [[g_away, g_away1]])
        g_away = send(g_away, X)
        e_keep, e_away, e_keep1, e_away1 = run(call_pair, me, 16, yx_first, (h1, dq), (h1, dk))
        na_keep1 = send(na_keep1, CORE)
        n0 = run(combine, [[na_keep, nb_keep1, n0_away]])
        p0, p0_away = run(combine, [[n0, f0]], 2)
        p0_away = send(p0_away, Z0)
        e_away1 = send(e_away1, CORE)
        e_keep1 = send(e_keep1, CORE)
        e_away = run(combine, [[e_away, e_away1]])
        e_away = send(e_away, Y)
        result, sums3 = run(
            call_result, me, True, mod, vec, tokens, out_grad, attn, [act0, act1, act2, act3], [w_down, down_a, down_b]
        )
        n1 = run(combine, [[nb_keep, na_keep1, n1_away]])
        p0, p0_away = run(combine, [[p0, p0_away]], 2)
        g_keep1 = send(g_keep1, CORE)
        p1, p1_away = run(combine, [[n1, f1]], 2)
        p1_away = send(p1_away, Z1)
        tok_grad, sums1 = run(call_tokens, mod, vec, tokens, dmid, dq, dk, dv, w_qkv)
        g, g_away = run(combine, [[g_keep, g_keep1, g_away]], 2)
        p0_away = send(p0_away, Z1)
        g_away = send(g_away, Y)
        e, e_away = run(combine, [[e_keep, e_keep1, e_away]], 2)
        e_away = send(e_away, X)
        p1, p1_away = run(combine, [[p1, p1_away]], 2)
        p1_away = send(p1_away, X)
        g, g_away = run(combine, [[g, g_away]], 2)
        g_away = send(g_away, Z0)
        e, e_away = run(combine, [[e, e_away]], 2)
        e_away = send(e_away, Z0)
        ffn = run(combine, [[p0, p0_away], [p1, p1_away]])
        g, g_away = run(combine, [[g, g_away]], 2)
        g_away = send(g_away, Z1)
        e, e_away = run(combine, [[e, e_away]], 2)
        pack = run(call_pack, timesteps, time_table, mod, vec, bd, sums1, sums2, sums3, [db0, db1, db2, db3])
        e_away = send(e_away, Z1)
        g = run(combine, [[g, g_away], [pack]])
        g_z = send(g, Z1)
        e = run(combine, [[e, e_away]])
        e_z = send(e, Z1)
        g = run(combine, [[g], [g_z]])
        g_z = send(g, Z0)
        ffn_z = send(ffn, Z1)
        e = run(combine, [[e], [e_z]])
        g = run(combine, [[g], [g_z]])
        g_x = send(g, X)
        e_z = send(e, Z0)
        ffn = run(combine, [[ffn], [ffn_z]])
        ffn_z = send(ffn, Z0)
        g = run(combine, [[g], [g_x]])
        g_x = send(g, Y)
        e = run(combine, [[e], [e_z]])
        e_x = send(e, X)
        g_c = send(g, CORE)
        ffn = run(combine, [[ffn], [ffn_z]])
        ffn_x = send(ffn, X)
        g_xc = send(g_x, CORE)
        e = run(combine, [[e], [e_x]])
        e_c = send(e, CORE)
        ffn_c = send(ffn, CORE)
        e_x = send(e, Y)
        qkv_wgrad, out_wgrad = run(call_attn_out, me, (8, 4), [g, g_x, g_c, g_xc])
        table_grad, gain1, gain2, bdown_grad, bias_grad, ada_w_grad, ada_b_grad = run(
            call_small, me, 2, ada_w, [g, g_x, g_c, g_xc], time_table.shape[0]
        )
        e_xc = send(e_x, CORE)
        (qkv_wgrad,) = run(call_attn_out, me, (8, 4), [e, e_x, e_c, e_xc], qkv_wgrad)
        ffn_xc = send(ffn_x, CORE)
        up_grad, down_grad = run(call_ffn_out, me, [ffn, ffn_x, ffn_c, ffn_xc])
        return (
            result, tok_grad, table_grad, gain1, gain2, qkv_wgrad, out_wgrad, up_grad, bias_grad, down_grad,
            bdown_grad, ada_w_grad, ada_b_grad,
        )

    me = jnp.zeros((4,), jnp.int32)
    parts = tokens.shape[0] // CHUNK
    h1, q, k, v, p, att, attn, h2, dbl, bd, mod, vec, *_ = call_forward(
        lengths, timesteps, small, cos, sin, time_table, ada_w, tokens, out_grad, w_qkv, w_out, parts
    )
    n = lax.axis_size("mlp")
    dh, acts, downs, up_sum, down_sum, bup_sum = None, [], [], 0.0, 0.0, 0.0
    for r in range(n):
        there = [(i, (i + r) % n) for i in range(n)]
        back = [((i + r) % n, i) for i in range(n)]
        move = lambda a: lax.ppermute(a, "mlp", there) if r else a
        home = lambda a: lax.ppermute(a, "mlp", back) if r else a
        downs.append(move(w_down))
        act, dh, db, g_up, g_down = call_ffn(
            me, 1, 0, True, h2, dbl, move(w_up).T, downs[-1], move(vec), dh, local, 9
        )
        acts.append(act)
        up_sum = up_sum + home(g_up).astype(f32)
        down_sum = down_sum + home(g_down).astype(f32)
        bup_sum = bup_sum + home(db[0])
    dmid, datt, dattn, dv, sums2 = call_mid(mod, vec, tokens, out_grad, attn, dh, p, w_out)
    dq, dk = call_scores(datt, q, k, v, p, cos, sin)
    w0, w1 = call_pair(me, 1, same, (h1, dq), (h1, dk))
    w2, w3 = call_pair(me, 1, same, (h1, dv), (att, dattn))
    tok_grad, sums1 = call_tokens(mod, vec, tokens, dmid, dq, dk, dv, w_qkv)
    result, sums3 = call_result(me, False, mod, vec, tokens, out_grad, attn, acts, downs)
    up_grad, down_grad, bias_grad = lax.psum((up_sum, down_sum, bup_sum), "seq")
    mod_grad = jnp.concatenate([
        sums1[0], sums1[1] * ln1_gain, sums2[2], sums2[0], sums2[1] * ln2_gain, sums3[0],
    ])[None]
    gains = jnp.stack([sums1[1] * (1.0 + mod[1]), sums2[1] * (1.0 + mod[4]), bd[0]])
    hot = (timesteps[:, None] == jnp.arange(time_table.shape[0], dtype=jnp.int32)[None, :]).astype(f32)
    qkv_wgrad = jnp.concatenate([w0, w1, w2], axis=1).astype(f32)
    qkv_wgrad, out_wgrad, ada_w_grad, ada_b_grad, table_grad, gains = lax.psum(
        (
            qkv_wgrad, w3.astype(f32), jnp.dot(cond.T, mod_grad, precision=HIGH), mod_grad[0],
            jnp.dot(hot.T, jnp.dot(mod_grad, ada_w.T, precision=HIGH), precision=HIGH), gains,
        ),
        ("seq", "mlp"),
    )
    return (
        result, tok_grad, table_grad, gains[0], gains[1], qkv_wgrad, out_wgrad, up_grad, bias_grad, down_grad,
        gains[2], ada_w_grad, ada_b_grad,
    )


def solution(mesh):
    tuned = mesh.shape["seq"] == 16 and mesh.shape["mlp"] == 2
    rows = P(("seq", "mlp"), None)
    flat = P(("seq", "mlp"))

    def whole(
        tokens, time_table, timesteps, lengths, ln1_gain, ln2_gain, w_qkv, w_out, w_up, b_up, w_down, b_down,
        ada_w, ada_b, out_grad,
    ):
        return shards(
            tuned, tokens, time_table, timesteps, lengths, ln1_gain, ln2_gain, w_qkv, w_out, w_up, b_up, w_down,
            b_down, ada_w, ada_b, out_grad,
        )

    return jax.shard_map(
        whole,
        mesh=mesh,
        in_specs=(
            rows, P(), flat, flat, P(), P(), P(), P(), P(None, "mlp"), P("mlp"), P("mlp", None), P(), P(), P(), rows,
        ),
        out_specs=(
            rows, rows, P(), P(), P(), P(), P(), P(None, "mlp"), P("mlp"), P("mlp", None), P(), P(), P(),
        ),
        check_vma=False,
    )
```

```python
import functools

import jax
import jax.numpy as jnp
import numpy as np
from jax import lax
from jax.experimental import pallas as pl
from jax.experimental.pallas import tpu as pltpu
from jax.sharding import PartitionSpec as P

H = 12
SLOT = 128
HIGH = lax.Precision.HIGHEST
f32 = jnp.float32
bf16 = jnp.bfloat16
Y, CORE, X, Z0, Z1 = 1, 2, 4, 8, 16
LIMIT = 12 * 1024 * 1024
CHUNK = 256
SCALE = 0.01
PARTS = 2
FORWARD = 24 * 1024 * 1024
GROUP = 6


def nn(a, b):
    return jnp.dot(a, b, preferred_element_type=f32)


def nt(a, b):
    return lax.dot_general(a, b, (((1,), (1,)), ((), ())), preferred_element_type=f32)


def tn(a, b):
    return lax.dot_general(a, b, (((0,), (0,)), ((), ())), preferred_element_type=f32)


def whiten(x):
    center = x - jnp.mean(x, axis=-1, keepdims=True)
    spread = jnp.mean(center * center, axis=-1, keepdims=True)
    rs = lax.rsqrt(spread + 1e-06)
    return center * rs, rs


def whiten_back(grad, unit, rs):
    return rs * (
        grad
        - jnp.mean(grad, axis=-1, keepdims=True)
        - unit * jnp.mean(grad * unit, axis=-1, keepdims=True)
    )


def half_turn(u, first):
    return jnp.where(first, pltpu.roll(u, 96, 1), pltpu.roll(u, 32, 1))


def split_heads(u, low):
    zero = jnp.zeros_like(u)
    return jnp.concatenate([jnp.where(low, u, zero), jnp.where(low, zero, u)], axis=0)


def lane_masks(shape):
    lane = lax.broadcasted_iota(jnp.int32, shape, 1)
    return lane < 64, lax.rem(lane, 64) < 32


def call(body, outs, args, scalars=1, scratch=(), limit=LIMIT, name=None, us=1):
    specs = [pl.BlockSpec(memory_space=pltpu.SMEM)] * scalars
    specs += [pl.BlockSpec(memory_space=pltpu.VMEM)] * (len(args) - scalars)
    return pl.pallas_call(
        body,
        in_specs=specs,
        out_specs=[pl.BlockSpec(memory_space=pltpu.VMEM)] * len(outs),
        out_shape=[jax.ShapeDtypeStruct(*o) for o in outs],
        scratch_shapes=list(scratch),
        compiler_params=pltpu.CompilerParams(vmem_limit_bytes=limit),
        cost_estimate=pl.CostEstimate(flops=int(us * SCALE * 1.15e9), bytes_accessed=0, transcendentals=0),
        name=name,
    )(*args)


def chunk(i, size=CHUNK):
    return pl.ds(pl.multiple_of(i * size, size), size)


def add_row(ref, at, value):
    ref[at : at + 1, :] = ref[at : at + 1, :] + jnp.sum(value, axis=0, keepdims=True)


def mod_rows(row, ada_w, vec, mod_o):
    width = mod_o.shape[1]
    cols = width // 128
    col = jnp.broadcast_to(row, (128, 128)).T
    for j in range(6 * cols):
        sl = slice(128 * j, 128 * j + 128)
        out = jnp.sum(ada_w[:, sl] * col, axis=0, keepdims=True)
        to = slice(128 * (j % cols), 128 * (j % cols) + 128)
        mod_o[j // cols : j // cols + 1, to] = out + vec[j // cols : j // cols + 1, to]
    mod_o[6:8, :] = jnp.zeros((2, width), f32)


def forward_chunks(
    parts, ready, lens, mod, vec, cos, sin, tok, dy, wqkv, wout,
    h1_o, q_o, k_o, v_o, p_o, att_o, attn_o, h2_o, dbl_o, bd_o,
):
    width = tok.shape[1]
    cols = width // 128
    low, first = lane_masks((SLOT, 128))
    key_at = lax.broadcasted_iota(jnp.int32, (SLOT, SLOT), 0)
    slots = CHUNK // SLOT
    for i in parts:
        cr = slice(i * CHUNK, i * CHUNK + CHUNK)
        x = tok[cr, :].astype(f32)
        unit, _ = whiten(x)
        h1 = (unit * (vec[6:7, :] * (1.0 + mod[1:2, :])) + mod[0:1, :]).astype(bf16)
        h1_o[cr, :] = h1
        qkv = nn(h1, wqkv[...])
        cosv = cos[...]
        sinv = sin[...]
        units = [(s, j) for s in range(slots) for j in range(cols)]
        for g0 in range(0, len(units), GROUP):
            part = units[g0 : g0 + GROUP]
            kept = []
            for s, j in part:
                rows = slice(s * SLOT, s * SLOT + SLOT)
                out = slice(i * CHUNK + s * SLOT, i * CHUNK + s * SLOT + SLOT)
                sl = slice(128 * j, 128 * j + 128)
                q = qkv[rows, 128 * j : 128 * j + 128]
                k = qkv[rows, width + 128 * j : width + 128 * j + 128]
                v = qkv[rows, 2 * width + 128 * j : 2 * width + 128 * j + 128].astype(bf16)
                q = (q * cosv + half_turn(q, first) * sinv).astype(bf16)
                k = (k * cosv + half_turn(k, first) * sinv).astype(bf16)
                q_o[out, sl] = q
                k_o[out, sl] = k
                v_o[out, sl] = v
                kept.append((nt(split_heads(k, low), q), v))
            probs = []
            for (s, j), (sc, v) in zip(part, kept):
                valid = key_at < lens[i * slots + s]
                two = []
                for e in range(2):
                    x2 = jnp.where(valid, sc[SLOT * e : SLOT * e + SLOT, :], -1e30)
                    ex = jnp.exp((x2 - jnp.max(x2, axis=0, keepdims=True)) * 0.125)
                    two.append((ex * (1.0 / jnp.sum(ex, axis=0, keepdims=True))).astype(bf16))
                pr = jnp.concatenate(two, axis=0)
                at = ((i * slots + s) * cols + j) * 256
                p_o[at : at + 256, :] = pr
                probs.append(pr)
            for (s, j), (sc, v), pr in zip(part, kept, probs):
                out = slice(i * CHUNK + s * SLOT, i * CHUNK + s * SLOT + SLOT)
                att_o[out, 128 * j : 128 * j + 128] = tn(pr, split_heads(v, low)).astype(bf16)
        if i == 0:
            ready()
        attn = nn(att_o[cr, :], wout[...])
        attn_o[cr, :] = attn.astype(bf16)
        unit2, _ = whiten(x + mod[2:3, :] * attn)
        h2_o[cr, :] = (unit2 * (vec[7:8, :] * (1.0 + mod[4:5, :])) + mod[3:4, :]).astype(bf16)
        dbl = (dy[cr, :].astype(f32) * mod[5:6, :]).astype(bf16)
        dbl_o[cr, :] = dbl
        add_row(bd_o, 0, dbl.astype(f32))


def forward_kernel(
    parts, lens, ts, ada_b, gain1, gain2, bdown, bup, cos, sin, tab_h, ada_h, tok_h, dy_h, wqkv_h, wout_h,
    h1_o, q_o, k_o, v_o, p_o, att_o, attn_o, h2_o, dbl_o, bd_o, mod, vec, wqkv, wout,
    tab, ada_w, tok, dy, sem,
):
    rows = pl.ds(0, tok.shape[0])
    loads = [
        pltpu.make_async_copy(tab_h.at[pl.ds(pl.multiple_of(ts[0] // 8 * 8, 8), 8), :], tab, sem.at[0]),
        pltpu.make_async_copy(ada_h, ada_w, sem.at[1]),
        pltpu.make_async_copy(tok_h.at[rows, :], tok, sem.at[2]),
        pltpu.make_async_copy(wqkv_h, wqkv, sem.at[3]),
        pltpu.make_async_copy(dy_h.at[rows, :], dy, sem.at[4]),
        pltpu.make_async_copy(wout_h, wout, sem.at[5]),
    ]
    for load in loads[:2]:
        load.start()
    vec_rows(ada_b, gain1, gain2, bdown, bup, vec)
    bd_o[...] = jnp.zeros_like(bd_o)
    loads[0].wait()
    loads[1].wait()
    for load in loads[2:4]:
        load.start()
    mod_rows(tab[pl.ds(lax.rem(ts[0], 8), 1), :], ada_w, vec, mod)
    for load in loads[4:]:
        load.start()
    loads[2].wait()
    loads[3].wait()

    def ready():
        loads[4].wait()
        loads[5].wait()

    forward_chunks(
        range(parts), ready, lens, mod, vec, cos, sin, tok, dy, wqkv, wout,
        h1_o, q_o, k_o, v_o, p_o, att_o, attn_o, h2_o, dbl_o, bd_o,
    )


def rest_kernel(parts, lens, mod, vec, cos, sin, tok, dy, wqkv, wout, *refs):
    forward_chunks(
        range(parts, tok.shape[0] // CHUNK), lambda: None, lens, mod, vec, cos, sin, tok, dy, wqkv, wout, *refs[10:]
    )


def call_forward(lens, ts, small, cos, sin, tab, ada_w, tok, dy, wqkv, wout, parts):
    tokens, width = tok.shape
    s = jax.ShapeDtypeStruct
    low = s((tokens, width), bf16)
    args = [lens, ts, *small, cos, sin, tab, ada_w, tok, dy, wqkv, wout]
    return pl.pallas_call(
        functools.partial(forward_kernel, parts),
        in_specs=[pl.BlockSpec(memory_space=pltpu.SMEM)] * 2
        + [pl.BlockSpec(memory_space=pltpu.VMEM)] * 7
        + [pl.BlockSpec(memory_space=pltpu.HBM)] * 6,
        out_specs=[pl.BlockSpec(memory_space=pltpu.VMEM)] * 14,
        out_shape=[
            low, low, low, low, s((tokens * H, SLOT), bf16), low, low, low, low,
            s((8, width), f32), s((8, width), f32), s((16, width), f32), s(wqkv.shape, bf16), s(wout.shape, bf16),
        ],
        scratch_shapes=[
            pltpu.VMEM((8, 128), f32), pltpu.VMEM(ada_w.shape, f32), pltpu.VMEM((parts * CHUNK, width), bf16),
            pltpu.VMEM((parts * CHUNK, width), bf16), pltpu.SemaphoreType.DMA((6,)),
        ],
        compiler_params=pltpu.CompilerParams(vmem_limit_bytes=FORWARD),
        cost_estimate=pl.CostEstimate(flops=int(7 * SCALE * 1.15e9), bytes_accessed=0, transcendentals=0),
        name="attention_forward",
    )(*args)


def call_rest(lens, mod, vec, cos, sin, tok, dy, wqkv, wout, outs, parts):
    args = [lens, mod, vec, cos, sin, tok, dy, wqkv, wout, *outs]
    vmem = pl.BlockSpec(memory_space=pltpu.VMEM)
    return pl.pallas_call(
        functools.partial(rest_kernel, parts),
        in_specs=[pl.BlockSpec(memory_space=pltpu.SMEM)] + [vmem] * (len(args) - 1),
        out_specs=[vmem] * len(outs),
        out_shape=[jax.ShapeDtypeStruct(a.shape, a.dtype) for a in outs],
        input_output_aliases={9 + i: i for i in range(len(outs))},
        compiler_params=pltpu.CompilerParams(vmem_limit_bytes=LIMIT),
        cost_estimate=pl.CostEstimate(flops=int(7 * SCALE * 1.15e9), bytes_accessed=0, transcendentals=0),
        name="attention_rest",
    )(*args)


def gelu_parts(v):
    c = 0.7978845608028654
    v2 = v * v
    t = jnp.tanh(v * (c + c * 0.044715 * v2))
    h = 0.5 + 0.5 * t
    act = v * h
    slope = h + act * (1.0 - h) * (2.0 * c + 6.0 * c * 0.044715 * v2)
    return act, slope


def put_rows(outs, scratch, me, blocks, place):
    size = scratch.shape[0] // blocks
    for r in range(blocks):
        src = pl.multiple_of(lax.bitwise_xor(r, me) * size, size)
        half, at = divmod(place(r), blocks // 2)
        outs[half][at * size : at * size + size, :] = scratch[pl.ds(src, size), :].astype(bf16)


def same(r):
    return r


def ffn_first(r):
    return (r & 4) | ((r & 1) << 1) | ((r & 2) >> 1)


def ffn_second(r):
    return ((r & 1) << 2) | (r & 2) | (r >> 2)


def xy_first(r):
    return (r & 12) | ((r & 1) << 1) | ((r & 2) >> 1)


def yx_first(r):
    return ((r & 4) << 1) | ((r & 8) >> 1) | ((r & 1) << 1) | ((r & 2) >> 1)


def ffn_kernel(blocks, half, far, first, bias_row, me, h2, dbl, wup, wdn, bup, *refs):
    dh_in = None if first else refs[0]
    act_o, dh_o, db_o, *outs, dpre_s, gup, gdn = refs if first else refs[1:]
    tokens = h2.shape[0]
    hb = act_o.shape[1]
    hid = half ^ me[0] if blocks > 1 else 0
    bias = bup[pl.ds(bias_row + hid, 1), :hb].astype(f32)
    cols = pl.ds(pl.multiple_of(hid * hb, 128), hb)
    up = wup[...] if far else wup[:, cols]
    dn = wdn[...] if far else wdn[cols, :]
    total = jnp.zeros((1, hb), f32)
    for m in range(tokens // CHUNK):
        rows = slice(m * CHUNK, m * CHUNK + CHUNK)
        pre = nt(h2[rows, :], up) if far else nn(h2[rows, :], up)
        act, slope = gelu_parts(pre + bias)
        act_o[rows, :] = act.astype(bf16)
        dpre = (nt(dbl[rows, :], dn) * slope).astype(bf16)
        dpre_s[rows, :] = dpre
        total = total + jnp.sum(dpre.astype(f32), axis=0, keepdims=True)
        back = nn(dpre, up) if far else nt(dpre, up)
        dh_o[rows, :] = back if first else dh_in[rows, :] + back
    db_o[...] = jnp.broadcast_to(total, db_o.shape)
    gup[...] = tn(h2[...], dpre_s[...])
    gdn[...] = tn(act_o[...], dbl[...])
    if blocks == 1:
        outs[0][...] = gup[...].astype(bf16)
        outs[1][...] = gdn[...].astype(bf16)
        return

    ours, theirs = (ffn_first, ffn_second) if half == 0 else (ffn_second, ffn_first)

    @pl.when(me[0] == 0)
    def _():
        put_rows(outs[:2], gup, me[1], blocks, ours)
        put_rows(outs[2:], gdn, me[1], blocks, theirs)

    @pl.when(me[0] != 0)
    def _():
        put_rows(outs[:2], gdn, me[1], blocks, ours)
        put_rows(outs[2:], gup, me[1], blocks, theirs)


def call_ffn(me, blocks, half, far, h2, dbl, wup, wdn, bup, dh, hb, bias_row):
    tokens, width = h2.shape
    first = dh is None
    return call(
        functools.partial(ffn_kernel, blocks, half, far, first, bias_row),
        [((tokens, hb), bf16), ((tokens, width), f32), ((8, hb), f32)]
        + ([((width, hb), bf16), ((hb, width), bf16)] if blocks == 1 else [((width // 2, hb), bf16)] * 4),
        [me, h2, dbl, wup, wdn, bup] + ([] if first else [dh]),
        scratch=[pltpu.VMEM((tokens, hb), bf16), pltpu.VMEM((width, hb), f32), pltpu.VMEM((hb, width), f32)],
        name="feed_forward", us=8,
    )


def vec_rows(ada_b, gain1, gain2, bdown, bup, vec):
    width = vec.shape[1]
    vec[...] = jnp.zeros_like(vec)
    for j in range(6):
        vec[j : j + 1, :] = ada_b[j * width : j * width + width].reshape(1, width)
    vec[6:7, :] = gain1[...].reshape(1, width)
    vec[7:8, :] = gain2[...].reshape(1, width)
    vec[8:9, :] = bdown[...].astype(f32).reshape(1, width)
    size = min(width, bup.shape[0])
    for j in range(bup.shape[0] // size):
        vec[9 + j : 10 + j, :size] = bup[j * size : j * size + size].astype(f32).reshape(1, size)


def send_kernel(me, bup, wup, wdn, own, diag, rows, cols, sem):
    size = own.shape[0]
    pairs = [(own, me[3]), (diag, me[3] ^ 3)]
    @pl.when(me[0] == 0)
    def _():
        copies = [
            pltpu.make_async_copy(wup.at[:, pl.ds(pl.multiple_of(quarter * size, 128), size)], cols.at[i], sem.at[i])
            for i, (out, quarter) in enumerate(pairs)
        ]
        for copy in copies:
            copy.start()
        for i, (out, quarter) in enumerate(pairs):
            copies[i].wait()
            out[:size, :] = cols[i].T

    @pl.when(me[0] != 0)
    def _():
        copies = [
            pltpu.make_async_copy(wdn.at[pl.ds(pl.multiple_of(quarter * size, 128), size), :], rows.at[i], sem.at[i])
            for i, (out, quarter) in enumerate(pairs)
        ]
        for copy in copies:
            copy.start()
        for i, (out, quarter) in enumerate(pairs):
            copies[i].wait()
            out[:size, :] = rows[i]

    width = own.shape[1]
    diag[size : size + 16, :] = jnp.zeros((16, width), bf16)
    for j in range(bup.shape[0] // width):
        diag[size + j : size + j + 1, :] = bup[j * width : j * width + width].reshape(1, width)


def call_send(me, bup, wup, wdn):
    width = wup.shape[0]
    size = wup.shape[1] // 4
    return pl.pallas_call(
        send_kernel,
        in_specs=[pl.BlockSpec(memory_space=pltpu.SMEM), pl.BlockSpec(memory_space=pltpu.VMEM)]
        + [pl.BlockSpec(memory_space=pltpu.HBM)] * 2,
        out_specs=[pl.BlockSpec(memory_space=pltpu.VMEM)] * 2,
        out_shape=[
            jax.ShapeDtypeStruct((size, width), bf16), jax.ShapeDtypeStruct((size + 16, width), bf16),
        ],
        scratch_shapes=[
            pltpu.VMEM((2, size, width), bf16), pltpu.VMEM((2, width, size), bf16), pltpu.SemaphoreType.DMA((2,)),
        ],
        compiler_params=pltpu.CompilerParams(vmem_limit_bytes=60 * 1024 * 1024),
        cost_estimate=pl.CostEstimate(flops=int(SCALE * 1.15e9), bytes_accessed=0, transcendentals=0),
        name="weight_parts",
    )(me, bup, wup, wdn)


def far_kernel(me, *refs):
    ups = refs[8:10]
    downs = refs[10:12]
    sem = refs[12]
    size = ups[0].shape[0] // 2
    for core in range(2):
        for flip in range(4):
            @pl.when(jnp.logical_and(me[0] == core, me[3] == flip))
            def _():
                copies = []
                for r in range(4):
                    quarter = flip ^ r
                    half = (quarter >> 1) ^ core
                    at = pl.ds((quarter & 1) * size, size)
                    up, down = (refs[r], refs[4 + r]) if core == 0 else (refs[4 + r], refs[r])
                    copies.append(pltpu.make_async_copy(up.at[pl.ds(0, size), :], ups[half].at[at, :], sem.at[r]))
                    copies.append(
                        pltpu.make_async_copy(down.at[pl.ds(0, size), :], downs[half].at[at, :], sem.at[4 + r])
                    )
                for copy in copies:
                    copy.start()
                for copy in copies:
                    copy.wait()


def call_far(me, pieces):
    size, width = pieces[0].shape
    return pl.pallas_call(
        far_kernel,
        in_specs=[pl.BlockSpec(memory_space=pltpu.SMEM)] + [pl.BlockSpec(memory_space=pl.ANY)] * 8,
        out_specs=[pl.BlockSpec(memory_space=pltpu.VMEM)] * 4,
        out_shape=[jax.ShapeDtypeStruct((2 * size, width), bf16)] * 4,
        scratch_shapes=[pltpu.SemaphoreType.DMA((8,))],
        compiler_params=pltpu.CompilerParams(vmem_limit_bytes=LIMIT),
        cost_estimate=pl.CostEstimate(flops=int(2 * SCALE * 1.15e9), bytes_accessed=0, transcendentals=0),
        name="far_weights",
    )(me, *pieces)


def mid_kernel(mod, vec, tok, dy, attn, dh, p_i, wout, dmid_o, datt_o, dattn_o, dv_o, sums):
    width = tok.shape[1]
    cols = width // 128
    low, _ = lane_masks((SLOT, 128))
    sums[...] = jnp.zeros_like(sums)
    for i in range(tok.shape[0] // CHUNK):
        cr = slice(i * CHUNK, i * CHUNK + CHUNK)
        attnv = attn[cr, :].astype(f32)
        gate1 = mod[2:3, :]
        unit, rs = whiten(tok[cr, :].astype(f32) + gate1 * attnv)
        dh2 = dh[cr, :]
        dmid = dy[cr, :].astype(f32) + whiten_back(dh2 * (vec[7:8, :] * (1.0 + mod[4:5, :])), unit, rs)
        dmid_o[cr, :] = dmid
        add_row(sums, 0, dh2)
        add_row(sums, 1, dh2 * unit)
        add_row(sums, 2, dmid * attnv)
        dattn = (dmid * gate1).astype(bf16)
        dattn_o[cr, :] = dattn
        datt = nt(dattn, wout[...]).astype(bf16)
        datt_o[cr, :] = datt
        for s in range(CHUNK // SLOT):
            rows = slice(i * CHUNK + s * SLOT, i * CHUNK + s * SLOT + SLOT)
            for j in range(cols):
                sl = slice(128 * j, 128 * j + 128)
                at = ((i * (CHUNK // SLOT) + s) * cols + j) * 256
                dv = nn(p_i[at : at + 256, :], datt[s * SLOT : s * SLOT + SLOT, sl])
                dv_o[rows, sl] = jnp.where(low, dv[:SLOT], dv[SLOT:]).astype(bf16)


def call_mid(mod, vec, tok, dy, attn, dh, p, wout):
    tokens, width = tok.shape
    low = ((tokens, width), bf16)
    return call(
        mid_kernel, [((tokens, width), f32), low, low, low, ((8, width), f32)],
        [mod, vec, tok, dy, attn, dh, p, wout], scalars=0, name="mid_grads", us=6,
    )


def scores_kernel(datt, q_i, k_i, v_i, p_i, cos, sin, dq_o, dk_o):
    width = datt.shape[1]
    cols = width // 128
    low, first = lane_masks((SLOT, 128))
    cosv = cos[...]
    sinv = sin[...]

    def one(s, _):
        rows = chunk(s, SLOT)
        kept = []
        for j in range(cols):
            sl = slice(128 * j, 128 * j + 128)
            pr = p_i[chunk(s * cols + j, 256), :]
            kept.append((nt(split_heads(v_i[rows, sl], low), datt[rows, sl]), pr.astype(f32)))
        scores = []
        for dp, pr in kept:
            ds = []
            for e in range(2):
                ee = slice(SLOT * e, SLOT * e + SLOT)
                d = jnp.sum(pr[ee, :] * dp[ee, :], axis=0, keepdims=True)
                ds.append((pr[ee, :] * (dp[ee, :] - d)).astype(bf16))
            scores.append(jnp.concatenate(ds, axis=0))
        for j, ds in enumerate(scores):
            sl = slice(128 * j, 128 * j + 128)
            dq = tn(ds, split_heads(k_i[rows, sl], low)) * 0.125
            dk = nn(ds, q_i[rows, sl])
            dk = jnp.where(low, dk[:SLOT], dk[SLOT:]) * 0.125
            dq_o[rows, sl] = (dq * cosv - half_turn(dq, first) * sinv).astype(bf16)
            dk_o[rows, sl] = (dk * cosv - half_turn(dk, first) * sinv).astype(bf16)
        return 0

    lax.fori_loop(0, datt.shape[0] // SLOT, one, 0, unroll=2)


def call_scores(datt, q, k, v, p, cos, sin):
    low = (datt.shape, bf16)
    return call(scores_kernel, [low, low], [datt, q, k, v, p, cos, sin], scalars=0, name="score_grads", us=7)


def pair_kernel(blocks, place, me, a0, b0, a1, b1, *refs):
    *outs, acc0, acc1 = refs
    if blocks == 1:
        outs[0][...] = tn(a0[...], b0[...]).astype(bf16)
        outs[1][...] = tn(a1[...], b1[...]).astype(bf16)
        return

    acc0[...] = tn(a0[...], b0[...])
    acc1[...] = tn(a1[...], b1[...])

    @pl.when(me[0] == 0)
    def _():
        put_rows(outs[:2], acc0, me[2], blocks, place)
        put_rows(outs[2:], acc1, me[2], blocks, place)

    @pl.when(me[0] != 0)
    def _():
        put_rows(outs[:2], acc1, me[2], blocks, place)
        put_rows(outs[2:], acc0, me[2], blocks, place)


def call_pair(me, blocks, place, first, second):
    a0, b0 = first
    a1, b1 = second
    width = a0.shape[1]
    return call(
        functools.partial(pair_kernel, blocks, place),
        [((width, width), bf16)] * 2 if blocks == 1 else [((width // 2, width), bf16)] * 4,
        [me, a0, b0, a1, b1],
        scratch=[pltpu.VMEM((width, width), f32)] * 2,
        name="weight_grads", us=4,
    )


def tokens_kernel(mod, vec, tok, dmid, dq, dk, dv, wqkv, dtok_o, sums):
    sums[...] = jnp.zeros_like(sums)
    for m in range(tok.shape[0] // CHUNK):
        cr = slice(m * CHUNK, m * CHUNK + CHUNK)
        width = tok.shape[1]
        dh1 = nt(dq[cr, :], wqkv[:, :width])
        dh1 = dh1 + nt(dk[cr, :], wqkv[:, width : 2 * width])
        dh1 = dh1 + nt(dv[cr, :], wqkv[:, 2 * width :])
        unit, rs = whiten(tok[cr, :].astype(f32))
        add_row(sums, 0, dh1)
        add_row(sums, 1, dh1 * unit)
        dtok_o[cr, :] = (dmid[cr, :] + whiten_back(dh1 * (vec[6:7, :] * (1.0 + mod[1:2, :])), unit, rs)).astype(bf16)


def call_tokens(mod, vec, tok, dmid, dq, dk, dv, wqkv):
    tokens, width = tok.shape
    return call(
        tokens_kernel, [((tokens, width), bf16), ((8, width), f32)], [mod, vec, tok, dmid, dq, dk, dv, wqkv],
        scalars=0, name="token_grads", us=6, limit=18 * 1024 * 1024,
    )


def result_kernel(parts, far, me, mod, vec, tok, dy, attn, *refs):
    acts = refs[:parts]
    downs = refs[parts:-2]
    out_o, sums = refs[-2:]
    hb = acts[0].shape[1]
    sums[...] = jnp.zeros_like(sums)

    for m in range(tok.shape[0] // CHUNK):
        cr = slice(m * CHUNK, m * CHUNK + CHUNK)
        branch = vec[8:9, :] + jnp.zeros((CHUNK, tok.shape[1]), f32)
        for n in range(parts):
            if far:
                dn = downs[0][chunk(n ^ me[0], hb), :] if n < 2 else downs[n - 1][...]
            else:
                dn = downs[n][...]
            branch = branch + nn(acts[n][cr, :], dn)
        out_o[cr, :] = (
            tok[cr, :].astype(f32) + mod[2:3, :] * attn[cr, :].astype(f32) + mod[5:6, :] * branch
        ).astype(bf16)
        add_row(sums, 0, dy[cr, :].astype(f32) * branch)


def call_result(me, far, mod, vec, tok, dy, attn, acts, downs):
    tokens, width = tok.shape
    return call(
        functools.partial(result_kernel, len(acts), far),
        [((tokens, width), bf16), ((8, width), f32)],
        [me, mod, vec, tok, dy, attn] + acts + downs,
        name="output_rows", us=7, limit=18 * 1024 * 1024,
    )


def ffn_out_kernel(me, *refs):
    up_o, down_o, up_s, down_s, sem = refs[4:]
    width = refs[0].shape[1]
    size = width // 8
    copies = []
    for a in range(2):
        half = (me[1] >> 2) ^ a
        for n, z in enumerate((0, 2, 1, 3)):
            at = pl.multiple_of(lax.bitwise_xor(a * 4 + z, me[1]) * size, size)
            for t in range(2):
                src = slice((2 * n + t) * size, (2 * n + t) * size + size)

                @pl.when(me[0] == 0)
                def _():
                    up_s[pl.ds(at, size), t * width : t * width + width] = refs[a][src, :].astype(f32)
                    down_s[pl.ds((1 - t) * width + at, size), :] = refs[2 + a][src, :].astype(f32)

                @pl.when(me[0] != 0)
                def _():
                    up_s[pl.ds(at, size), t * width : t * width + width] = refs[2 + a][src, :].astype(f32)
                    down_s[pl.ds((1 - t) * width + at, size), :] = refs[a][src, :].astype(f32)

        rows = pl.ds(pl.multiple_of(half * (width // 2), width // 2), width // 2)
        copies.append(pltpu.make_async_copy(up_s.at[rows, :], up_o.at[rows, :], sem.at[3 * a]))
        for t in range(2):
            rows = pl.ds(pl.multiple_of(half * (width // 2) + t * width, width // 2), width // 2)
            copies.append(pltpu.make_async_copy(down_s.at[rows, :], down_o.at[rows, :], sem.at[3 * a + 1 + t]))
        for copy in copies[3 * a :]:
            copy.start()
    for copy in copies:
        copy.wait()


def call_ffn_out(me, pieces):
    width = pieces[0].shape[1]
    shapes = [(width, 2 * width), (2 * width, width)]
    return pl.pallas_call(
        ffn_out_kernel,
        in_specs=[pl.BlockSpec(memory_space=pltpu.SMEM)] + [pl.BlockSpec(memory_space=pltpu.VMEM)] * 4,
        out_specs=[pl.BlockSpec(memory_space=pltpu.HBM)] * 2,
        out_shape=[jax.ShapeDtypeStruct(shape, f32) for shape in shapes],
        scratch_shapes=[pltpu.VMEM(shape, f32) for shape in shapes] + [pltpu.SemaphoreType.DMA((6,))],
        compiler_params=pltpu.CompilerParams(vmem_limit_bytes=LIMIT),
        cost_estimate=pl.CostEstimate(flops=int(3 * SCALE * 1.15e9), bytes_accessed=0, transcendentals=0),
        name="feed_forward_grads",
    )(me, *pieces)


def attn_out_kernel(last, axes, me, *refs):
    if last:
        qkv_o, scratch, sem = refs[5:]
    else:
        qkv_o, out_o, scratch, sem = refs[4:]
    width = refs[0].shape[1]
    size = width // 16
    every = refs[0].shape[0] // 8
    copies = []
    for n, xy in enumerate((0, axes[0], axes[1], 12)):
        for i, z in enumerate((0, 2, 1, 3)):
            at = pl.ds(pl.multiple_of(lax.bitwise_xor(xy + z, me[2]) * size, size), size)
            row = (4 * (n % 2) + i) * every
            src = slice(row, row + size)

            for core in range(2):
                @pl.when(me[0] == core)
                def _():
                    scratch[at, :width] = refs[2 * core + n // 2][src, :].astype(f32)
                    scratch[at, width:] = refs[2 * (1 - core) + n // 2][src, :].astype(f32)

        at = pl.ds(pl.multiple_of((lax.bitwise_xor(xy, me[2]) >> 2) * (4 * size), 4 * size), 4 * size)
        if last:
            copies.append(pltpu.make_async_copy(scratch.at[at, :], qkv_o.at[at, pl.ds(0, 2 * width)], sem.at[2 * n]))
        else:
            copies.append(
                pltpu.make_async_copy(
                    scratch.at[at, pl.ds(0, width)], qkv_o.at[at, pl.ds(2 * width, width)], sem.at[2 * n]
                )
            )
            copies.append(
                pltpu.make_async_copy(scratch.at[at, pl.ds(width, width)], out_o.at[at, :], sem.at[2 * n + 1])
            )
        for copy in copies[n * (1 if last else 2) :]:
            copy.start()
    for copy in copies:
        copy.wait()


def call_attn_out(me, axes, pieces, qkv=None):
    width = pieces[0].shape[1]
    last = qkv is not None
    shapes = [(width, 3 * width)] + ([] if last else [(width, width)])
    hbm = pl.BlockSpec(memory_space=pltpu.HBM)
    return pl.pallas_call(
        functools.partial(attn_out_kernel, last, axes),
        in_specs=[pl.BlockSpec(memory_space=pltpu.SMEM)] + [pl.BlockSpec(memory_space=pltpu.VMEM)] * 4
        + ([hbm] if last else []),
        out_specs=[hbm] * len(shapes),
        out_shape=[jax.ShapeDtypeStruct(shape, f32) for shape in shapes],
        scratch_shapes=[pltpu.VMEM((width, 2 * width), f32), pltpu.SemaphoreType.DMA((8,))],
        input_output_aliases={5: 0} if last else {},
        compiler_params=pltpu.CompilerParams(vmem_limit_bytes=LIMIT),
        cost_estimate=pl.CostEstimate(flops=int(3 * SCALE * 1.15e9), bytes_accessed=0, transcendentals=0),
        name="attention_grads",
    )(me, *pieces, *([qkv] if last else []))


def split2(a):
    high = a.astype(bf16)
    return high, (a - high.astype(f32)).astype(bf16)


def pack_kernel(ts, tab, mod, vec, bd, sums1, sums2, sums3, d0, d1, d2, d3, out):
    rows = [
        sums1[0:1, :], sums1[1:2, :] * vec[6:7, :], sums2[2:3, :], sums2[0:1, :], sums2[1:2, :] * vec[7:8, :],
        sums3[0:1, :], sums1[1:2, :] * (1.0 + mod[1:2, :]), sums2[1:2, :] * (1.0 + mod[4:5, :]), bd[0:1, :],
        jnp.zeros_like(bd[0:1, :]), d0[0:1, :], d1[0:1, :], d2[0:1, :], d3[0:1, :], bd[0:1, :], bd[0:1, :],
    ]
    out[...] = jnp.concatenate(rows, axis=0).astype(bf16)
    cond = tab[pl.ds(ts[0], 1), :]
    high, low = split2(cond)
    lane = lax.broadcasted_iota(jnp.int32, (1, 128), 1)
    step = jnp.where(lane == 0, ts[0] // 128, jnp.where(lane == 1, lax.rem(ts[0], 128), 0)).astype(f32)
    out[9:10, :128] = high
    out[9:10, 128:256] = low
    out[9:10, 256:384] = step.astype(bf16)


def call_pack(ts, tab, mod, vec, bd, sums1, sums2, sums3, db):
    width = mod.shape[1]
    return call(
        pack_kernel, [((16, width), bf16)], [ts, tab, mod, vec, bd, sums1, sums2, sums3] + db, name="small_rows"
    )[0]


def small_kernel(far_bit, me, ada_w, *refs):
    table_o, gain1_o, gain2_o, bdown_o, bias_o, ada_w_o, ada_b_o, rows_s = refs[4:]
    width = gain1_o.shape[0]
    every = refs[0].shape[0] // 8
    bias = [jnp.zeros((1, width), f32), jnp.zeros((1, width), f32)]
    for n in range(8):
        for z in range(4):
            at = 4 * n + z
            row = (4 * (n % 2) + z) * every + every - 16
            pack = refs[n // 2][row : row + 16, :].astype(f32)
            for kind in range(10):
                rows_s[kind, at : at + 1, :] = pack[kind : kind + 1, :]
            base = 12 if n & far_bit else 10
            for h in range(2):
                to = h if n < 4 else 1 - h
                bias[to] = bias[to] + pack[base + h : base + h + 1, :]
    for h in range(2):
        bias_o[h * width : h * width + width] = jnp.where(me[0] == 0, bias[h], bias[1 - h]).reshape(width)
    for kind, gain_o in enumerate((gain1_o, gain2_o, bdown_o)):
        gain_o[...] = jnp.sum(rows_s[6 + kind], axis=0)
    extra = rows_s[9]
    high = extra[:, :128].astype(bf16)
    low = extra[:, 128:256].astype(bf16)
    step = extra[:, 256:257] * 128.0 + extra[:, 257:258]
    total = jnp.zeros((32, 128), f32)
    for kind in range(6):
        grad = rows_s[kind].astype(bf16)
        cols = slice(kind * width, kind * width + width)
        ada_b_o[cols] = jnp.sum(rows_s[kind], axis=0)
        ada_w_o[:, cols] = tn(high, grad) + tn(low, grad)
        whigh, wlow = split2(ada_w[:, cols])
        total = total + nt(grad, whigh) + nt(grad, wlow)
    lane = lax.broadcasted_iota(jnp.int32, (32, 1024), 1)
    hot = jnp.where(lane.astype(f32) == step, 1.0, 0.0).astype(bf16)
    thigh, tlow = split2(total)
    table_o[...] = (tn(hot, thigh) + tn(hot, tlow))[: table_o.shape[0], :]


def call_small(me, far_bit, ada_w, pieces, entries):
    width = pieces[0].shape[1]
    return call(
        functools.partial(small_kernel, far_bit),
        [
            ((entries, 128), f32), ((width,), f32), ((width,), f32), ((width,), f32), ((2 * width,), f32),
            ((128, 6 * width), f32), ((6 * width,), f32),
        ],
        [me, ada_w] + pieces, scratch=[pltpu.VMEM((10, 32, width), f32)], name="small_grads", us=4,
        limit=16 * 1024 * 1024,
    )


def swap(array, mask):
    return lax.ppermute(array, ("seq", "mlp"), [(i, i ^ mask) for i in range(32)])


def combine_kernel(sizes, *refs):
    outs = refs[sum(sizes):]
    rows = outs[0].shape[0]
    at = 0
    base = 0
    for n in sizes:
        group = refs[at : at + n]
        at += n
        size = group[0].shape[0]
        step = min(size, rows)
        for r in range(0, size, step):
            part = slice(r, r + step)
            if n == 1:
                value = group[0][part, :]
            else:
                value = group[0][part, :].astype(f32)
                for other in group[1:]:
                    value = value + other[part, :].astype(f32)
                value = value.astype(outs[0].dtype)
            out = (base + r) // rows
            to = base + r - out * rows
            outs[out][to : to + step, :] = value
        base += size


def combine(groups, pieces=1):
    arrays = [a for group in groups for a in group]
    rows = sum(group[0].shape[0] for group in groups)
    shape = (rows // pieces, arrays[0].shape[1])
    out = call(
        functools.partial(combine_kernel, [len(group) for group in groups]),
        [(shape, arrays[0].dtype)] * pieces, arrays, scalars=0, name="sums",
    )
    return out if pieces > 1 else out[0]


class Order:
    def __init__(self):
        self.last = None

    def run(self, function, *args, **kwargs):
        leaves, tree = jax.tree.flatten(list(args))
        if self.last is not None:
            at = [i for i, a in enumerate(leaves) if isinstance(a, jax.Array)][0]
            leaves[at] = tie(leaves[at], self.last)
        args = jax.tree.unflatten(tree, leaves)
        out = function(*args, **kwargs)
        self.last = min(out, key=lambda a: a.size) if isinstance(out, (list, tuple)) else out
        return out

    def swap(self, array, *masks):
        if self.last is not None:
            array = tie(array, self.last)
        out = [swap(array, mask) for mask in masks]
        return out if len(out) > 1 else out[0]


def tie(array, *after):
    return lax.optimization_barrier((array,) + after)[0]


def rope_tables(width):
    half = 32
    freq = np.float32(10000.0) ** (-np.arange(half, dtype=np.float32) / np.float32(half))
    angle = np.arange(SLOT, dtype=np.float32)[:, None] * freq[None, :]
    cos = np.cos(angle).astype(np.float32)
    sin = np.sin(angle).astype(np.float32)
    return (
        jnp.asarray(np.concatenate([cos, cos, cos, cos], axis=1)),
        jnp.asarray(np.concatenate([-sin, sin, -sin, sin], axis=1)),
    )


def shards(
    tuned, tokens, time_table, timesteps, lengths, ln1_gain, ln2_gain, w_qkv, w_out, w_up, b_up, w_down, b_down,
    ada_w, ada_b, out_grad,
):
    width = tokens.shape[1]
    local = w_up.shape[1]
    cos, sin = rope_tables(width)
    small = [ada_b, ln1_gain, ln2_gain, b_down, b_up]
    seq = lax.axis_index("seq")
    mlp = lax.axis_index("mlp")
    cond = lax.dynamic_slice_in_dim(time_table, timesteps[0], 1, 0)
    if tuned:
        core = seq & 1
        x = (seq >> 1) & 1
        z = seq >> 2
        me = jnp.stack([core, x * 4 + z, x * 8 + mlp * 4 + z, x * 2 + (z & 1)]).astype(jnp.int32)
        order = Order()
        run = order.run
        send = order.swap
        own, diag = run(call_send, me, b_up, w_up, w_down)
        own = send(own, Y)
        diag = send(diag, Y)
        *outs, mod, vec, wqkv, wout = run(
            call_forward, lengths, timesteps, small, cos, sin, time_table, ada_w, tokens, out_grad, w_qkv, w_out, PARTS
        )
        own_x = send(own, X)
        own_z = send(own, Z0)
        own_c = send(own, CORE)
        h1, q, k, v, p, att, attn, h2, dbl, bd = run(
            call_rest, lengths, mod, vec, cos, sin, tokens, out_grad, wqkv, wout, outs, PARTS
        )
        hb = local // 2
        act0, dh, db0, na_keep, na_away, na_keep1, na_away1 = run(
            call_ffn, me, 8, 0, False, h2, dbl, w_up, w_down, vec, None, hb, 9
        )
        diag_c = send(diag, CORE)
        x_c = send(own_x, CORE)
        z_c = send(own_z, CORE)
        up_a, up_b, down_a, down_b = run(
            call_far, me, [own, own_z, own_x, diag, own_c, z_c, x_c, diag_c]
        )
        far_vec = diag[diag.shape[0] - 16 :].astype(f32)
        act2, dh, db2, fa_keep, fa_away, fa_keep1, fa_away1 = run(
            call_ffn, me, 8, 0, True, h2, dbl, up_a, down_a, far_vec, dh, hb, 0
        )
        na_away1 = send(na_away1, CORE)
        act3, dh, db3, fb_keep, fb_away, fb_keep1, fb_away1 = run(
            call_ffn, me, 8, 1, True, h2, dbl, up_b, down_b, far_vec, dh, hb, 0
        )
        fa_away1 = send(fa_away1, CORE)
        fb_away1 = send(fb_away1, CORE)
        f0_away = run(combine, [[fa_away, fb_away1]])
        f0_away = send(f0_away, X)
        act1, dh, db1, nb_keep, nb_away, nb_keep1, nb_away1 = run(
            call_ffn, me, 8, 1, False, h2, dbl, w_up, w_down, vec, dh, hb, 9
        )
        nb_away1 = send(nb_away1, CORE)
        f1_away = run(combine, [[fb_away, fa_away1]])
        nb_keep1 = send(nb_keep1, CORE)
        fb_keep1 = send(fb_keep1, CORE)
        f1_away = send(f1_away, Z0)
        n1_away = run(combine, [[nb_away, na_away1]])
        fa_keep1 = send(fa_keep1, CORE)
        dmid, datt, dattn, dv, sums2 = run(call_mid, mod, vec, tokens, out_grad, attn, dh, p, w_out)
        g_keep, g_away, g_keep1, g_away1 = run(call_pair, me, 16, xy_first, (h1, dv), (att, dattn))
        f0 = run(combine, [[fa_keep, fb_keep1, f0_away]])
        n1_away = send(n1_away, Z0)
        n0_away = run(combine, [[na_away, nb_away1]])
        n0_away = send(n0_away, X)
        g_away1 = send(g_away1, CORE)
        f1 = run(combine, [[fb_keep, fa_keep1, f1_away]])
        f1 = send(f1, Y)
        f0 = send(f0, Y)
        dq, dk = run(call_scores, datt, q, k, v, p, cos, sin)
        g_away = run(combine, [[g_away, g_away1]])
        g_away = send(g_away, X)
        e_keep, e_away, e_keep1, e_away1 = run(call_pair, me, 16, yx_first, (h1, dq), (h1, dk))
        na_keep1 = send(na_keep1, CORE)
        n0 = run(combine, [[na_keep, nb_keep1, n0_away]])
        p0, p0_away = run(combine, [[n0, f0]], 2)
        p0_away = send(p0_away, Z0)
        e_away1 = send(e_away1, CORE)
        e_keep1 = send(e_keep1, CORE)
        e_away = run(combine, [[e_away, e_away1]])
        e_away = send(e_away, Y)
        result, sums3 = run(
            call_result, me, True, mod, vec, tokens, out_grad, attn, [act0, act1, act2, act3], [w_down, down_a, down_b]
        )
        n1 = run(combine, [[nb_keep, na_keep1, n1_away]])
        p0, p0_away = run(combine, [[p0, p0_away]], 2)
        g_keep1 = send(g_keep1, CORE)
        p1, p1_away = run(combine, [[n1, f1]], 2)
        p1_away = send(p1_away, Z1)
        tok_grad, sums1 = run(call_tokens, mod, vec, tokens, dmid, dq, dk, dv, w_qkv)
        g, g_away = run(combine, [[g_keep, g_keep1, g_away]], 2)
        p0_away = send(p0_away, Z1)
        g_away = send(g_away, Y)
        e, e_away = run(combine, [[e_keep, e_keep1, e_away]], 2)
        e_away = send(e_away, X)
        p1, p1_away = run(combine, [[p1, p1_away]], 2)
        p1_away = send(p1_away, X)
        g, g_away = run(combine, [[g, g_away]], 2)
        g_away = send(g_away, Z0)
        e, e_away = run(combine, [[e, e_away]], 2)
        e_away = send(e_away, Z0)
        ffn = run(combine, [[p0, p0_away], [p1, p1_away]])
        g, g_away = run(combine, [[g, g_away]], 2)
        g_away = send(g_away, Z1)
        e, e_away = run(combine, [[e, e_away]], 2)
        pack = run(call_pack, timesteps, time_table, mod, vec, bd, sums1, sums2, sums3, [db0, db1, db2, db3])
        e_away = send(e_away, Z1)
        g = run(combine, [[g, g_away], [pack]])
        g_z = send(g, Z1)
        e = run(combine, [[e, e_away]])
        e_z = send(e, Z1)
        g = run(combine, [[g], [g_z]])
        g_z = send(g, Z0)
        ffn_z = send(ffn, Z1)
        e = run(combine, [[e], [e_z]])
        g = run(combine, [[g], [g_z]])
        g_x = send(g, X)
        e_z = send(e, Z0)
        ffn = run(combine, [[ffn], [ffn_z]])
        ffn_z = send(ffn, Z0)
        g = run(combine, [[g], [g_x]])
        g_x = send(g, Y)
        e = run(combine, [[e], [e_z]])
        e_x = send(e, X)
        g_c = send(g, CORE)
        ffn = run(combine, [[ffn], [ffn_z]])
        ffn_x = send(ffn, X)
        g_xc = send(g_x, CORE)
        e = run(combine, [[e], [e_x]])
        e_c = send(e, CORE)
        ffn_c = send(ffn, CORE)
        e_x = send(e, Y)
        qkv_wgrad, out_wgrad = run(call_attn_out, me, (8, 4), [g, g_x, g_c, g_xc])
        table_grad, gain1, gain2, bdown_grad, bias_grad, ada_w_grad, ada_b_grad = run(
            call_small, me, 2, ada_w, [g, g_x, g_c, g_xc], time_table.shape[0]
        )
        e_xc = send(e_x, CORE)
        (qkv_wgrad,) = run(call_attn_out, me, (8, 4), [e, e_x, e_c, e_xc], qkv_wgrad)
        ffn_xc = send(ffn_x, CORE)
        up_grad, down_grad = run(call_ffn_out, me, [ffn, ffn_x, ffn_c, ffn_xc])
        return (
            result, tok_grad, table_grad, gain1, gain2, qkv_wgrad, out_wgrad, up_grad, bias_grad, down_grad,
            bdown_grad, ada_w_grad, ada_b_grad,
        )

    me = jnp.zeros((4,), jnp.int32)
    parts = tokens.shape[0] // CHUNK
    h1, q, k, v, p, att, attn, h2, dbl, bd, mod, vec, *_ = call_forward(
        lengths, timesteps, small, cos, sin, time_table, ada_w, tokens, out_grad, w_qkv, w_out, parts
    )
    n = lax.axis_size("mlp")
    dh, acts, downs, up_sum, down_sum, bup_sum = None, [], [], 0.0, 0.0, 0.0
    for r in range(n):
        there = [(i, (i + r) % n) for i in range(n)]
        back = [((i + r) % n, i) for i in range(n)]
        move = lambda a: lax.ppermute(a, "mlp", there) if r else a
        home = lambda a: lax.ppermute(a, "mlp", back) if r else a
        downs.append(move(w_down))
        act, dh, db, g_up, g_down = call_ffn(
            me, 1, 0, True, h2, dbl, move(w_up).T, downs[-1], move(vec), dh, local, 9
        )
        acts.append(act)
        up_sum = up_sum + home(g_up).astype(f32)
        down_sum = down_sum + home(g_down).astype(f32)
        bup_sum = bup_sum + home(db[0])
    dmid, datt, dattn, dv, sums2 = call_mid(mod, vec, tokens, out_grad, attn, dh, p, w_out)
    dq, dk = call_scores(datt, q, k, v, p, cos, sin)
    w0, w1 = call_pair(me, 1, same, (h1, dq), (h1, dk))
    w2, w3 = call_pair(me, 1, same, (h1, dv), (att, dattn))
    tok_grad, sums1 = call_tokens(mod, vec, tokens, dmid, dq, dk, dv, w_qkv)
    result, sums3 = call_result(me, False, mod, vec, tokens, out_grad, attn, acts, downs)
    up_grad, down_grad, bias_grad = lax.psum((up_sum, down_sum, bup_sum), "seq")
    mod_grad = jnp.concatenate([
        sums1[0], sums1[1] * ln1_gain, sums2[2], sums2[0], sums2[1] * ln2_gain, sums3[0],
    ])[None]
    gains = jnp.stack([sums1[1] * (1.0 + mod[1]), sums2[1] * (1.0 + mod[4]), bd[0]])
    hot = (timesteps[:, None] == jnp.arange(time_table.shape[0], dtype=jnp.int32)[None, :]).astype(f32)
    qkv_wgrad = jnp.concatenate([w0, w1, w2], axis=1).astype(f32)
    qkv_wgrad, out_wgrad, ada_w_grad, ada_b_grad, table_grad, gains = lax.psum(
        (
            qkv_wgrad, w3.astype(f32), jnp.dot(cond.T, mod_grad, precision=HIGH), mod_grad[0],
            jnp.dot(hot.T, jnp.dot(mod_grad, ada_w.T, precision=HIGH), precision=HIGH), gains,
        ),
        ("seq", "mlp"),
    )
    return (
        result, tok_grad, table_grad, gains[0], gains[1], qkv_wgrad, out_wgrad, up_grad, bias_grad, down_grad,
        gains[2], ada_w_grad, ada_b_grad,
    )


def solution(mesh):
    tuned = mesh.shape["seq"] == 16 and mesh.shape["mlp"] == 2
    rows = P(("seq", "mlp"), None)
    flat = P(("seq", "mlp"))

    def whole(
        tokens, time_table, timesteps, lengths, ln1_gain, ln2_gain, w_qkv, w_out, w_up, b_up, w_down, b_down,
        ada_w, ada_b, out_grad,
    ):
        return shards(
            tuned, tokens, time_table, timesteps, lengths, ln1_gain, ln2_gain, w_qkv, w_out, w_up, b_up, w_down,
            b_down, ada_w, ada_b, out_grad,
        )

    return jax.shard_map(
        whole,
        mesh=mesh,
        in_specs=(
            rows, P(), flat, flat, P(), P(), P(), P(), P(None, "mlp"), P("mlp"), P("mlp", None), P(), P(), P(), rows,
        ),
        out_specs=(
            rows, rows, P(), P(), P(), P(), P(), P(None, "mlp"), P("mlp"), P("mlp", None), P(), P(), P(),
        ),
        check_vma=False,
    )
```
